128 devices in a mesh: dp: 64 (over y, x, z), mp: 2 (over core).
Axes of the slice: x: 4, y: 4, z: 4, core: 2. Of those that a mesh axis runs over, the one named last changes fastest.
Arguments:
- tokens: bfloat16 [1792, 64, 1024], P('dp', None, 'mp'), may hold values from -10.2 to 10.2, as said below
- doc_ids: int32 [1792, 64], P('dp'), may hold values from 0 to 3, never falling along the last dimension, each value on 1 to 32 neighbouring positions
- dest: int32 [1792], P('dp'), may hold values from 0 to 1791, as said below
- owner: int32 [1792, 4], P('dp'), may hold values from 0 to 63, as said below
- w_qkv: bfloat16 [1024, 3, 1024], P(None, None, 'mp'), may hold values from -0.1875 to 0.1875
- w_out: bfloat16 [1024, 1024], P('mp'), may hold values from -0.1875 to 0.1875
- gain_attn: float32 [1024], replicated, may hold values from 0.1 to 1.9
- w_up: bfloat16 [1024, 4096], P(None, 'mp'), may hold values from -0.1875 to 0.1875
- w_down: bfloat16 [4096, 1024], P('mp'), may hold values from -0.09375 to 0.09375
- gain_ffn: float32 [1024], replicated, may hold values from 0.1 to 1.9
Outputs:
- encoded: bfloat16 [1792, 64, 1024], P('dp', None, 'mp')
- index_rows: float32 [64, 192, 1024], P('dp', None, 'mp')
The draws below stay inside these ranges and needn't reach their ends.
Inputs may be any that keep to these rules, and one draw needn't show every extreme that they name: `tokens`: values of a standard normal scale. `dest`: A permutation of the rows; slot j of an index of dp goes to slot j; at most 1 row of one index of dp go to the same index of dp, and that many do in every draw. At most 3 documents of one index of dp have the same owner, and some owner receives exactly 3 from every index.
All inputs are finite; a program needn't handle non-finite values.
Results may differ from the reference program's by a relative error of at most 0.0078.
Values may be sent and summed in bfloat16 or wider, within the bound.
No kernel may reach another device: no remote copies, remote signals or barrier semaphores. Data moves between devices by JAX's collectives and lax.ppermute only.
A program may use at most 128 MiB of HBM per device.

```python
import math
import jax
import jax.numpy as jnp
import numpy as np
from jax import lax

D = 1024
FF = 4096
HD = 64
S = 64
DOCS_ROW = 4
ROWS_DEV = 28
ROWS = 1792
CAP = 3
N_DP = 64


def draw_dest(key, part):
    key = jax.random.fold_in(key, 7)
    first_key, second_key = jax.random.split(key)
    shuffle = jax.random.permutation(first_key, N_DP).astype(jnp.int32)
    inverse = jnp.argsort(shuffle, stable=True).astype(jnp.int32)
    offset_table = jax.random.permutation(second_key, N_DP).astype(jnp.int32)
    slot_index = jnp.arange(ROWS_DEV, dtype=jnp.int32)
    offsets = offset_table[slot_index % N_DP]
    to_dev = inverse[(shuffle[:, None] + offsets[None, :]) % N_DP]
    return (to_dev * ROWS_DEV + slot_index).reshape(-1)


def draw_owner(key, part):
    key = jax.random.fold_in(key, 11)
    first_key, second_key = jax.random.split(key)
    busiest = jax.random.randint(first_key, (), 0, N_DP, dtype=jnp.int32)
    doc_total = ROWS_DEV * DOCS_ROW

    def one_source(source):
        chosen = jax.random.permutation(jax.random.fold_in(second_key, source), N_DP - 1).astype(jnp.int32)
        mapped = chosen + (chosen >= busiest).astype(jnp.int32)
        order_table = jnp.concatenate([busiest[None], mapped])
        owners = order_table[jnp.arange(doc_total, dtype=jnp.int32) % N_DP]
        return owners.at[doc_total - 1].set(busiest)
    table = jax.vmap(one_source)(jnp.arange(N_DP, dtype=jnp.int32))
    return table.reshape(ROWS, DOCS_ROW)


def draw_tokens(key, part):
    key = jax.random.fold_in(key, 1)
    first_key = jax.random.fold_in(key, 0)
    base = jnp.clip(jax.random.normal(first_key, (ROWS, S, D), jnp.float32), -6.0, 6.0)
    return base.astype(jnp.bfloat16)


def levels(key, dims, cuts, low, high):
    loudness, own = 1.0, jax.random.fold_in(key, 6)
    for dim, parts in cuts:
        steps = jnp.exp(jax.random.uniform(jax.random.fold_in(own, dim), (parts,), jnp.float32, low / len(cuts), high / len(cuts)))
        loudness = loudness * jnp.repeat(steps, dims[dim] // parts).reshape([-1 if axis == dim else 1 for axis in range(len(dims))])
    return loudness


def length_profile(amount, total, bound, slope):
    loads = [(1 << 20) // math.isqrt(standing ** slope) + 1 for standing in range(2, amount + 1)]
    surplus, holding = total - bound - (amount - 1), [1] * (amount - 1)
    while surplus > 0:
        candidates = [i for i in range(amount - 1) if holding[i] < bound]
        mass, left = sum([loads[i] for i in candidates]), surplus
        for i in candidates:
            more = min(bound - holding[i], max(1, left * loads[i] // mass), surplus)
            holding[i] = holding[i] + more
            surplus = surplus - more
    return np.array([bound] + holding)


def uneven(own_key, count, total, most, lean):
    if count == 2:
        one = jax.random.randint(own_key, (), max(1, total - most), min(most, total - 1) + 1)
        return jnp.stack([one, total - one])
    sizes = jnp.asarray(length_profile(count, total, most, lean), jnp.int32)
    pairs = (count - 1) // 2
    giver, receiver = sizes[1:1 + 2 * pairs:2], sizes[2:2 + 2 * pairs:2]
    margin = jnp.minimum(giver - 1, most - receiver)
    moved = jax.random.randint(jax.random.fold_in(own_key, 1), (pairs,), 0, 1 << 20) % (margin + 1)
    sizes = sizes.at[1:1 + 2 * pairs:2].set(giver - moved).at[2:2 + 2 * pairs:2].set(receiver + moved)
    return sizes[jax.random.permutation(jax.random.fold_in(own_key, 2), count)]


def bell_draw(own_key, extent, width, most, cuts=(), kind=jnp.bfloat16):
    level = levels(own_key, extent, cuts, -0.22, 0.18) if cuts else 1.0
    values = jax.random.normal(own_key, extent, jnp.float32) * width * level
    return jnp.minimum(jnp.maximum(values, -most), most).astype(kind)


def setup_inputs(seed: int = 0) -> dict:
    key_list = jax.random.split(jax.random.key(seed), 11)
    tokens = draw_tokens(jax.random.fold_in(key_list[10], 71), 0)
    doc_ids = jax.vmap(lambda own: jnp.searchsorted(jnp.cumsum(uneven(own, DOCS_ROW, S, S // 2, 2)), jnp.arange(S), side="right"))(jax.random.split(key_list[1], ROWS)).reshape((ROWS, S)).astype(jnp.int32)
    dest = draw_dest(jax.random.fold_in(key_list[10], 71), 0)
    owner = draw_owner(jax.random.fold_in(key_list[10], 71), 0)
    w_qkv = bell_draw(key_list[4], (D, 3, D), D ** -0.5, 0.1875, ((2, 2),))
    w_out = bell_draw(key_list[5], (D, D), D ** -0.5, 0.1875, ((0, 2),))
    gain_attn = jnp.clip(1.0 + 0.18 * jax.random.normal(key_list[6], (D,), jnp.float32), 0.1, 1.9)
    w_up = bell_draw(key_list[7], (D, FF), D ** -0.5, 0.1875, ((1, 2),))
    w_down = bell_draw(key_list[8], (FF, D), FF ** -0.5, 0.09375, ((0, 2),))
    gain_ffn = jnp.clip(1.0 + 0.18 * jax.random.normal(key_list[9], (D,), jnp.float32), 0.1, 1.9)
    return {"tokens": tokens, "doc_ids": doc_ids, "dest": dest, "owner": owner, "w_qkv": w_qkv, "w_out": w_out, "gain_attn": gain_attn, "w_up": w_up, "w_down": w_down, "gain_ffn": gain_ffn}


def norm_rows(values, gain):
    row_mean = lax.optimization_barrier(jnp.mean(values, -1, keepdims=True))
    centred = values - row_mean
    row_var = lax.optimization_barrier(jnp.mean(centred * centred, -1, keepdims=True))
    return centred * lax.rsqrt(row_var + 1e-05) * gain

def reference(tokens, doc_ids, dest, owner, w_qkv, w_out, gain_attn, w_up, w_down, gain_ffn):
    moved = jnp.zeros_like(tokens).at[dest].set(tokens)
    segment = jnp.zeros_like(doc_ids).at[dest].set(doc_ids)
    head_count = D // HD

    def block(pair):
        row_block, segment_ids = pair
        flat_rows = row_block.reshape(-1, D)
        qkv = jnp.dot(flat_rows, w_qkv.reshape(D, 3 * D), preferred_element_type=jnp.float32).astype(jnp.bfloat16)
        qkv = qkv.reshape(ROWS_DEV, S, 3, head_count, HD)
        queries = qkv[:, :, 0].astype(jnp.float32)
        keys_all = qkv[:, :, 1].astype(jnp.float32)
        values_all = qkv[:, :, 2].astype(jnp.float32)
        scores = jnp.einsum('rqhd,rkhd->rhqk', queries, keys_all) / math.sqrt(HD)
        same_doc = segment_ids[:, :, None] == segment_ids[:, None, :]
        scores = jnp.where(same_doc[:, None], scores, jnp.float32(-1e+30))
        row_top = lax.optimization_barrier(jnp.max(scores, -1, keepdims=True))
        weights_exp = jnp.exp(scores - row_top)
        probs = (weights_exp / lax.optimization_barrier(jnp.sum(weights_exp, -1, keepdims=True))).astype(jnp.bfloat16)
        context = jnp.einsum('rhqk,rkhd->rqhd', probs.astype(jnp.float32), values_all).astype(jnp.bfloat16)
        mixed_heads = jnp.dot(context.reshape(-1, D), w_out, preferred_element_type=jnp.float32)
        normed = norm_rows(flat_rows.astype(jnp.float32) + mixed_heads, gain_attn).astype(jnp.bfloat16)
        hidden = jax.nn.gelu(jnp.dot(normed, w_up, preferred_element_type=jnp.float32), approximate=False).astype(jnp.bfloat16)
        ffn_out = jnp.dot(hidden, w_down, preferred_element_type=jnp.float32)
        encoded = norm_rows(normed.astype(jnp.float32) + ffn_out, gain_ffn).astype(jnp.bfloat16)
        encoded = encoded.reshape(ROWS_DEV, S, D)
        onehot = (segment_ids[..., None] == jnp.arange(DOCS_ROW, dtype=jnp.int32)).astype(jnp.float32)
        doc_sums = jnp.einsum('rsk,rsf->rkf', onehot, encoded.astype(jnp.float32), precision=lax.Precision.HIGHEST)
        doc_counts = lax.optimization_barrier(jnp.sum(onehot, 1))[..., None]
        pooled = doc_sums / doc_counts
        embedded = pooled * lax.rsqrt(lax.optimization_barrier(jnp.mean(pooled * pooled, -1, keepdims=True)) + 1e-06)
        return (encoded, embedded.reshape(-1, D))
    encoded, embedded = lax.map(block, (moved.reshape(N_DP, ROWS_DEV, S, D), segment.reshape(N_DP, ROWS_DEV, S)))
    doc_total = ROWS_DEV * DOCS_ROW
    owners = owner.reshape(N_DP, doc_total)
    position = jnp.arange(doc_total, dtype=jnp.int32)
    earlier = (owners[:, :, None] == owners[:, None, :]) & (position[None, None, :] < position[None, :, None])
    slot_rank = lax.optimization_barrier(jnp.sum(earlier.astype(jnp.int32), -1)).astype(jnp.int32)
    columns = jnp.arange(N_DP, dtype=jnp.int32)[:, None] * CAP + slot_rank
    index_rows = jnp.zeros((N_DP, N_DP * CAP, D), jnp.float32).at[owners, columns].set(embedded)
    return (encoded.reshape(ROWS, S, D), index_rows)
```

```python
import jax
import jax.numpy as jnp
from jax import lax
from jax.experimental import pallas as pl
from jax.experimental.pallas import tpu as pltpu
from jax.sharding import PartitionSpec as P

HD = 64
HEADS = 4
TILE = 512
SLOTS = 4
ERF = (
    0.797884941,
    0.0363330846,
    -3.25949759e-05,
    -5.53061935e-05,
    3.96474438e-06,
    -1.32263336e-07,
    1.75617062e-09,
)
SWAP = [(0, 1), (1, 0)]


def gelu(x):
    u = jnp.minimum(x * x, 30.25)
    poly = jnp.full_like(u, ERF[-1])
    for coef in ERF[-2::-1]:
        poly = poly * u + coef
    half = 0.5 * x
    return half + half * jnp.tanh(x * poly)


def norm(values, gain):
    mean = jnp.mean(values, -1, keepdims=True)
    centred = values - mean
    var = jnp.mean(centred * centred, -1, keepdims=True)
    return centred * lax.rsqrt(var + 1e-05) * gain


def pack_kernel(target, tokens, out, sems):
    rows = tokens.shape[0]
    copies = [
        pltpu.make_async_copy(tokens.at[r], out.at[target[r]], sems.at[r]) for r in range(rows)
    ]
    for copy in copies:
        copy.start()
    for copy in copies:
        copy.wait()


def pack(target, tokens, slots):
    rows, seq, width = tokens.shape
    return pl.pallas_call(
        pack_kernel,
        out_shape=jax.ShapeDtypeStruct((slots, seq, width), tokens.dtype),
        in_specs=[
            pl.BlockSpec(memory_space=pltpu.SMEM),
            pl.BlockSpec(memory_space=pl.ANY),
        ],
        out_specs=pl.BlockSpec(memory_space=pl.ANY),
        scratch_shapes=[pltpu.SemaphoreType.DMA((rows,))],
        name="pack_rows",
    )(target, tokens)


def unpack_kernel(source, received, out, sems):
    copies = [
        pltpu.make_async_copy(received.at[source[r]], out.at[r], sems.at[r])
        for r in range(out.shape[0])
    ]
    for copy in copies:
        copy.start()
    for copy in copies:
        copy.wait()


def unpack(source, received):
    rows = source.shape[0]
    _, seq, width = received.shape
    return pl.pallas_call(
        unpack_kernel,
        out_shape=jax.ShapeDtypeStruct((rows, seq, width), received.dtype),
        in_specs=[
            pl.BlockSpec(memory_space=pltpu.SMEM),
            pl.BlockSpec(memory_space=pl.ANY),
        ],
        out_specs=pl.BlockSpec(memory_space=pl.ANY),
        scratch_shapes=[pltpu.SemaphoreType.DMA((rows,))],
        name="unpack_rows",
    )(source, received)


def layer_kernel(
    info,
    received,
    x_other,
    wq_own,
    wq_oth,
    wo_own,
    wo_oth,
    wu_own,
    wu_oth,
    wd_own,
    wd_oth,
    gain_attn,
    gain_ffn,
    enc_own,
    enc_oth,
    emb_own,
    emb_oth,
    x_scr,
    qkv_scr,
    ctx_scr,
    normed_scr,
    acc_scr,
    emb_scr,
    wq,
    wo,
    wu,
    wd,
    row_sems,
    x_sem,
    q_sems,
    w_sems,
):
    rows = enc_own.shape[0] // 64
    seq = 64
    tokens = rows * seq
    half = enc_own.shape[1]
    model = 2 * half
    me = info[0]
    own_col = pl.multiple_of(me * half, half)
    oth_col = pl.multiple_of((1 - me) * half, half)
    row_copies = [
        pltpu.make_async_copy(
            received.at[info[8 + r]],
            x_scr.at[pl.ds(r * seq, seq), pl.ds(own_col, half)],
            row_sems.at[r],
        )
        for r in range(rows)
    ]
    x_copy = pltpu.make_async_copy(x_other, x_scr.at[:, pl.ds(oth_col, half)], x_sem)
    q_copies = [
        pltpu.make_async_copy(ref.at[i], wq.at[3 * h + i], q_sems.at[3 * h + i])
        for h, ref in enumerate((wq_own, wq_oth))
        for i in range(3)
    ]
    width_up = wu_own.shape[1]
    w_copies = [
        pltpu.make_async_copy(wo_own, wo.at[pl.ds(0, half)], w_sems.at[0]),
        pltpu.make_async_copy(wo_oth, wo.at[pl.ds(half, half)], w_sems.at[1]),
        pltpu.make_async_copy(wu_own, wu.at[0], w_sems.at[2]),
        pltpu.make_async_copy(wu_oth, wu.at[1], w_sems.at[3]),
        pltpu.make_async_copy(wd_own, wd.at[0], w_sems.at[4]),
        pltpu.make_async_copy(wd_oth, wd.at[1], w_sems.at[5]),
    ]
    for copy in row_copies:
        copy.start()
    x_copy.start()
    for copy in q_copies + w_copies:
        copy.start()
    for copy in row_copies:
        copy.wait()
    x_copy.wait()

    for n in range(6):
        q_copies[n].wait()
        qkv_scr[:, n * half : (n + 1) * half] = jnp.dot(
            x_scr[...], wq[n], preferred_element_type=jnp.float32
        ).astype(jnp.bfloat16)

    group = HEADS * HD
    block = (
        lax.broadcasted_iota(jnp.int32, (group, group), 0) // HD
        == lax.broadcasted_iota(jnp.int32, (group, group), 1) // HD
    )
    lane_head = lax.broadcasted_iota(jnp.int32, (seq, group), 1) // HD
    key_pos = lax.broadcasted_iota(jnp.int32, (seq, group), 0)
    query_pos = lax.broadcasted_iota(jnp.int32, (seq, group), 1) % HD

    def attend(r, carry):
        base = pl.multiple_of(r * seq, seq)
        bounds = [info[32 + 4 * r + i] for i in range(3)]
        key_seg = sum([(key_pos >= b).astype(jnp.int32) for b in bounds])
        query_seg = sum([(query_pos >= b).astype(jnp.int32) for b in bounds])
        same = key_seg == query_seg
        for g in range(model // group):
            at = (g * group // half) * 3 * half + (g * group) % half
            q = qkv_scr[pl.ds(base, seq), at : at + group]
            k = qkv_scr[pl.ds(base, seq), at + half : at + half + group]
            v = qkv_scr[pl.ds(base, seq), at + 2 * half : at + 2 * half + group]
            spread = jnp.where(block, jnp.concatenate([q] * HEADS, 0), jnp.zeros((), q.dtype))
            scores = lax.dot_general(
                k, spread, (((1,), (1,)), ((), ())), preferred_element_type=jnp.float32
            )
            scores = jnp.where(same, scores * (1.0 / 8.0), jnp.float32(-1e30))
            top = jnp.max(scores, 0, keepdims=True)
            weight = jnp.exp(scores - top)
            probs = (weight / jnp.sum(weight, 0, keepdims=True)).astype(jnp.bfloat16)
            mixed = lax.dot_general(
                probs, v, (((0,), (0,)), ((), ())), preferred_element_type=jnp.float32
            )
            context = jnp.where(lane_head == 0, mixed[:seq], 0.0)
            for h in range(1, HEADS):
                context = jnp.where(lane_head == h, mixed[h * seq : (h + 1) * seq], context)
            ctx_scr[pl.ds(base, seq), g * group : (g + 1) * group] = context.astype(jnp.bfloat16)
        return carry

    lax.fori_loop(0, rows, attend, 0)

    w_copies[0].wait()
    w_copies[1].wait()
    part = tokens // 4

    def mix(m, carry):
        at = pl.ds(pl.multiple_of(m * part, part), part)
        mixed = jnp.dot(ctx_scr[at, :], wo[...], preferred_element_type=jnp.float32)
        mixed = mixed + x_scr[at, :].astype(jnp.float32)
        normed_scr[at, :] = norm(mixed, gain_attn[...]).astype(jnp.bfloat16)
        return carry

    lax.fori_loop(0, 4, mix, 0)

    tiles = width_up // TILE
    for h in range(2):
        w_copies[2 + h].wait()
        w_copies[4 + h].wait()

        def feed(t, carry, h=h):
            at = pl.ds(pl.multiple_of(t * TILE, TILE), TILE)
            up = jnp.dot(normed_scr[...], wu[h, :, at], preferred_element_type=jnp.float32)
            hidden = gelu(up).astype(jnp.bfloat16)
            down = jnp.dot(hidden, wd[h, at, :], preferred_element_type=jnp.float32)
            acc_scr[...] += down
            return carry

        if h == 0:
            acc_scr[...] = normed_scr[...].astype(jnp.float32)
        lax.fori_loop(0, tiles, feed, 0)

    doc_iota = lax.broadcasted_iota(jnp.int32, (8, seq), 0)
    pos_iota = lax.broadcasted_iota(jnp.int32, (8, seq), 1)

    def finish(r, carry):
        at = pl.ds(pl.multiple_of(r * seq, seq), seq)
        out_at = pl.ds(pl.multiple_of(r * 8, 8), 8)
        encoded = norm(acc_scr[at, :], gain_ffn[...]).astype(jnp.bfloat16)
        x_scr[at, :] = encoded
        bounds = [info[32 + 4 * r + i] for i in range(3)]
        seg = sum([(pos_iota >= b).astype(jnp.int32) for b in bounds])
        member = (seg == doc_iota).astype(jnp.float32)
        count = jnp.sum(member, -1, keepdims=True)
        pooled = jnp.dot(member.astype(jnp.bfloat16), encoded, preferred_element_type=jnp.float32)
        pooled = pooled / jnp.maximum(count, 1.0)
        square = jnp.mean(pooled * pooled, -1, keepdims=True)
        emb_scr[out_at, :] = pooled * lax.rsqrt(square + 1e-06)
        return carry

    lax.fori_loop(0, rows, finish, 0)
    enc_own[...] = x_scr[:, pl.ds(own_col, half)]
    enc_oth[...] = x_scr[:, pl.ds(oth_col, half)]
    emb_own[...] = emb_scr[:, pl.ds(own_col, half)].astype(jnp.bfloat16)
    emb_oth[...] = emb_scr[:, pl.ds(oth_col, half)].astype(jnp.bfloat16)


def layer(info, received, x_other, weights, gain_attn, gain_ffn):
    tokens, half = x_other.shape
    rows = tokens // 64
    model = 2 * half
    wq, wo, wu, wd = weights[0], weights[2], weights[4], weights[6]
    flops = 2 * tokens * model * (3 * model + model + 4 * wu.shape[1])
    any_spec = pl.BlockSpec(memory_space=pl.ANY)
    vmem = pl.BlockSpec(memory_space=pltpu.VMEM)
    return pl.pallas_call(
        layer_kernel,
        out_shape=(
            jax.ShapeDtypeStruct((tokens, half), jnp.bfloat16),
            jax.ShapeDtypeStruct((tokens, half), jnp.bfloat16),
            jax.ShapeDtypeStruct((rows * 8, half), jnp.bfloat16),
            jax.ShapeDtypeStruct((rows * 8, half), jnp.bfloat16),
        ),
        in_specs=[pl.BlockSpec(memory_space=pltpu.SMEM)] + [any_spec] * 10 + [vmem] * 2,
        out_specs=(vmem,) * 4,
        scratch_shapes=[
            pltpu.VMEM((tokens, model), jnp.bfloat16),
            pltpu.VMEM((tokens, 3 * model), jnp.bfloat16),
            pltpu.VMEM((tokens, model), jnp.bfloat16),
            pltpu.VMEM((tokens, model), jnp.bfloat16),
            pltpu.VMEM((tokens, model), jnp.float32),
            pltpu.VMEM((rows * 8, model), jnp.float32),
            pltpu.VMEM((6, model, half), jnp.bfloat16),
            pltpu.VMEM((model, model), jnp.bfloat16),
            pltpu.VMEM((2,) + wu.shape, jnp.bfloat16),
            pltpu.VMEM((2,) + wd.shape, jnp.bfloat16),
            pltpu.SemaphoreType.DMA((rows,)),
            pltpu.SemaphoreType.DMA,
            pltpu.SemaphoreType.DMA((6,)),
            pltpu.SemaphoreType.DMA((6,)),
        ],
        compiler_params=pltpu.CompilerParams(vmem_limit_bytes=60 * 1024 * 1024),
        cost_estimate=pl.CostEstimate(
            flops=flops, bytes_accessed=28 * 1024 * 1024, transcendentals=0
        ),
        name="layer",
    )(info, received, x_other, *weights, gain_attn, gain_ffn)


def shards(tokens, doc_ids, dest, owner, w_qkv, w_out, gain_attn, w_up, w_down, gain_ffn):
    devices = lax.axis_size("dp")
    row_count, seq, half = tokens.shape
    docs = owner.shape[1]
    mine = row_count // 2
    me = lax.axis_index("mp")
    index = lax.axis_index("dp")

    qkv_own = jnp.moveaxis(w_qkv, 1, 0)
    weights = []
    for own in (qkv_own, w_out, w_up, w_down):
        weights += [own, lax.ppermute(own, "mp", SWAP)]

    bounds = jnp.stack([jnp.sum((doc_ids < k).astype(jnp.int32), -1) for k in range(1, docs)], -1)
    facts = lax.all_gather(jnp.concatenate([dest[:, None], bounds], -1), "dp", axis=0)
    slot = jnp.arange(row_count, dtype=jnp.int32)
    here = facts[:, :, 0] == (index * row_count + slot)[None, :]
    source = jnp.sum(jnp.where(here, jnp.arange(devices, dtype=jnp.int32)[:, None], 0), 0)
    new_bounds = jnp.sum(jnp.where(here[:, :, None], facts[:, :, 1:], 0), 0)

    received = lax.all_to_all(
        pack(dest // row_count, tokens, devices), "dp", split_axis=0, concat_axis=0, tiled=True
    )
    source_own = lax.dynamic_slice_in_dim(source, me * mine, mine)
    source_oth = lax.dynamic_slice_in_dim(source, (1 - me) * mine, mine)
    bounds_own = lax.dynamic_slice_in_dim(new_bounds, me * mine, mine)
    info = jnp.concatenate(
        [
            jnp.full((8,), me, jnp.int32),
            source_own,
            jnp.zeros((24 - mine,), jnp.int32),
            jnp.pad(bounds_own, ((0, 0), (0, 1))).reshape(-1),
        ]
    )
    x_other = lax.ppermute(unpack(source_oth, received), "mp", SWAP).reshape(-1, half)
    enc_own, enc_oth, emb_own, emb_oth = layer(
        info, received, x_other, weights, gain_attn[None], gain_ffn[None]
    )
    emb_recv = lax.ppermute(emb_oth, "mp", SWAP)
    enc_recv = lax.ppermute(enc_oth, "mp", SWAP)

    owners = owner.reshape(-1)
    position = jnp.arange(row_count * docs, dtype=jnp.int32)
    earlier = (owners[:, None] == owners[None, :]) & (position[None, :] < position[:, None])
    rank = jnp.sum(earlier.astype(jnp.int32), -1)
    target = jnp.pad(
        (owners * SLOTS + rank).reshape(2, mine, docs), ((0, 0), (0, 0), (0, 8 - docs)),
        constant_values=-1,
    ).reshape(2, mine * 8)
    out_slot = jnp.arange(devices * SLOTS, dtype=jnp.int32)[:, None]
    place_own = (lax.dynamic_index_in_dim(target, me, 0) == out_slot).astype(jnp.bfloat16)
    place_oth = (lax.dynamic_index_in_dim(target, 1 - me, 0) == out_slot).astype(jnp.bfloat16)
    sending = (
        jnp.dot(place_own, emb_own, preferred_element_type=jnp.float32)
        + jnp.dot(place_oth, emb_recv, preferred_element_type=jnp.float32)
    ).astype(jnp.bfloat16)
    got = lax.all_to_all(
        sending.reshape(devices, SLOTS, half), "dp", split_axis=0, concat_axis=0, tiled=True
    )
    index_part = got[:, : SLOTS - 1].astype(jnp.float32).reshape(1, devices * (SLOTS - 1), half)

    enc_own = enc_own.reshape(mine, seq, half)
    enc_recv = enc_recv.reshape(mine, seq, half)
    first = me == 0
    encoded = jnp.concatenate(
        [jnp.where(first, enc_own, enc_recv), jnp.where(first, enc_recv, enc_own)], 0
    )
    return (encoded, index_part)


def solution(mesh):
    return jax.shard_map(
        shards,
        mesh=mesh,
        in_specs=(
            P("dp", None, "mp"),
            P("dp", None),
            P("dp"),
            P("dp", None),
            P(None, None, "mp"),
            P("mp", None),
            P(),
            P(None, "mp"),
            P("mp", None),
            P(),
        ),
        out_specs=(P("dp", None, "mp"), P("dp", None, "mp")),
        check_vma=False,
    )
```

```python
import jax
import jax.numpy as jnp
from jax import lax
from jax.experimental import pallas as pl
from jax.experimental.pallas import tpu as pltpu
from jax.sharding import PartitionSpec as P

HD = 64
HEADS = 4
TILE = 512
SLOTS = 4
ERF = (
    0.797884941,
    0.0363330846,
    -3.25949759e-05,
    -5.53061935e-05,
    3.96474438e-06,
    -1.32263336e-07,
    1.75617062e-09,
)
SWAP = [(0, 1), (1, 0)]
LANES = 128
FACTS = 8


def gelu(x):
    u = jnp.minimum(x * x, 30.25)
    poly = jnp.full_like(u, ERF[-1])
    for coef in ERF[-2::-1]:
        poly = poly * u + coef
    half = 0.5 * x
    return half + half * jnp.tanh(x * poly)


def norm(values, gain):
    mean = jnp.mean(values, -1, keepdims=True)
    centred = values - mean
    var = jnp.mean(centred * centred, -1, keepdims=True)
    return centred * lax.rsqrt(var + 1e-05) * gain


def pack_kernel(target, tokens, facts, out, staged, sems, fact_sem):
    rows, seq, width = tokens.shape
    body = seq * width // LANES
    fact_copy = pltpu.make_async_copy(facts, out.at[:, pl.ds(body, FACTS)], fact_sem)
    fact_copy.start()
    copies = []
    for r in range(rows):
        for c in range(width // LANES):
            staged[r, c * seq : (c + 1) * seq, :] = tokens[r, :, c * LANES : (c + 1) * LANES]
        copies.append(
            pltpu.make_async_copy(
                staged.at[r], out.at[target[r], pl.ds(0, body)], sems.at[r]
            )
        )
        copies[-1].start()
    for copy in copies:
        copy.wait()
    fact_copy.wait()


def pack(target, tokens, facts):
    rows, seq, width = tokens.shape
    slots = facts.shape[0]
    body = seq * width // LANES
    return pl.pallas_call(
        pack_kernel,
        out_shape=jax.ShapeDtypeStruct((slots, body + FACTS, LANES), tokens.dtype),
        in_specs=[
            pl.BlockSpec(memory_space=pltpu.SMEM),
            pl.BlockSpec(memory_space=pltpu.VMEM),
            pl.BlockSpec(memory_space=pltpu.VMEM),
        ],
        out_specs=pl.BlockSpec(memory_space=pl.ANY),
        scratch_shapes=[
            pltpu.VMEM((rows, body, LANES), tokens.dtype),
            pltpu.SemaphoreType.DMA((rows,)),
            pltpu.SemaphoreType.DMA,
        ],
        compiler_params=pltpu.CompilerParams(vmem_limit_bytes=16 * 1024 * 1024),
        name="pack_rows",
    )(target, tokens, facts)


def unpack_kernel(source, received, out, sems):
    rows, body, _ = out.shape
    copies = [
        pltpu.make_async_copy(
            received.at[source[r], pl.ds(0, body)], out.at[r], sems.at[r]
        )
        for r in range(rows)
    ]
    for copy in copies:
        copy.start()
    for copy in copies:
        copy.wait()


def unpack(source, received):
    rows = source.shape[0]
    body = received.shape[1] - FACTS
    return pl.pallas_call(
        unpack_kernel,
        out_shape=jax.ShapeDtypeStruct((rows, body, LANES), received.dtype),
        in_specs=[
            pl.BlockSpec(memory_space=pltpu.SMEM),
            pl.BlockSpec(memory_space=pl.ANY),
        ],
        out_specs=pl.BlockSpec(memory_space=pltpu.VMEM),
        scratch_shapes=[pltpu.SemaphoreType.DMA((rows,))],
        compiler_params=pltpu.CompilerParams(vmem_limit_bytes=16 * 1024 * 1024),
        name="unpack_rows",
    )(source, received)


def layer_kernel(
    info,
    received,
    x_other,
    wq_own,
    wq_oth,
    wo_own,
    wo_oth,
    wu_own,
    wu_oth,
    wd_own,
    wd_oth,
    gain_attn,
    gain_ffn,
    enc_own,
    enc_oth,
    emb_own,
    emb_oth,
    x_scr,
    qkv_scr,
    ctx_scr,
    normed_scr,
    acc_scr,
    emb_scr,
    wq,
    wo,
    wu,
    wd,
    row_sems,
    x_sems,
    q_sems,
    w_sems,
):
    rows = enc_own.shape[0] // 64
    seq = 64
    tokens = rows * seq
    half = enc_own.shape[1]
    model = 2 * half
    me = info[0]
    own_col = pl.multiple_of(me * half, half)
    oth_col = pl.multiple_of((1 - me) * half, half)
    row_copies = []
    x_copies = []
    for r in range(rows):
        for c in range(half // LANES):
            piece = pl.ds(c * seq, seq)
            lanes = pl.ds(pl.multiple_of(own_col + c * LANES, LANES), LANES)
            dst = x_scr.at[pl.ds(r * seq, seq), lanes]
            row_copies.append(
                pltpu.make_async_copy(received.at[info[8 + r], piece], dst, row_sems.at[r, c])
            )
    for c in range(half // LANES):
        lanes = pl.ds(pl.multiple_of(oth_col + c * LANES, LANES), LANES)
        for r in range(rows):
            dst = x_scr.at[pl.ds(r * seq, seq), lanes]
            x_copies.append(
                pltpu.make_async_copy(
                    x_other.at[r, pl.ds(c * seq, seq)], dst, x_sems.at[r, c]
                )
            )
    q_copies = [
        pltpu.make_async_copy(ref.at[i], wq.at[3 * h + i], q_sems.at[3 * h + i])
        for h, ref in enumerate((wq_own, wq_oth))
        for i in range(3)
    ]
    width_up = wu_own.shape[1]
    w_copies = [
        pltpu.make_async_copy(wo_own, wo.at[pl.ds(0, half)], w_sems.at[0]),
        pltpu.make_async_copy(wo_oth, wo.at[pl.ds(half, half)], w_sems.at[1]),
        pltpu.make_async_copy(wu_own, wu.at[0], w_sems.at[2]),
        pltpu.make_async_copy(wu_oth, wu.at[1], w_sems.at[3]),
        pltpu.make_async_copy(wd_own, wd.at[0], w_sems.at[4]),
        pltpu.make_async_copy(wd_oth, wd.at[1], w_sems.at[5]),
    ]
    for copy in row_copies + x_copies + q_copies + w_copies:
        copy.start()
    for copy in row_copies + x_copies:
        copy.wait()

    for n in range(6):
        q_copies[n].wait()
        qkv_scr[:, n * half : (n + 1) * half] = jnp.dot(
            x_scr[...], wq[n], preferred_element_type=jnp.float32
        ).astype(jnp.bfloat16)

    group = HEADS * HD
    block = (
        lax.broadcasted_iota(jnp.int32, (group, group), 0) // HD
        == lax.broadcasted_iota(jnp.int32, (group, group), 1) // HD
    )
    lane_head = lax.broadcasted_iota(jnp.int32, (seq, group), 1) // HD
    key_pos = lax.broadcasted_iota(jnp.int32, (seq, group), 0)
    query_pos = lax.broadcasted_iota(jnp.int32, (seq, group), 1) % HD

    def attend(r, carry):
        base = pl.multiple_of(r * seq, seq)
        bounds = [info[32 + 4 * r + i] for i in range(3)]
        key_seg = sum([(key_pos >= b).astype(jnp.int32) for b in bounds])
        query_seg = sum([(query_pos >= b).astype(jnp.int32) for b in bounds])
        same = key_seg == query_seg
        for g in range(model // group):
            at = (g * group // half) * 3 * half + (g * group) % half
            q = qkv_scr[pl.ds(base, seq), at : at + group]
            k = qkv_scr[pl.ds(base, seq), at + half : at + half + group]
            v = qkv_scr[pl.ds(base, seq), at + 2 * half : at + 2 * half + group]
            spread = jnp.where(block, jnp.concatenate([q] * HEADS, 0), jnp.zeros((), q.dtype))
            scores = lax.dot_general(
                k, spread, (((1,), (1,)), ((), ())), preferred_element_type=jnp.float32
            )
            scores = jnp.where(same, scores * (1.0 / 8.0), jnp.float32(-1e30))
            top = jnp.max(scores, 0, keepdims=True)
            weight = jnp.exp(scores - top)
            probs = (weight / jnp.sum(weight, 0, keepdims=True)).astype(jnp.bfloat16)
            mixed = lax.dot_general(
                probs, v, (((0,), (0,)), ((), ())), preferred_element_type=jnp.float32
            )
            context = jnp.where(lane_head == 0, mixed[:seq], 0.0)
            for h in range(1, HEADS):
                context = jnp.where(lane_head == h, mixed[h * seq : (h + 1) * seq], context)
            ctx_scr[pl.ds(base, seq), g * group : (g + 1) * group] = context.astype(jnp.bfloat16)
        return carry

    lax.fori_loop(0, rows, attend, 0)

    w_copies[0].wait()
    w_copies[1].wait()
    part = tokens // 4

    def mix(m, carry):
        at = pl.ds(pl.multiple_of(m * part, part), part)
        mixed = jnp.dot(ctx_scr[at, :], wo[...], preferred_element_type=jnp.float32)
        mixed = mixed + x_scr[at, :].astype(jnp.float32)
        normed_scr[at, :] = norm(mixed, gain_attn[...]).astype(jnp.bfloat16)
        return carry

    lax.fori_loop(0, 4, mix, 0)

    tiles = width_up // TILE
    for h in range(2):
        w_copies[2 + h].wait()
        w_copies[4 + h].wait()

        def feed(t, carry, h=h):
            at = pl.ds(pl.multiple_of(t * TILE, TILE), TILE)
            up = jnp.dot(normed_scr[...], wu[h, :, at], preferred_element_type=jnp.float32)
            hidden = gelu(up).astype(jnp.bfloat16)
            down = jnp.dot(hidden, wd[h, at, :], preferred_element_type=jnp.float32)
            acc_scr[...] += down
            return carry

        if h == 0:
            acc_scr[...] = normed_scr[...].astype(jnp.float32)
        lax.fori_loop(0, tiles, feed, 0)

    doc_iota = lax.broadcasted_iota(jnp.int32, (8, seq), 0)
    pos_iota = lax.broadcasted_iota(jnp.int32, (8, seq), 1)

    def finish(r, carry):
        at = pl.ds(pl.multiple_of(r * seq, seq), seq)
        out_at = pl.ds(pl.multiple_of(r * 8, 8), 8)
        encoded = norm(acc_scr[at, :], gain_ffn[...]).astype(jnp.bfloat16)
        x_scr[at, :] = encoded
        bounds = [info[32 + 4 * r + i] for i in range(3)]
        seg = sum([(pos_iota >= b).astype(jnp.int32) for b in bounds])
        member = (seg == doc_iota).astype(jnp.float32)
        count = jnp.sum(member, -1, keepdims=True)
        pooled = jnp.dot(member.astype(jnp.bfloat16), encoded, preferred_element_type=jnp.float32)
        pooled = pooled / jnp.maximum(count, 1.0)
        square = jnp.mean(pooled * pooled, -1, keepdims=True)
        emb_scr[out_at, :] = pooled * lax.rsqrt(square + 1e-06)
        return carry

    lax.fori_loop(0, rows, finish, 0)
    enc_own[...] = x_scr[:, pl.ds(own_col, half)]
    enc_oth[...] = x_scr[:, pl.ds(oth_col, half)]
    emb_own[...] = emb_scr[:, pl.ds(own_col, half)].astype(jnp.bfloat16)
    emb_oth[...] = emb_scr[:, pl.ds(oth_col, half)].astype(jnp.bfloat16)


def layer(info, received, x_other, weights, gain_attn, gain_ffn):
    rows, body, _ = x_other.shape
    half = body * LANES // 64
    tokens = rows * 64
    model = 2 * half
    wq, wo, wu, wd = weights[0], weights[2], weights[4], weights[6]
    flops = 2 * tokens * model * (3 * model + model + 4 * wu.shape[1])
    any_spec = pl.BlockSpec(memory_space=pl.ANY)
    vmem = pl.BlockSpec(memory_space=pltpu.VMEM)
    return pl.pallas_call(
        layer_kernel,
        out_shape=(
            jax.ShapeDtypeStruct((tokens, half), jnp.bfloat16),
            jax.ShapeDtypeStruct((tokens, half), jnp.bfloat16),
            jax.ShapeDtypeStruct((rows * 8, half), jnp.bfloat16),
            jax.ShapeDtypeStruct((rows * 8, half), jnp.bfloat16),
        ),
        in_specs=[pl.BlockSpec(memory_space=pltpu.SMEM)] + [any_spec] * 10 + [vmem] * 2,
        out_specs=(vmem,) * 4,
        scratch_shapes=[
            pltpu.VMEM((tokens, model), jnp.bfloat16),
            pltpu.VMEM((tokens, 3 * model), jnp.bfloat16),
            pltpu.VMEM((tokens, model), jnp.bfloat16),
            pltpu.VMEM((tokens, model), jnp.bfloat16),
            pltpu.VMEM((tokens, model), jnp.float32),
            pltpu.VMEM((rows * 8, model), jnp.float32),
            pltpu.VMEM((6, model, half), jnp.bfloat16),
            pltpu.VMEM((model, model), jnp.bfloat16),
            pltpu.VMEM((2,) + wu.shape, jnp.bfloat16),
            pltpu.VMEM((2,) + wd.shape, jnp.bfloat16),
            pltpu.SemaphoreType.DMA((rows, half // LANES)),
            pltpu.SemaphoreType.DMA((rows, half // LANES)),
            pltpu.SemaphoreType.DMA((6,)),
            pltpu.SemaphoreType.DMA((6,)),
        ],
        compiler_params=pltpu.CompilerParams(vmem_limit_bytes=60 * 1024 * 1024),
        cost_estimate=pl.CostEstimate(
            flops=flops, bytes_accessed=28 * 1024 * 1024, transcendentals=0
        ),
        name="layer",
    )(info, received, x_other, *weights, gain_attn, gain_ffn)


def shards(tokens, doc_ids, dest, owner, w_qkv, w_out, gain_attn, w_up, w_down, gain_ffn):
    devices = lax.axis_size("dp")
    row_count, seq, half = tokens.shape
    docs = owner.shape[1]
    mine = row_count // 2
    me = lax.axis_index("mp")

    qkv_own = jnp.moveaxis(w_qkv, 1, 0)
    weights = []
    for own in (qkv_own, w_out, w_up, w_down):
        weights += [own, lax.ppermute(own, "mp", SWAP)]

    target = dest // row_count
    sent = (jnp.arange(devices, dtype=jnp.int32)[:, None] == target[None, :]).astype(jnp.int32)
    bounds = [jnp.sum((doc_ids < k).astype(jnp.int32), -1) for k in range(1, docs)]
    fact_list = [dest % row_count + 1] + bounds
    facts = jnp.stack([jnp.sum(sent * fact[None, :], -1) for fact in fact_list], -1)
    facts = jnp.broadcast_to(
        jnp.pad(facts, ((0, 0), (0, LANES - len(fact_list))))[:, None, :].astype(jnp.bfloat16),
        (devices, FACTS, LANES),
    )
    received = lax.all_to_all(
        pack(target, tokens, facts), "dp", split_axis=0, concat_axis=0, tiled=True
    )
    got_facts = received[:, -FACTS, : len(fact_list)].astype(jnp.int32)
    slot = jnp.arange(row_count, dtype=jnp.int32)
    here = got_facts[:, :1] == slot[None, :] + 1
    source = jnp.sum(jnp.where(here, jnp.arange(devices, dtype=jnp.int32)[:, None], 0), 0)
    new_bounds = jnp.sum(jnp.where(here[:, :, None], got_facts[:, None, 1:], 0), 0)
    source_own = lax.dynamic_slice_in_dim(source, me * mine, mine)
    source_oth = lax.dynamic_slice_in_dim(source, (1 - me) * mine, mine)
    bounds_own = lax.dynamic_slice_in_dim(new_bounds, me * mine, mine)
    info = jnp.concatenate(
        [
            jnp.full((8,), me, jnp.int32),
            source_own,
            jnp.zeros((24 - mine,), jnp.int32),
            jnp.pad(bounds_own, ((0, 0), (0, 1))).reshape(-1),
        ]
    )
    x_other = lax.ppermute(unpack(source_oth, received), "mp", SWAP)
    enc_own, enc_oth, emb_own, emb_oth = layer(
        info, received, x_other, weights, gain_attn[None], gain_ffn[None]
    )
    emb_recv = lax.ppermute(emb_oth, "mp", SWAP)
    enc_recv = lax.ppermute(enc_oth, "mp", SWAP)

    owners = owner.reshape(-1)
    position = jnp.arange(row_count * docs, dtype=jnp.int32)
    earlier = (owners[:, None] == owners[None, :]) & (position[None, :] < position[:, None])
    rank = jnp.sum(earlier.astype(jnp.int32), -1)
    target = jnp.pad(
        (owners * SLOTS + rank).reshape(2, mine, docs), ((0, 0), (0, 0), (0, 8 - docs)),
        constant_values=-1,
    ).reshape(2, mine * 8)
    out_slot = jnp.arange(devices * SLOTS, dtype=jnp.int32)[:, None]
    place_own = (lax.dynamic_index_in_dim(target, me, 0) == out_slot).astype(jnp.bfloat16)
    place_oth = (lax.dynamic_index_in_dim(target, 1 - me, 0) == out_slot).astype(jnp.bfloat16)
    sending = (
        jnp.dot(place_own, emb_own, preferred_element_type=jnp.float32)
        + jnp.dot(place_oth, emb_recv, preferred_element_type=jnp.float32)
    ).astype(jnp.bfloat16)
    got = lax.all_to_all(
        sending.reshape(devices, SLOTS, half), "dp", split_axis=0, concat_axis=0, tiled=True
    )
    index_part = got[:, : SLOTS - 1].astype(jnp.float32).reshape(1, devices * (SLOTS - 1), half)

    enc_own = enc_own.reshape(mine, seq, half)
    enc_recv = enc_recv.reshape(mine, seq, half)
    first = me == 0
    encoded = jnp.concatenate(
        [jnp.where(first, enc_own, enc_recv), jnp.where(first, enc_recv, enc_own)], 0
    )
    return (encoded, index_part)


def solution(mesh):
    return jax.shard_map(
        shards,
        mesh=mesh,
        in_specs=(
            P("dp", None, "mp"),
            P("dp", None),
            P("dp"),
            P("dp", None),
            P(None, None, "mp"),
            P("mp", None),
            P(),
            P(None, "mp"),
            P("mp", None),
            P(),
        ),
        out_specs=(P("dp", None, "mp"), P("dp", None, "mp")),
        check_vma=False,
    )
```

```python
import math

import jax
import jax.numpy as jnp
from jax import lax
from jax.experimental import pallas as pl
from jax.experimental.pallas import tpu as pltpu
from jax.sharding import PartitionSpec as P

HD = 64
TILE = 1024
PART = 448
SLOTS = 4
SWAP = [(0, 1), (1, 0)]
LANES = 128
FACTS = 8


def gelu(x):
    half = 0.5 * x
    return half + half * lax.erf(x * math.sqrt(0.5))


def norm(values, gain):
    mean = jnp.mean(values, -1, keepdims=True)
    centred = values - mean
    var = jnp.mean(centred * centred, -1, keepdims=True)
    return centred * lax.rsqrt(var + 1e-05) * gain


def pack_kernel(target, tokens, facts, out, staged, sems, fact_sem):
    rows, seq, width = tokens.shape
    body = seq * width // LANES
    fact_copy = pltpu.make_async_copy(facts, out.at[:, pl.ds(body, FACTS)], fact_sem)
    fact_copy.start()
    copies = []
    for r in range(rows):
        for c in range(width // LANES):
            staged[r, c * seq : (c + 1) * seq, :] = tokens[r, :, c * LANES : (c + 1) * LANES]
        copies.append(
            pltpu.make_async_copy(
                staged.at[r], out.at[target[r], pl.ds(0, body)], sems.at[r]
            )
        )
        copies[-1].start()
    for copy in copies:
        copy.wait()
    fact_copy.wait()


def pack(target, tokens, facts):
    rows, seq, width = tokens.shape
    slots = facts.shape[0]
    body = seq * width // LANES
    return pl.pallas_call(
        pack_kernel,
        out_shape=jax.ShapeDtypeStruct((slots, body + FACTS, LANES), tokens.dtype),
        in_specs=[
            pl.BlockSpec(memory_space=pltpu.SMEM),
            pl.BlockSpec(memory_space=pltpu.VMEM),
            pl.BlockSpec(memory_space=pltpu.VMEM),
        ],
        out_specs=pl.BlockSpec(memory_space=pl.ANY),
        scratch_shapes=[
            pltpu.VMEM((rows, body, LANES), tokens.dtype),
            pltpu.SemaphoreType.DMA((rows,)),
            pltpu.SemaphoreType.DMA,
        ],
        compiler_params=pltpu.CompilerParams(vmem_limit_bytes=16 * 1024 * 1024),
        name="pack_rows",
    )(target, tokens, facts)


def unpack_kernel(source, received, out, sems):
    rows, body, _ = out.shape
    copies = [
        pltpu.make_async_copy(
            received.at[source[r], pl.ds(0, body)], out.at[r], sems.at[r]
        )
        for r in range(rows)
    ]
    for copy in copies:
        copy.start()
    for copy in copies:
        copy.wait()


def unpack(source, received):
    rows = source.shape[0]
    body = received.shape[1] - FACTS
    return pl.pallas_call(
        unpack_kernel,
        out_shape=jax.ShapeDtypeStruct((rows, body, LANES), received.dtype),
        in_specs=[
            pl.BlockSpec(memory_space=pltpu.SMEM),
            pl.BlockSpec(memory_space=pl.ANY),
        ],
        out_specs=pl.BlockSpec(memory_space=pltpu.VMEM),
        scratch_shapes=[pltpu.SemaphoreType.DMA((rows,))],
        compiler_params=pltpu.CompilerParams(vmem_limit_bytes=16 * 1024 * 1024),
        name="unpack_rows",
    )(source, received)


def layer_kernel(
    info,
    received,
    x_other,
    wq_own,
    wq_oth,
    wo_own,
    wo_oth,
    wu_own,
    wu_oth,
    wd_own,
    wd_oth,
    gain_attn,
    gain_ffn,
    enc_own,
    enc_oth,
    emb,
    x_scr,
    qkv_scr,
    acc_scr,
    wu,
    wd,
    row_sems,
    x_sem,
    w_sems,
    out_sems,
):
    rows = x_scr.shape[0]
    seq = HD
    tokens, half = enc_own.shape
    model = 2 * half
    chunks = model // LANES
    body = half * seq // LANES
    me = info[0]
    own_at = pl.ds(pl.multiple_of(me * body, body), body)
    oth_at = pl.ds(pl.multiple_of((1 - me) * body, body), body)
    x_copies = [
        pltpu.make_async_copy(
            received.at[info[8 + r], pl.ds(0, body)], x_scr.at[r, own_at], row_sems.at[r]
        )
        for r in range(rows)
    ]
    x_copies.append(pltpu.make_async_copy(x_other, x_scr.at[:, oth_at], x_sem))
    w_copies = [
        pltpu.make_async_copy(src, dst.at[h], w_sems.at[i, h])
        for h, srcs in enumerate(((wu_own, wd_own), (wu_oth, wd_oth)))
        for i, (src, dst) in enumerate(zip(srcs, (wu, wd)))
    ]
    for copy in x_copies:
        copy.start()
    for copy in x_copies:
        copy.wait()
    for copy in w_copies:
        copy.start()

    def inputs(first, count):
        pieces = [
            x_scr[pl.ds(first, count), c * seq : (c + 1) * seq, :].reshape(count * seq, LANES)
            for c in range(chunks)
        ]
        return jnp.concatenate(pieces, 1)

    for h, wq in enumerate((wq_own, wq_oth)):
        for i in range(3):
            n = 3 * h + i
            qkv_scr[:, n * half : (n + 1) * half] = jnp.dot(
                inputs(0, rows), wq[i], preferred_element_type=jnp.float32
            ).astype(jnp.bfloat16)

    pair = 2 * HD
    block = (lax.broadcasted_iota(jnp.int32, (pair, pair), 0) < HD) == (
        lax.broadcasted_iota(jnp.int32, (pair, pair), 1) < HD
    )
    lane_low = lax.broadcasted_iota(jnp.int32, (seq, pair), 1) < HD
    key_pos = lax.broadcasted_iota(jnp.int32, (seq, pair), 0)
    query_pos = lax.broadcasted_iota(jnp.int32, (seq, pair), 1) % HD
    per_half = half // pair

    def attend(r, carry):
        here = pl.ds(pl.multiple_of(r * seq, seq), seq)
        bounds = [info[32 + 4 * r + i] for i in range(3)]
        key_seg = sum([(key_pos >= b).astype(jnp.int32) for b in bounds])
        query_seg = sum([(query_pos >= b).astype(jnp.int32) for b in bounds])
        same = key_seg == query_seg
        scores = []
        for p in range(2 * per_half):
            at = (p // per_half) * 3 * half + (p % per_half) * pair
            q = qkv_scr[here, at : at + pair]
            k = qkv_scr[here, at + half : at + half + pair]
            spread = jnp.where(block, jnp.concatenate([q, q], 0), jnp.zeros((), q.dtype))
            scores.append(
                lax.dot_general(
                    k, spread, (((1,), (1,)), ((), ())), preferred_element_type=jnp.float32
                )
            )
        probs = []
        for score in scores:
            score = jnp.where(same, score * (1.0 / math.sqrt(HD)), jnp.float32(-1e30))
            weight = jnp.exp(score - jnp.max(score, 0, keepdims=True))
            probs.append(
                (weight * (1.0 / jnp.sum(weight, 0, keepdims=True))).astype(jnp.bfloat16)
            )
        mixed = []
        for p in range(2 * per_half):
            at = (p // per_half) * 3 * half + 2 * half + (p % per_half) * pair
            mixed.append(
                lax.dot_general(
                    probs[p],
                    qkv_scr[here, at : at + pair],
                    (((0,), (0,)), ((), ())),
                    preferred_element_type=jnp.float32,
                )
            )
        for p in range(2 * per_half):
            at = (p // per_half) * 3 * half + (p % per_half) * pair
            qkv_scr[here, at : at + pair] = jnp.where(
                lane_low, mixed[p][:seq], mixed[p][seq:]
            ).astype(jnp.bfloat16)
        return carry

    lax.fori_loop(0, rows, attend, 0)

    count = 2
    for m in range(rows // count):
        at = slice(m * count * seq, (m + 1) * count * seq)
        mixed = jnp.dot(qkv_scr[at, :half], wo_own[...], preferred_element_type=jnp.float32)
        mixed += jnp.dot(
            qkv_scr[at, 3 * half : 4 * half], wo_oth[...], preferred_element_type=jnp.float32
        )
        mixed = mixed + inputs(m * count, count).astype(jnp.float32)
        normed = norm(mixed, gain_attn[...]).astype(jnp.bfloat16)
        qkv_scr[at, half : 3 * half] = normed
        acc_scr[at, :] = normed.astype(jnp.float32)

    for copy in w_copies:
        copy.wait()
    tiles = wu.shape[2] // TILE
    parts = tokens // PART

    def feed(t, carry):
        h = t // (tiles * parts)
        at = pl.ds(pl.multiple_of((t % tiles) * TILE, TILE), TILE)
        here = pl.ds(pl.multiple_of((t // tiles) % parts * PART, PART), PART)
        normed = qkv_scr[here, half : 3 * half]
        up = jnp.dot(normed, wu[h, :, at], preferred_element_type=jnp.float32)
        acc_scr[here, :] += jnp.dot(
            gelu(up).astype(jnp.bfloat16), wd[h, at, :], preferred_element_type=jnp.float32
        )
        return carry

    lax.fori_loop(0, 2 * tiles * parts, feed, 0)

    doc_iota = lax.broadcasted_iota(jnp.int32, (8, seq), 0)
    pos_iota = lax.broadcasted_iota(jnp.int32, (8, seq), 1)
    for r in range(rows):
        at = slice(r * seq, (r + 1) * seq)
        encoded = norm(acc_scr[at, :], gain_ffn[...]).astype(jnp.bfloat16)
        qkv_scr[at, : 2 * half] = encoded
        bounds = [info[32 + 4 * r + i] for i in range(3)]
        seg = sum([(pos_iota >= b).astype(jnp.int32) for b in bounds])
        member = (seg == doc_iota).astype(jnp.float32)
        total = jnp.sum(member, -1, keepdims=True)
        pooled = jnp.dot(member.astype(jnp.bfloat16), encoded, preferred_element_type=jnp.float32)
        pooled = pooled * (1.0 / jnp.maximum(total, 1.0))
        square = jnp.mean(pooled * pooled, -1, keepdims=True)
        embedded = pooled * lax.rsqrt(square + 1e-06)
        emb[me, r * 8 : (r + 1) * 8, :] = embedded[:, :half]
        emb[1 - me, r * 8 : (r + 1) * 8, :] = embedded[:, half:]
    own_col = pl.ds(pl.multiple_of(me * half, half), half)
    oth_col = pl.ds(pl.multiple_of((1 - me) * half, half), half)
    outs = [
        pltpu.make_async_copy(qkv_scr.at[:, own_col], enc_own, out_sems.at[0]),
        pltpu.make_async_copy(qkv_scr.at[:, oth_col], enc_oth, out_sems.at[1]),
    ]
    for copy in outs:
        copy.start()
    for copy in outs:
        copy.wait()


def layer(info, received, x_other, weights, gain_attn, gain_ffn):
    rows, body, _ = x_other.shape
    half = body * LANES // HD
    tokens = rows * HD
    model = 2 * half
    wu, wd = weights[4], weights[6]
    flops = 2 * tokens * model * (3 * model + model + 4 * wu.shape[1])
    any_spec = pl.BlockSpec(memory_space=pl.ANY)
    vmem = pl.BlockSpec(memory_space=pltpu.VMEM)
    return pl.pallas_call(
        layer_kernel,
        out_shape=(
            jax.ShapeDtypeStruct((tokens, half), jnp.bfloat16),
            jax.ShapeDtypeStruct((tokens, half), jnp.bfloat16),
            jax.ShapeDtypeStruct((2, rows * 8, half), jnp.float32),
        ),
        in_specs=[pl.BlockSpec(memory_space=pltpu.SMEM)]
        + [any_spec] * 2 + [vmem] * 4 + [any_spec] * 4 + [vmem] * 2,
        out_specs=(any_spec, any_spec, vmem),
        scratch_shapes=[
            pltpu.VMEM((rows, 2 * body, LANES), jnp.bfloat16),
            pltpu.VMEM((tokens, 3 * model), jnp.bfloat16),
            pltpu.VMEM((tokens, model), jnp.float32),
            pltpu.VMEM((2,) + wu.shape, jnp.bfloat16),
            pltpu.VMEM((2,) + wd.shape, jnp.bfloat16),
            pltpu.SemaphoreType.DMA((rows,)),
            pltpu.SemaphoreType.DMA,
            pltpu.SemaphoreType.DMA((2, 2)),
            pltpu.SemaphoreType.DMA((2,)),
        ],
        compiler_params=pltpu.CompilerParams(vmem_limit_bytes=46 * 1024 * 1024),
        cost_estimate=pl.CostEstimate(
            flops=flops, bytes_accessed=28 * 1024 * 1024, transcendentals=0
        ),
        name="layer",
    )(info, received, x_other, *weights, gain_attn, gain_ffn)


def shards(tokens, doc_ids, dest, owner, w_qkv, w_out, gain_attn, w_up, w_down, gain_ffn):
    devices = lax.axis_size("dp")
    row_count, seq, half = tokens.shape
    docs = owner.shape[1]
    mine = row_count // 2
    me = lax.axis_index("mp")

    qkv_own = jnp.moveaxis(w_qkv, 1, 0)
    weights = []
    for own in (qkv_own, w_out, w_up, w_down):
        weights += [own, lax.ppermute(own, "mp", SWAP)]

    target = dest // row_count
    sent = (jnp.arange(devices, dtype=jnp.int32)[:, None] == target[None, :]).astype(jnp.int32)
    bounds = [jnp.sum((doc_ids < k).astype(jnp.int32), -1) for k in range(1, docs)]
    fact_list = [dest % row_count + 1] + bounds
    facts = jnp.stack([jnp.sum(sent * fact[None, :], -1) for fact in fact_list], -1)
    facts = jnp.broadcast_to(
        jnp.pad(facts, ((0, 0), (0, LANES - len(fact_list))))[:, None, :].astype(jnp.bfloat16),
        (devices, FACTS, LANES),
    )
    received = lax.all_to_all(
        pack(target, tokens, facts), "dp", split_axis=0, concat_axis=0, tiled=True
    )
    got_facts = received[:, -FACTS, : len(fact_list)].astype(jnp.int32)
    slot = jnp.arange(row_count, dtype=jnp.int32)
    here = got_facts[:, :1] == slot[None, :] + 1
    source = jnp.sum(jnp.where(here, jnp.arange(devices, dtype=jnp.int32)[:, None], 0), 0)
    new_bounds = jnp.sum(jnp.where(here[:, :, None], got_facts[:, None, 1:], 0), 0)
    source_own = lax.dynamic_slice_in_dim(source, me * mine, mine)
    source_oth = lax.dynamic_slice_in_dim(source, (1 - me) * mine, mine)
    bounds_own = lax.dynamic_slice_in_dim(new_bounds, me * mine, mine)
    info = jnp.concatenate(
        [
            jnp.full((8,), me, jnp.int32),
            source_own,
            jnp.zeros((24 - mine,), jnp.int32),
            jnp.pad(bounds_own, ((0, 0), (0, 1))).reshape(-1),
        ]
    )
    x_other = lax.ppermute(unpack(source_oth, received), "mp", SWAP)
    enc_own, enc_oth, emb = layer(
        info, received, x_other, weights, gain_attn[None], gain_ffn[None]
    )
    emb = emb.astype(jnp.bfloat16)
    emb_recv = lax.ppermute(emb[1], "mp", SWAP)
    enc_recv = lax.ppermute(enc_oth, "mp", SWAP)

    owners = owner.reshape(-1)
    position = jnp.arange(row_count * docs, dtype=jnp.int32)
    earlier = (owners[:, None] == owners[None, :]) & (position[None, :] < position[:, None])
    rank = jnp.sum(earlier.astype(jnp.int32), -1)
    target = jnp.pad(
        (owners * SLOTS + rank).reshape(2, mine, docs), ((0, 0), (0, 0), (0, 8 - docs)),
        constant_values=-1,
    ).reshape(2, mine * 8)
    out_slot = jnp.arange(devices * SLOTS, dtype=jnp.int32)[:, None]
    place_own = (lax.dynamic_index_in_dim(target, me, 0) == out_slot).astype(jnp.bfloat16)
    place_oth = (lax.dynamic_index_in_dim(target, 1 - me, 0) == out_slot).astype(jnp.bfloat16)
    sending = (
        jnp.dot(place_own, emb[0], preferred_element_type=jnp.float32)
        + jnp.dot(place_oth, emb_recv, preferred_element_type=jnp.float32)
    ).astype(jnp.bfloat16)
    got = lax.all_to_all(
        sending.reshape(devices, SLOTS, half), "dp", split_axis=0, concat_axis=0, tiled=True
    )
    index_part = got[:, : SLOTS - 1].astype(jnp.float32).reshape(1, devices * (SLOTS - 1), half)

    enc_own = enc_own.reshape(mine, seq, half)
    enc_recv = enc_recv.reshape(mine, seq, half)
    first = me == 0
    encoded = jnp.concatenate(
        [jnp.where(first, enc_own, enc_recv), jnp.where(first, enc_recv, enc_own)], 0
    )
    return (encoded, index_part)


def solution(mesh):
    return jax.shard_map(
        shards,
        mesh=mesh,
        in_specs=(
            P("dp", None, "mp"),
            P("dp", None),
            P("dp"),
            P("dp", None),
            P(None, None, "mp"),
            P("mp", None),
            P(),
            P(None, "mp"),
            P("mp", None),
            P(),
        ),
        out_specs=(P("dp", None, "mp"), P("dp", None, "mp")),
        check_vma=False,
    )
```

```python
import math

import jax
import jax.numpy as jnp
from jax import lax
from jax.experimental import pallas as pl
from jax.experimental.pallas import tpu as pltpu
from jax.sharding import PartitionSpec as P

HD = 64
TILE = 1024
PART = 448
SLOTS = 4
SWAP = [(0, 1), (1, 0)]
LANES = 128
FACTS = 8


def gelu(x):
    half = 0.5 * x
    return half + half * lax.erf(x * math.sqrt(0.5))


def norm(values, gain):
    mean = jnp.mean(values, -1, keepdims=True)
    centred = values - mean
    var = jnp.mean(centred * centred, -1, keepdims=True)
    return centred * lax.rsqrt(var + 1e-05) * gain


def pack_kernel(dest, doc_ids, tokens, out, raw, staged, empty, in_sems, out_sems, empty_sem):
    rows, seq, width = tokens.shape
    body = seq * width // LANES
    loads = [pltpu.make_async_copy(tokens.at[r], raw.at[r], in_sems.at[r]) for r in range(rows)]
    for copy in loads:
        copy.start()
    empty[...] = jnp.zeros_like(empty)
    clear = pltpu.make_async_copy(empty, out.at[:, pl.ds(body, FACTS)], empty_sem)
    clear.start()
    lane = lax.broadcasted_iota(jnp.int32, (rows, LANES), 1)
    facts = jnp.where(lane == 0, lax.broadcasted_iota(jnp.int32, (rows, LANES), 0) + 1, 0)
    ids = doc_ids[...]
    for k in range(1, 4):
        bound = jnp.sum((ids < k).astype(jnp.float32), -1, keepdims=True).astype(jnp.int32)
        facts = jnp.where(lane == k, bound, facts)
    facts = facts.astype(jnp.float32)
    stores = []
    for r in range(rows):
        staged[r, body:, :] = jnp.broadcast_to(facts[r : r + 1, :], (FACTS, LANES)).astype(
            jnp.bfloat16
        )
        loads[r].wait()
        for c in range(width // LANES):
            staged[r, c * seq : (c + 1) * seq, :] = raw[r, :, c * LANES : (c + 1) * LANES]
        if r == 0:
            clear.wait()
        stores.append(
            pltpu.make_async_copy(
                staged.at[r], out.at[lax.div(dest[r], rows)], out_sems.at[r]
            )
        )
        stores[-1].start()
    for copy in stores:
        copy.wait()


def pack(dest, doc_ids, tokens, slots):
    rows, seq, width = tokens.shape
    body = seq * width // LANES
    return pl.pallas_call(
        pack_kernel,
        out_shape=jax.ShapeDtypeStruct((slots, body + FACTS, LANES), tokens.dtype),
        in_specs=[
            pl.BlockSpec(memory_space=pltpu.SMEM),
            pl.BlockSpec(memory_space=pltpu.VMEM),
            pl.BlockSpec(memory_space=pltpu.HBM),
        ],
        out_specs=pl.BlockSpec(memory_space=pltpu.HBM),
        scratch_shapes=[
            pltpu.VMEM((rows, seq, width), tokens.dtype),
            pltpu.VMEM((rows, body + FACTS, LANES), tokens.dtype),
            pltpu.VMEM((slots, FACTS, LANES), tokens.dtype),
            pltpu.SemaphoreType.DMA((rows,)),
            pltpu.SemaphoreType.DMA((rows,)),
            pltpu.SemaphoreType.DMA,
        ],
        compiler_params=pltpu.CompilerParams(vmem_limit_bytes=16 * 1024 * 1024),
        name="pack_rows",
    )(dest, doc_ids, tokens)


def unpack_kernel(core, received, out, info, facts, table, fact_sem, info_sem, sems):
    rows, body, _ = out.shape
    slots = received.shape[0]
    load = pltpu.make_async_copy(received.at[:, pl.ds(body, FACTS)], facts, fact_sem)
    load.start()
    load.wait()
    values = facts[...].astype(jnp.float32)
    shape = (slots, FACTS, LANES)
    here = values[:, :, :1] == (lax.broadcasted_iota(jnp.int32, shape, 2) + 1).astype(jnp.float32)
    source = lax.broadcasted_iota(jnp.int32, shape, 0).astype(jnp.float32)
    result = jnp.sum(jnp.where(here, source, 0.0), 0)
    kind = lax.broadcasted_iota(jnp.int32, (FACTS, LANES), 0)
    for k in range(1, 4):
        bound = jnp.sum(jnp.where(here, values[:, :, k : k + 1], 0.0), 0)
        result = jnp.where(kind == k, bound, result)
    table[...] = result.astype(jnp.int32)
    keep = pltpu.make_async_copy(table, info, info_sem)
    keep.start()
    keep.wait()
    first = (1 - core[0]) * rows
    copies = [
        pltpu.make_async_copy(
            received.at[info[0, first + r], pl.ds(0, body)], out.at[r], sems.at[r]
        )
        for r in range(rows)
    ]
    for copy in copies:
        copy.start()
    for copy in copies:
        copy.wait()


def unpack(core, received, rows):
    slots = received.shape[0]
    body = received.shape[1] - FACTS
    return pl.pallas_call(
        unpack_kernel,
        out_shape=(
            jax.ShapeDtypeStruct((rows, body, LANES), received.dtype),
            jax.ShapeDtypeStruct((FACTS, LANES), jnp.int32),
        ),
        in_specs=[
            pl.BlockSpec(memory_space=pltpu.SMEM),
            pl.BlockSpec(memory_space=pltpu.HBM),
        ],
        out_specs=(
            pl.BlockSpec(memory_space=pltpu.VMEM),
            pl.BlockSpec(memory_space=pltpu.SMEM),
        ),
        scratch_shapes=[
            pltpu.VMEM((slots, FACTS, LANES), received.dtype),
            pltpu.VMEM((FACTS, LANES), jnp.int32),
            pltpu.SemaphoreType.DMA,
            pltpu.SemaphoreType.DMA,
            pltpu.SemaphoreType.DMA((rows,)),
        ],
        compiler_params=pltpu.CompilerParams(vmem_limit_bytes=16 * 1024 * 1024),
        name="unpack_rows",
    )(core, received)


def layer_kernel(
    core,
    info,
    received,
    x_other,
    wq_own,
    wq_oth,
    wo_own,
    wo_oth,
    wu_own,
    wu_oth,
    wd_own,
    wd_oth,
    gain_attn,
    gain_ffn,
    enc_own,
    enc_oth,
    emb,
    x_scr,
    qkv_scr,
    acc_scr,
    wu,
    wd,
    row_sems,
    x_sem,
    w_sems,
    out_sems,
):
    rows = x_scr.shape[0]
    seq = HD
    tokens, half = enc_own.shape
    model = 2 * half
    chunks = model // LANES
    body = half * seq // LANES
    me = core[0]
    first_row = me * rows
    own_at = pl.ds(pl.multiple_of(me * body, body), body)
    oth_at = pl.ds(pl.multiple_of((1 - me) * body, body), body)
    x_copies = [
        pltpu.make_async_copy(
            received.at[info[0, first_row + r], pl.ds(0, body)], x_scr.at[r, own_at], row_sems.at[r]
        )
        for r in range(rows)
    ]
    x_copies.append(pltpu.make_async_copy(x_other, x_scr.at[:, oth_at], x_sem))
    w_copies = [
        pltpu.make_async_copy(src, dst.at[h], w_sems.at[i, h])
        for h, srcs in enumerate(((wu_own, wd_own), (wu_oth, wd_oth)))
        for i, (src, dst) in enumerate(zip(srcs, (wu, wd)))
    ]
    for copy in x_copies:
        copy.start()
    for copy in x_copies:
        copy.wait()
    for copy in w_copies:
        copy.start()

    def inputs(first, count):
        pieces = [
            x_scr[pl.ds(first, count), c * seq : (c + 1) * seq, :].reshape(count * seq, LANES)
            for c in range(chunks)
        ]
        return jnp.concatenate(pieces, 1)

    for h, wq in enumerate((wq_own, wq_oth)):
        for i in range(3):
            n = 3 * h + i
            qkv_scr[:, n * half : (n + 1) * half] = jnp.dot(
                inputs(0, rows), wq[i], preferred_element_type=jnp.float32
            ).astype(jnp.bfloat16)

    pair = 2 * HD
    block = (lax.broadcasted_iota(jnp.int32, (pair, pair), 0) < HD) == (
        lax.broadcasted_iota(jnp.int32, (pair, pair), 1) < HD
    )
    lane_low = lax.broadcasted_iota(jnp.int32, (seq, pair), 1) < HD
    key_pos = lax.broadcasted_iota(jnp.int32, (seq, pair), 0)
    query_pos = lax.broadcasted_iota(jnp.int32, (seq, pair), 1) % HD
    per_half = half // pair

    def attend(r, carry):
        here = pl.ds(pl.multiple_of(r * seq, seq), seq)
        bounds = [info[k, first_row + r] for k in range(1, 4)]
        key_seg = sum([(key_pos >= b).astype(jnp.int32) for b in bounds])
        query_seg = sum([(query_pos >= b).astype(jnp.int32) for b in bounds])
        same = key_seg == query_seg
        scores = []
        for p in range(2 * per_half):
            at = (p // per_half) * 3 * half + (p % per_half) * pair
            q = qkv_scr[here, at : at + pair]
            k = qkv_scr[here, at + half : at + half + pair]
            spread = jnp.where(block, jnp.concatenate([q, q], 0), jnp.zeros((), q.dtype))
            scores.append(
                lax.dot_general(
                    k, spread, (((1,), (1,)), ((), ())), preferred_element_type=jnp.float32
                )
            )
        probs = []
        for score in scores:
            score = jnp.where(same, score * (1.0 / math.sqrt(HD)), jnp.float32(-1e30))
            weight = jnp.exp(score - jnp.max(score, 0, keepdims=True))
            probs.append(
                (weight * (1.0 / jnp.sum(weight, 0, keepdims=True))).astype(jnp.bfloat16)
            )
        mixed = []
        for p in range(2 * per_half):
            at = (p // per_half) * 3 * half + 2 * half + (p % per_half) * pair
            mixed.append(
                lax.dot_general(
                    probs[p],
                    qkv_scr[here, at : at + pair],
                    (((0,), (0,)), ((), ())),
                    preferred_element_type=jnp.float32,
                )
            )
        for p in range(2 * per_half):
            at = (p // per_half) * 3 * half + (p % per_half) * pair
            qkv_scr[here, at : at + pair] = jnp.where(
                lane_low, mixed[p][:seq], mixed[p][seq:]
            ).astype(jnp.bfloat16)
        return carry

    lax.fori_loop(0, rows, attend, 0)

    count = 2
    for m in range(rows // count):
        at = slice(m * count * seq, (m + 1) * count * seq)
        mixed = jnp.dot(qkv_scr[at, :half], wo_own[...], preferred_element_type=jnp.float32)
        mixed += jnp.dot(
            qkv_scr[at, 3 * half : 4 * half], wo_oth[...], preferred_element_type=jnp.float32
        )
        mixed = mixed + inputs(m * count, count).astype(jnp.float32)
        normed = norm(mixed, gain_attn[...]).astype(jnp.bfloat16)
        qkv_scr[at, half : 3 * half] = normed
        acc_scr[at, :] = normed.astype(jnp.float32)

    for copy in w_copies:
        copy.wait()
    tiles = wu.shape[2] // TILE
    parts = tokens // PART

    def feed(t, carry):
        h = t // (tiles * parts)
        at = pl.ds(pl.multiple_of((t % tiles) * TILE, TILE), TILE)
        here = pl.ds(pl.multiple_of((t // tiles) % parts * PART, PART), PART)
        normed = qkv_scr[here, half : 3 * half]
        up = jnp.dot(normed, wu[h, :, at], preferred_element_type=jnp.float32)
        acc_scr[here, :] += jnp.dot(
            gelu(up).astype(jnp.bfloat16), wd[h, at, :], preferred_element_type=jnp.float32
        )
        return carry

    lax.fori_loop(0, 2 * tiles * parts, feed, 0)

    doc_iota = lax.broadcasted_iota(jnp.int32, (8, seq), 0)
    pos_iota = lax.broadcasted_iota(jnp.int32, (8, seq), 1)
    for r in range(rows):
        at = slice(r * seq, (r + 1) * seq)
        encoded = norm(acc_scr[at, :], gain_ffn[...]).astype(jnp.bfloat16)
        qkv_scr[at, : 2 * half] = encoded
        bounds = [info[k, first_row + r] for k in range(1, 4)]
        seg = sum([(pos_iota >= b).astype(jnp.int32) for b in bounds])
        member = (seg == doc_iota).astype(jnp.float32)
        total = jnp.sum(member, -1, keepdims=True)
        pooled = jnp.dot(member.astype(jnp.bfloat16), encoded, preferred_element_type=jnp.float32)
        pooled = pooled * (1.0 / jnp.maximum(total, 1.0))
        square = jnp.mean(pooled * pooled, -1, keepdims=True)
        embedded = pooled * lax.rsqrt(square + 1e-06)
        emb[me, r * 8 : (r + 1) * 8, :] = embedded[:, :half]
        emb[1 - me, r * 8 : (r + 1) * 8, :] = embedded[:, half:]
    own_col = pl.ds(pl.multiple_of(me * half, half), half)
    oth_col = pl.ds(pl.multiple_of((1 - me) * half, half), half)
    outs = [
        pltpu.make_async_copy(qkv_scr.at[:, own_col], enc_own, out_sems.at[0]),
        pltpu.make_async_copy(qkv_scr.at[:, oth_col], enc_oth, out_sems.at[1]),
    ]
    for copy in outs:
        copy.start()
    for copy in outs:
        copy.wait()


def layer(core, info, received, x_other, weights, gain_attn, gain_ffn):
    rows, body, _ = x_other.shape
    half = body * LANES // HD
    tokens = rows * HD
    model = 2 * half
    wu, wd = weights[4], weights[6]
    flops = 2 * tokens * model * (3 * model + model + 4 * wu.shape[1])
    any_spec = pl.BlockSpec(memory_space=pl.ANY)
    vmem = pl.BlockSpec(memory_space=pltpu.VMEM)
    return pl.pallas_call(
        layer_kernel,
        out_shape=(
            jax.ShapeDtypeStruct((tokens, half), jnp.bfloat16),
            jax.ShapeDtypeStruct((tokens, half), jnp.bfloat16),
            jax.ShapeDtypeStruct((2, rows * 8, half), jnp.float32),
        ),
        in_specs=[pl.BlockSpec(memory_space=pltpu.SMEM)] * 2
        + [any_spec] * 2 + [vmem] * 4 + [any_spec] * 4 + [vmem] * 2,
        out_specs=(any_spec, any_spec, vmem),
        scratch_shapes=[
            pltpu.VMEM((rows, 2 * body, LANES), jnp.bfloat16),
            pltpu.VMEM((tokens, 3 * model), jnp.bfloat16),
            pltpu.VMEM((tokens, model), jnp.float32),
            pltpu.VMEM((2,) + wu.shape, jnp.bfloat16),
            pltpu.VMEM((2,) + wd.shape, jnp.bfloat16),
            pltpu.SemaphoreType.DMA((rows,)),
            pltpu.SemaphoreType.DMA,
            pltpu.SemaphoreType.DMA((2, 2)),
            pltpu.SemaphoreType.DMA((2,)),
        ],
        compiler_params=pltpu.CompilerParams(vmem_limit_bytes=46 * 1024 * 1024),
        cost_estimate=pl.CostEstimate(
            flops=flops, bytes_accessed=28 * 1024 * 1024, transcendentals=0
        ),
        name="layer",
    )(core, info, received, x_other, *weights, gain_attn, gain_ffn)


def shards(tokens, doc_ids, dest, owner, w_qkv, w_out, gain_attn, w_up, w_down, gain_ffn):
    devices = lax.axis_size("dp")
    row_count, seq, half = tokens.shape
    docs = owner.shape[1]
    mine = row_count // 2
    me = lax.axis_index("mp")

    qkv_own = jnp.moveaxis(w_qkv, 1, 0)
    weights = []
    for own in (qkv_own, w_out, w_up, w_down):
        weights += [own, lax.ppermute(own, "mp", SWAP)]

    received = lax.all_to_all(
        pack(dest, doc_ids, tokens, devices), "dp", split_axis=0, concat_axis=0, tiled=True
    )
    core = me.astype(jnp.int32)[None]
    x_send, info = unpack(core, received, mine)
    x_other = lax.ppermute(x_send, "mp", SWAP)
    enc_own, enc_oth, emb = layer(
        core, info, received, x_other, weights, gain_attn[None], gain_ffn[None]
    )
    emb = emb.astype(jnp.bfloat16)
    emb_recv = lax.ppermute(emb[1], "mp", SWAP)
    enc_recv = lax.ppermute(enc_oth, "mp", SWAP)

    owners = owner.reshape(-1)
    position = jnp.arange(row_count * docs, dtype=jnp.int32)
    earlier = (owners[:, None] == owners[None, :]) & (position[None, :] < position[:, None])
    rank = jnp.sum(earlier.astype(jnp.int32), -1)
    target = jnp.pad(
        (owners * SLOTS + rank).reshape(2, mine, docs), ((0, 0), (0, 0), (0, 8 - docs)),
        constant_values=-1,
    ).reshape(2, mine * 8)
    out_slot = jnp.arange(devices * SLOTS, dtype=jnp.int32)[:, None]
    place_own = (lax.dynamic_index_in_dim(target, me, 0) == out_slot).astype(jnp.bfloat16)
    place_oth = (lax.dynamic_index_in_dim(target, 1 - me, 0) == out_slot).astype(jnp.bfloat16)
    sending = (
        jnp.dot(place_own, emb[0], preferred_element_type=jnp.float32)
        + jnp.dot(place_oth, emb_recv, preferred_element_type=jnp.float32)
    ).astype(jnp.bfloat16)
    got = lax.all_to_all(
        sending.reshape(devices, SLOTS, half), "dp", split_axis=0, concat_axis=0, tiled=True
    )
    index_part = got[:, : SLOTS - 1].astype(jnp.float32).reshape(1, devices * (SLOTS - 1), half)

    enc_own = enc_own.reshape(mine, seq, half)
    enc_recv = enc_recv.reshape(mine, seq, half)
    first = me == 0
    encoded = jnp.concatenate(
        [jnp.where(first, enc_own, enc_recv), jnp.where(first, enc_recv, enc_own)], 0
    )
    return (encoded, index_part)


def solution(mesh):
    return jax.shard_map(
        shards,
        mesh=mesh,
        in_specs=(
            P("dp", None, "mp"),
            P("dp", None),
            P("dp"),
            P("dp", None),
            P(None, None, "mp"),
            P("mp", None),
            P(),
            P(None, "mp"),
            P("mp", None),
            P(),
        ),
        out_specs=(P("dp", None, "mp"), P("dp", None, "mp")),
        check_vma=False,
    )
```

```python
import math

import jax
import jax.numpy as jnp
from jax import lax
from jax.experimental import pallas as pl
from jax.experimental.pallas import tpu as pltpu
from jax.sharding import PartitionSpec as P

HD = 64
TILE = 1024
PART = 448
SLOTS = 4
SWAP = [(0, 1), (1, 0)]
LANES = 128
FACTS = 8


def gelu(x):
    half = 0.5 * x
    return half + half * lax.erf(x * math.sqrt(0.5))


def norm(values, gain):
    mean = jnp.mean(values, -1, keepdims=True)
    centred = values - mean
    var = jnp.mean(centred * centred, -1, keepdims=True)
    return centred * lax.rsqrt(var + 1e-05) * gain


def pack_kernel(dest, doc_ids, tokens, out, raw, staged, empty, in_sems, out_sems, empty_sem):
    rows, seq, width = tokens.shape
    body = seq * width // LANES
    loads = [pltpu.make_async_copy(tokens.at[r], raw.at[r], in_sems.at[r]) for r in range(rows)]
    for copy in loads:
        copy.start()
    empty[...] = jnp.zeros_like(empty)
    clear = pltpu.make_async_copy(empty, out.at[:, pl.ds(body, FACTS)], empty_sem)
    clear.start()
    lane = lax.broadcasted_iota(jnp.int32, (rows, LANES), 1)
    facts = jnp.where(lane == 0, lax.broadcasted_iota(jnp.int32, (rows, LANES), 0) + 1, 0)
    ids = doc_ids[...]
    for k in range(1, 4):
        bound = jnp.sum((ids < k).astype(jnp.float32), -1, keepdims=True).astype(jnp.int32)
        facts = jnp.where(lane == k, bound, facts)
    facts = facts.astype(jnp.float32)
    stores = []
    for r in range(rows):
        staged[r, body:, :] = jnp.broadcast_to(facts[r : r + 1, :], (FACTS, LANES)).astype(
            jnp.bfloat16
        )
        loads[r].wait()
        for c in range(width // LANES):
            staged[r, c * seq : (c + 1) * seq, :] = raw[r, :, c * LANES : (c + 1) * LANES]
        if r == 0:
            clear.wait()
        stores.append(
            pltpu.make_async_copy(
                staged.at[r], out.at[lax.div(dest[r], rows)], out_sems.at[r]
            )
        )
        stores[-1].start()
    for copy in stores:
        copy.wait()


def pack(dest, doc_ids, tokens, slots):
    rows, seq, width = tokens.shape
    body = seq * width // LANES
    return pl.pallas_call(
        pack_kernel,
        out_shape=jax.ShapeDtypeStruct((slots, body + FACTS, LANES), tokens.dtype),
        in_specs=[
            pl.BlockSpec(memory_space=pltpu.SMEM),
            pl.BlockSpec(memory_space=pltpu.VMEM),
            pl.BlockSpec(memory_space=pltpu.HBM),
        ],
        out_specs=pl.BlockSpec(memory_space=pltpu.HBM),
        scratch_shapes=[
            pltpu.VMEM((rows, seq, width), tokens.dtype),
            pltpu.VMEM((rows, body + FACTS, LANES), tokens.dtype),
            pltpu.VMEM((slots, FACTS, LANES), tokens.dtype),
            pltpu.SemaphoreType.DMA((rows,)),
            pltpu.SemaphoreType.DMA((rows,)),
            pltpu.SemaphoreType.DMA,
        ],
        compiler_params=pltpu.CompilerParams(vmem_limit_bytes=60 * 1024 * 1024),
        name="pack_rows",
    )(dest, doc_ids, tokens)


def unpack_kernel(core, received, out, info, facts, table, fact_sem, info_sem, sems):
    rows, body, _ = out.shape
    slots = received.shape[0]
    load = pltpu.make_async_copy(received.at[:, pl.ds(body, FACTS)], facts, fact_sem)
    load.start()
    load.wait()
    values = facts[...].astype(jnp.float32)
    shape = (slots, FACTS, LANES)
    here = values[:, :, :1] == (lax.broadcasted_iota(jnp.int32, shape, 2) + 1).astype(jnp.float32)
    source = lax.broadcasted_iota(jnp.int32, shape, 0).astype(jnp.float32)
    result = jnp.sum(jnp.where(here, source, 0.0), 0)
    kind = lax.broadcasted_iota(jnp.int32, (FACTS, LANES), 0)
    for k in range(1, 4):
        bound = jnp.sum(jnp.where(here, values[:, :, k : k + 1], 0.0), 0)
        result = jnp.where(kind == k, bound, result)
    table[...] = result.astype(jnp.int32)
    keep = pltpu.make_async_copy(table, info, info_sem)
    keep.start()
    keep.wait()
    first = (1 - core[0]) * rows
    copies = [
        pltpu.make_async_copy(
            received.at[info[0, first + r], pl.ds(0, body)], out.at[r], sems.at[r]
        )
        for r in range(rows)
    ]
    for copy in copies:
        copy.start()
    for copy in copies:
        copy.wait()


def unpack(core, received, rows):
    slots = received.shape[0]
    body = received.shape[1] - FACTS
    return pl.pallas_call(
        unpack_kernel,
        out_shape=(
            jax.ShapeDtypeStruct((rows, body, LANES), received.dtype),
            jax.ShapeDtypeStruct((FACTS, LANES), jnp.int32),
        ),
        in_specs=[
            pl.BlockSpec(memory_space=pltpu.SMEM),
            pl.BlockSpec(memory_space=pltpu.HBM),
        ],
        out_specs=(
            pl.BlockSpec(memory_space=pltpu.VMEM),
            pl.BlockSpec(memory_space=pltpu.SMEM),
        ),
        scratch_shapes=[
            pltpu.VMEM((slots, FACTS, LANES), received.dtype),
            pltpu.VMEM((FACTS, LANES), jnp.int32),
            pltpu.SemaphoreType.DMA,
            pltpu.SemaphoreType.DMA,
            pltpu.SemaphoreType.DMA((rows,)),
        ],
        compiler_params=pltpu.CompilerParams(vmem_limit_bytes=60 * 1024 * 1024),
        name="unpack_rows",
    )(core, received)


def layer_kernel(
    core,
    info,
    received,
    x_other,
    wq_own,
    wq_oth,
    wo_own,
    wo_oth,
    wu_own,
    wu_oth,
    wd_own,
    wd_oth,
    gain_attn,
    gain_ffn,
    enc_own,
    enc_oth,
    emb,
    x_scr,
    qkv_scr,
    acc_scr,
    wu,
    wd,
    row_sems,
    x_sem,
    w_sems,
    out_sems,
):
    rows = x_scr.shape[0]
    seq = HD
    tokens, half = enc_own.shape
    model = 2 * half
    chunks = model // LANES
    body = half * seq // LANES
    me = core[0]
    first_row = me * rows
    own_at = pl.ds(pl.multiple_of(me * body, body), body)
    oth_at = pl.ds(pl.multiple_of((1 - me) * body, body), body)
    x_copies = [
        pltpu.make_async_copy(
            received.at[info[0, first_row + r], pl.ds(0, body)], x_scr.at[r, own_at], row_sems.at[r]
        )
        for r in range(rows)
    ]
    x_copies.append(pltpu.make_async_copy(x_other, x_scr.at[:, oth_at], x_sem))
    w_copies = [
        pltpu.make_async_copy(src, dst.at[h], w_sems.at[i, h])
        for h, srcs in enumerate(((wu_own, wd_own), (wu_oth, wd_oth)))
        for i, (src, dst) in enumerate(zip(srcs, (wu, wd)))
    ]
    for copy in x_copies:
        copy.start()
    for copy in x_copies:
        copy.wait()
    for copy in w_copies:
        copy.start()

    def inputs(first, count):
        pieces = [
            x_scr[pl.ds(first, count), c * seq : (c + 1) * seq, :].reshape(count * seq, LANES)
            for c in range(chunks)
        ]
        return jnp.concatenate(pieces, 1)

    for h, wq in enumerate((wq_own, wq_oth)):
        for i in range(3):
            n = 3 * h + i
            qkv_scr[:, n * half : (n + 1) * half] = jnp.dot(
                inputs(0, rows), wq[i], preferred_element_type=jnp.float32
            ).astype(jnp.bfloat16)

    pair = 2 * HD
    block = (lax.broadcasted_iota(jnp.int32, (pair, pair), 0) < HD) == (
        lax.broadcasted_iota(jnp.int32, (pair, pair), 1) < HD
    )
    lane_low = lax.broadcasted_iota(jnp.int32, (seq, pair), 1) < HD
    key_pos = lax.broadcasted_iota(jnp.int32, (seq, pair), 0)
    query_pos = lax.broadcasted_iota(jnp.int32, (seq, pair), 1) % HD
    per_half = half // pair

    def attend(r, carry):
        here = pl.ds(pl.multiple_of(r * seq, seq), seq)
        bounds = [info[k, first_row + r] for k in range(1, 4)]
        key_seg = sum([(key_pos >= b).astype(jnp.int32) for b in bounds])
        query_seg = sum([(query_pos >= b).astype(jnp.int32) for b in bounds])
        same = key_seg == query_seg
        scores = []
        for p in range(2 * per_half):
            at = (p // per_half) * 3 * half + (p % per_half) * pair
            q = qkv_scr[here, at : at + pair]
            k = qkv_scr[here, at + half : at + half + pair]
            spread = jnp.where(block, jnp.concatenate([q, q], 0), jnp.zeros((), q.dtype))
            scores.append(
                lax.dot_general(
                    k, spread, (((1,), (1,)), ((), ())), preferred_element_type=jnp.float32
                )
            )
        probs = []
        for score in scores:
            score = jnp.where(same, score * (1.0 / math.sqrt(HD)), jnp.float32(-1e30))
            weight = jnp.exp(score - jnp.max(score, 0, keepdims=True))
            probs.append(
                (weight * (1.0 / jnp.sum(weight, 0, keepdims=True))).astype(jnp.bfloat16)
            )
        mixed = []
        for p in range(2 * per_half):
            at = (p // per_half) * 3 * half + 2 * half + (p % per_half) * pair
            mixed.append(
                lax.dot_general(
                    probs[p],
                    qkv_scr[here, at : at + pair],
                    (((0,), (0,)), ((), ())),
                    preferred_element_type=jnp.float32,
                )
            )
        for p in range(2 * per_half):
            at = (p // per_half) * 3 * half + (p % per_half) * pair
            qkv_scr[here, at : at + pair] = jnp.where(
                lane_low, mixed[p][:seq], mixed[p][seq:]
            ).astype(jnp.bfloat16)
        return carry

    lax.fori_loop(0, rows, attend, 0)

    count = 2
    for m in range(rows // count):
        at = slice(m * count * seq, (m + 1) * count * seq)
        mixed = jnp.dot(qkv_scr[at, :half], wo_own[...], preferred_element_type=jnp.float32)
        mixed += jnp.dot(
            qkv_scr[at, 3 * half : 4 * half], wo_oth[...], preferred_element_type=jnp.float32
        )
        mixed = mixed + inputs(m * count, count).astype(jnp.float32)
        normed = norm(mixed, gain_attn[...]).astype(jnp.bfloat16)
        qkv_scr[at, half : 3 * half] = normed
        acc_scr[at, :] = normed.astype(jnp.float32)

    for copy in w_copies:
        copy.wait()
    tiles = wu.shape[2] // TILE
    parts = tokens // PART

    def feed(t, carry):
        h = t // (tiles * parts)
        at = pl.ds(pl.multiple_of((t % tiles) * TILE, TILE), TILE)
        here = pl.ds(pl.multiple_of((t // tiles) % parts * PART, PART), PART)
        normed = qkv_scr[here, half : 3 * half]
        up = jnp.dot(normed, wu[h, :, at], preferred_element_type=jnp.float32)
        acc_scr[here, :] += jnp.dot(
            gelu(up).astype(jnp.bfloat16), wd[h, at, :], preferred_element_type=jnp.float32
        )
        return carry

    lax.fori_loop(0, 2 * tiles * parts, feed, 0)

    two = 2 * seq
    doc = lax.broadcasted_iota(jnp.int32, (16, two), 0)
    position = lax.broadcasted_iota(jnp.int32, (16, two), 1)
    same_row = (doc < 8) == (position < seq)
    doc = doc % 8
    own_col = pl.ds(pl.multiple_of(me * half, half), half)
    oth_col = pl.ds(pl.multiple_of((1 - me) * half, half), half)
    outs = []
    for m in range(rows // 2):
        at = slice(m * two, (m + 1) * two)
        encoded = norm(acc_scr[at, :], gain_ffn[...]).astype(jnp.bfloat16)
        qkv_scr[at, : 2 * half] = encoded
        for i, (col, out) in enumerate(((own_col, enc_own), (oth_col, enc_oth))):
            outs.append(
                pltpu.make_async_copy(
                    qkv_scr.at[pl.ds(m * two, two), col],
                    out.at[pl.ds(m * two, two)],
                    out_sems.at[m, i],
                )
            )
            outs[-1].start()
        seg = jnp.zeros_like(position)
        for k in range(1, 4):
            bound = jnp.where(
                position < seq,
                info[k, first_row + 2 * m],
                info[k, first_row + 2 * m + 1] + seq,
            )
            seg += (position >= bound).astype(jnp.int32)
        member = ((seg == doc) & same_row).astype(jnp.float32)
        total = jnp.sum(member, -1, keepdims=True)
        pooled = jnp.dot(member.astype(jnp.bfloat16), encoded, preferred_element_type=jnp.float32)
        pooled = pooled * (1.0 / jnp.maximum(total, 1.0))
        square = jnp.mean(pooled * pooled, -1, keepdims=True)
        embedded = (pooled * lax.rsqrt(square + 1e-06)).astype(jnp.bfloat16)
        emb[me, m * 16 : (m + 1) * 16, :] = embedded[:, :half]
        emb[1 - me, m * 16 : (m + 1) * 16, :] = embedded[:, half:]
    for copy in outs:
        copy.wait()


def layer(core, info, received, x_other, weights, gain_attn, gain_ffn):
    rows, body, _ = x_other.shape
    half = body * LANES // HD
    tokens = rows * HD
    model = 2 * half
    wu, wd = weights[4], weights[6]
    flops = 2 * tokens * model * (3 * model + model + 4 * wu.shape[1])
    any_spec = pl.BlockSpec(memory_space=pl.ANY)
    vmem = pl.BlockSpec(memory_space=pltpu.VMEM)
    return pl.pallas_call(
        layer_kernel,
        out_shape=(
            jax.ShapeDtypeStruct((tokens, half), jnp.bfloat16),
            jax.ShapeDtypeStruct((tokens, half), jnp.bfloat16),
            jax.ShapeDtypeStruct((2, rows * 8, half), jnp.bfloat16),
        ),
        in_specs=[pl.BlockSpec(memory_space=pltpu.SMEM)] * 2
        + [any_spec] * 2 + [vmem] * 4 + [any_spec] * 4 + [vmem] * 2,
        out_specs=(any_spec, any_spec, vmem),
        scratch_shapes=[
            pltpu.VMEM((rows, 2 * body, LANES), jnp.bfloat16),
            pltpu.VMEM((tokens, 3 * model), jnp.bfloat16),
            pltpu.VMEM((tokens, model), jnp.float32),
            pltpu.VMEM((2,) + wu.shape, jnp.bfloat16),
            pltpu.VMEM((2,) + wd.shape, jnp.bfloat16),
            pltpu.SemaphoreType.DMA((rows,)),
            pltpu.SemaphoreType.DMA,
            pltpu.SemaphoreType.DMA((2, 2)),
            pltpu.SemaphoreType.DMA((rows // 2, 2)),
        ],
        compiler_params=pltpu.CompilerParams(vmem_limit_bytes=46 * 1024 * 1024),
        cost_estimate=pl.CostEstimate(
            flops=flops, bytes_accessed=28 * 1024 * 1024, transcendentals=0
        ),
        name="layer",
    )(core, info, received, x_other, *weights, gain_attn, gain_ffn)


def shards(tokens, doc_ids, dest, owner, w_qkv, w_out, gain_attn, w_up, w_down, gain_ffn):
    devices = lax.axis_size("dp")
    row_count, seq, half = tokens.shape
    docs = owner.shape[1]
    mine = row_count // 2
    me = lax.axis_index("mp")

    qkv_own = jnp.moveaxis(w_qkv, 1, 0)
    weights = []
    for own in (qkv_own, w_out, w_up, w_down):
        weights += [own, lax.ppermute(own, "mp", SWAP)]

    received = lax.all_to_all(
        pack(dest, doc_ids, tokens, devices), "dp", split_axis=0, concat_axis=0, tiled=True
    )
    core = me.astype(jnp.int32)[None]
    x_send, info = unpack(core, received, mine)
    x_other = lax.ppermute(x_send, "mp", SWAP)
    enc_own, enc_oth, emb = layer(
        core, info, received, x_other, weights, gain_attn[None], gain_ffn[None]
    )
    emb_recv = lax.ppermute(emb[1], "mp", SWAP)
    enc_recv = lax.ppermute(enc_oth, "mp", SWAP)

    owners = owner.reshape(-1)
    position = jnp.arange(row_count * docs, dtype=jnp.int32)
    earlier = (owners[:, None] == owners[None, :]) & (position[None, :] < position[:, None])
    rank = jnp.sum(earlier.astype(jnp.int32), -1)
    target = jnp.pad(
        (owners * SLOTS + rank).reshape(2, mine, docs), ((0, 0), (0, 0), (0, 8 - docs)),
        constant_values=-1,
    ).reshape(2, mine * 8)
    out_slot = jnp.arange(devices * SLOTS, dtype=jnp.int32)[:, None]
    place_own = (lax.dynamic_index_in_dim(target, me, 0) == out_slot).astype(jnp.bfloat16)
    place_oth = (lax.dynamic_index_in_dim(target, 1 - me, 0) == out_slot).astype(jnp.bfloat16)
    sending = (
        jnp.dot(place_own, emb[0], preferred_element_type=jnp.float32)
        + jnp.dot(place_oth, emb_recv, preferred_element_type=jnp.float32)
    ).astype(jnp.bfloat16)
    got = lax.all_to_all(
        sending.reshape(devices, SLOTS, half), "dp", split_axis=0, concat_axis=0, tiled=True
    )
    enc_own = enc_own.reshape(mine, seq, half)
    enc_recv = enc_recv.reshape(mine, seq, half)
    first = me == 0
    encoded = jnp.concatenate(
        [jnp.where(first, enc_own, enc_recv), jnp.where(first, enc_recv, enc_own)], 0
    )
    got, encoded = lax.optimization_barrier((got, encoded))
    index_part = got[:, : SLOTS - 1].astype(jnp.float32).reshape(1, devices * (SLOTS - 1), half)
    return (encoded, index_part)


def solution(mesh):
    return jax.shard_map(
        shards,
        mesh=mesh,
        in_specs=(
            P("dp", None, "mp"),
            P("dp", None),
            P("dp"),
            P("dp", None),
            P(None, None, "mp"),
            P("mp", None),
            P(),
            P(None, "mp"),
            P("mp", None),
            P(),
        ),
        out_specs=(P("dp", None, "mp"), P("dp", None, "mp")),
        check_vma=False,
    )
```

```python
import math

import jax
import jax.numpy as jnp
from jax import lax
from jax.experimental import pallas as pl
from jax.experimental.pallas import tpu as pltpu
from jax.sharding import PartitionSpec as P

HD = 64
TILE = 1024
PART = 896
SLOTS = 4
SWAP = [(0, 1), (1, 0)]
LANES = 128
FACTS = 8


def gelu(x):
    half = 0.5 * x
    return half + half * lax.erf(x * math.sqrt(0.5))


def norm(values, gain):
    mean = jnp.mean(values, -1, keepdims=True)
    centred = values - mean
    var = jnp.mean(centred * centred, -1, keepdims=True)
    return centred * lax.rsqrt(var + 1e-05) * gain


def pack_kernel(dest, doc_ids, tokens, out, raw, staged, empty, in_sems, out_sems, empty_sem):
    rows, seq, width = tokens.shape
    body = seq * width // LANES
    loads = [pltpu.make_async_copy(tokens.at[r], raw.at[r], in_sems.at[r]) for r in range(rows)]
    for copy in loads:
        copy.start()
    empty[...] = jnp.zeros_like(empty)
    clear = pltpu.make_async_copy(empty, out.at[:, pl.ds(body, FACTS)], empty_sem)
    clear.start()
    lane = lax.broadcasted_iota(jnp.int32, (rows, LANES), 1)
    facts = jnp.where(lane == 0, lax.broadcasted_iota(jnp.int32, (rows, LANES), 0) + 1, 0)
    ids = doc_ids[...]
    for k in range(1, 4):
        bound = jnp.sum((ids < k).astype(jnp.float32), -1, keepdims=True).astype(jnp.int32)
        facts = jnp.where(lane == k, bound, facts)
    facts = facts.astype(jnp.float32)
    stores = []
    for r in range(rows):
        staged[r, body:, :] = jnp.broadcast_to(facts[r : r + 1, :], (FACTS, LANES)).astype(
            jnp.bfloat16
        )
        loads[r].wait()
        for c in range(width // LANES):
            staged[r, c * seq : (c + 1) * seq, :] = raw[r, :, c * LANES : (c + 1) * LANES]
        if r == 0:
            clear.wait()
        stores.append(
            pltpu.make_async_copy(
                staged.at[r], out.at[lax.div(dest[r], rows)], out_sems.at[r]
            )
        )
        stores[-1].start()
    for copy in stores:
        copy.wait()


def pack(dest, doc_ids, tokens, slots):
    rows, seq, width = tokens.shape
    body = seq * width // LANES
    return pl.pallas_call(
        pack_kernel,
        out_shape=jax.ShapeDtypeStruct((slots, body + FACTS, LANES), tokens.dtype),
        in_specs=[
            pl.BlockSpec(memory_space=pltpu.SMEM),
            pl.BlockSpec(memory_space=pltpu.VMEM),
            pl.BlockSpec(memory_space=pltpu.HBM),
        ],
        out_specs=pl.BlockSpec(memory_space=pltpu.HBM),
        scratch_shapes=[
            pltpu.VMEM((rows, seq, width), tokens.dtype),
            pltpu.VMEM((rows, body + FACTS, LANES), tokens.dtype),
            pltpu.VMEM((slots, FACTS, LANES), tokens.dtype),
            pltpu.SemaphoreType.DMA((rows,)),
            pltpu.SemaphoreType.DMA((rows,)),
            pltpu.SemaphoreType.DMA,
        ],
        compiler_params=pltpu.CompilerParams(vmem_limit_bytes=60 * 1024 * 1024),
        name="pack_rows",
    )(dest, doc_ids, tokens)


def unpack_kernel(core, received, out, info, facts, table, fact_sem, info_sem, sems):
    rows, body, _ = out.shape
    slots = received.shape[0]
    load = pltpu.make_async_copy(received.at[:, pl.ds(body, FACTS)], facts, fact_sem)
    load.start()
    load.wait()
    values = facts[...].astype(jnp.float32)
    shape = (slots, FACTS, LANES)
    here = values[:, :, :1] == (lax.broadcasted_iota(jnp.int32, shape, 2) + 1).astype(jnp.float32)
    source = lax.broadcasted_iota(jnp.int32, shape, 0).astype(jnp.float32)
    result = jnp.sum(jnp.where(here, source, 0.0), 0)
    kind = lax.broadcasted_iota(jnp.int32, (FACTS, LANES), 0)
    for k in range(1, 4):
        bound = jnp.sum(jnp.where(here, values[:, :, k : k + 1], 0.0), 0)
        result = jnp.where(kind == k, bound, result)
    table[...] = result.astype(jnp.int32)
    keep = pltpu.make_async_copy(table, info, info_sem)
    keep.start()
    keep.wait()
    first = (1 - core[0]) * rows
    copies = [
        pltpu.make_async_copy(
            received.at[info[0, first + r], pl.ds(0, body)], out.at[r], sems.at[r]
        )
        for r in range(rows)
    ]
    for copy in copies:
        copy.start()
    for copy in copies:
        copy.wait()


def unpack(core, received, rows):
    slots = received.shape[0]
    body = received.shape[1] - FACTS
    return pl.pallas_call(
        unpack_kernel,
        out_shape=(
            jax.ShapeDtypeStruct((rows, body, LANES), received.dtype),
            jax.ShapeDtypeStruct((FACTS, LANES), jnp.int32),
        ),
        in_specs=[
            pl.BlockSpec(memory_space=pltpu.SMEM),
            pl.BlockSpec(memory_space=pltpu.HBM),
        ],
        out_specs=(
            pl.BlockSpec(memory_space=pltpu.VMEM),
            pl.BlockSpec(memory_space=pltpu.SMEM),
        ),
        scratch_shapes=[
            pltpu.VMEM((slots, FACTS, LANES), received.dtype),
            pltpu.VMEM((FACTS, LANES), jnp.int32),
            pltpu.SemaphoreType.DMA,
            pltpu.SemaphoreType.DMA,
            pltpu.SemaphoreType.DMA((rows,)),
        ],
        compiler_params=pltpu.CompilerParams(vmem_limit_bytes=60 * 1024 * 1024),
        name="unpack_rows",
    )(core, received)


def layer_kernel(
    core,
    info,
    received,
    x_other,
    wq_own,
    wq_oth,
    wo_own,
    wo_oth,
    wu_own,
    wu_oth,
    wd_own,
    wd_oth,
    gain_attn,
    gain_ffn,
    enc_own,
    enc_oth,
    emb,
    x_scr,
    qkv_scr,
    acc_scr,
    wq,
    wo,
    wu,
    wd,
    row_sems,
    x_sem,
    q_sems,
    w_sems,
    out_sems,
):
    rows = x_scr.shape[0]
    seq = HD
    tokens, half = enc_own.shape
    model = 2 * half
    chunks = model // LANES
    body = half * seq // LANES
    me = core[0]
    first_row = me * rows
    own_at = pl.ds(pl.multiple_of(me * body, body), body)
    oth_at = pl.ds(pl.multiple_of((1 - me) * body, body), body)
    x_copies = [
        pltpu.make_async_copy(
            received.at[info[0, first_row + r], pl.ds(0, body)], x_scr.at[r, own_at], row_sems.at[r]
        )
        for r in range(rows)
    ]
    x_copies.append(pltpu.make_async_copy(x_other, x_scr.at[:, oth_at], x_sem))
    q_copies = [
        pltpu.make_async_copy(src.at[i], wq.at[3 * h + i], q_sems.at[3 * h + i])
        for h, src in enumerate((wq_own, wq_oth))
        for i in range(3)
    ]
    w_copies = [
        pltpu.make_async_copy(src, dst.at[h], w_sems.at[i, h])
        for i, (srcs, dst) in enumerate((((wo_own, wo_oth), wo), ((wu_own, wu_oth), wu), ((wd_own, wd_oth), wd)))
        for h, src in enumerate(srcs)
    ]
    for copy in x_copies + q_copies[:2]:
        copy.start()
    for copy in x_copies:
        copy.wait()
    for copy in q_copies[2:]:
        copy.start()

    def inputs(first, count):
        pieces = [
            x_scr[pl.ds(first, count), c * seq : (c + 1) * seq, :].reshape(count * seq, LANES)
            for c in range(chunks)
        ]
        return jnp.concatenate(pieces, 1)

    for n in range(6):
        q_copies[n].wait()
        w_copies[n].start()
        qkv_scr[:, n * half : (n + 1) * half] = jnp.dot(
            inputs(0, rows), wq[n], preferred_element_type=jnp.float32
        ).astype(jnp.bfloat16)

    pair = 2 * HD
    block = (lax.broadcasted_iota(jnp.int32, (pair, pair), 0) < HD) == (
        lax.broadcasted_iota(jnp.int32, (pair, pair), 1) < HD
    )
    lane_low = lax.broadcasted_iota(jnp.int32, (seq, pair), 1) < HD
    key_pos = lax.broadcasted_iota(jnp.int32, (seq, pair), 0)
    query_pos = lax.broadcasted_iota(jnp.int32, (seq, pair), 1) % HD
    per_half = half // pair

    def attend(r, carry):
        here = pl.ds(pl.multiple_of(r * seq, seq), seq)
        bounds = [info[k, first_row + r] for k in range(1, 4)]
        key_seg = sum([(key_pos >= b).astype(jnp.int32) for b in bounds])
        query_seg = sum([(query_pos >= b).astype(jnp.int32) for b in bounds])
        same = key_seg == query_seg
        scores = []
        for p in range(2 * per_half):
            at = (p // per_half) * 3 * half + (p % per_half) * pair
            q = qkv_scr[here, at : at + pair]
            k = qkv_scr[here, at + half : at + half + pair]
            spread = jnp.where(block, jnp.concatenate([q, q], 0), jnp.zeros((), q.dtype))
            scores.append(
                lax.dot_general(
                    k, spread, (((1,), (1,)), ((), ())), preferred_element_type=jnp.float32
                )
            )
        probs = []
        for score in scores:
            score = jnp.where(same, score * (1.0 / math.sqrt(HD)), jnp.float32(-1e30))
            weight = jnp.exp(score - jnp.max(score, 0, keepdims=True))
            probs.append(
                (weight * (1.0 / jnp.sum(weight, 0, keepdims=True))).astype(jnp.bfloat16)
            )
        mixed = []
        for p in range(2 * per_half):
            at = (p // per_half) * 3 * half + 2 * half + (p % per_half) * pair
            mixed.append(
                lax.dot_general(
                    probs[p],
                    qkv_scr[here, at : at + pair],
                    (((0,), (0,)), ((), ())),
                    preferred_element_type=jnp.float32,
                )
            )
        for p in range(2 * per_half):
            at = (p // per_half) * 3 * half + (p % per_half) * pair
            qkv_scr[here, at : at + pair] = jnp.where(
                lane_low, mixed[p][:seq], mixed[p][seq:]
            ).astype(jnp.bfloat16)
        return carry

    lax.fori_loop(0, rows, attend, 0)

    for copy in w_copies[:2]:
        copy.wait()
    count = 2
    for m in range(rows // count):
        at = slice(m * count * seq, (m + 1) * count * seq)
        mixed = jnp.dot(qkv_scr[at, :half], wo[0], preferred_element_type=jnp.float32)
        mixed += jnp.dot(
            qkv_scr[at, 3 * half : 4 * half], wo[1], preferred_element_type=jnp.float32
        )
        mixed = mixed + inputs(m * count, count).astype(jnp.float32)
        normed = norm(mixed, gain_attn[...]).astype(jnp.bfloat16)
        qkv_scr[at, half : 3 * half] = normed
        acc_scr[at, :] = normed.astype(jnp.float32)

    for copy in w_copies[2:]:
        copy.wait()
    tiles = wu.shape[2] // TILE
    parts = tokens // PART

    def feed(t, carry):
        h = t // (tiles * parts)
        at = pl.ds(pl.multiple_of((t % tiles) * TILE, TILE), TILE)
        here = pl.ds(pl.multiple_of((t // tiles) % parts * PART, PART), PART)
        normed = qkv_scr[here, half : 3 * half]
        up = jnp.dot(normed, wu[h, :, at], preferred_element_type=jnp.float32)
        acc_scr[here, :] += jnp.dot(
            gelu(up).astype(jnp.bfloat16), wd[h, at, :], preferred_element_type=jnp.float32
        )
        return carry

    lax.fori_loop(0, 2 * tiles * parts, feed, 0)

    two = 2 * seq
    doc = lax.broadcasted_iota(jnp.int32, (16, two), 0)
    position = lax.broadcasted_iota(jnp.int32, (16, two), 1)
    same_row = (doc < 8) == (position < seq)
    doc = doc % 8
    own_col = pl.ds(pl.multiple_of(me * half, half), half)
    oth_col = pl.ds(pl.multiple_of((1 - me) * half, half), half)
    outs = []
    for m in range(rows // 2):
        at = slice(m * two, (m + 1) * two)
        encoded = norm(acc_scr[at, :], gain_ffn[...]).astype(jnp.bfloat16)
        qkv_scr[at, : 2 * half] = encoded
        for i, (col, out) in enumerate(((own_col, enc_own), (oth_col, enc_oth))):
            outs.append(
                pltpu.make_async_copy(
                    qkv_scr.at[pl.ds(m * two, two), col],
                    out.at[pl.ds(m * two, two)],
                    out_sems.at[m, i],
                )
            )
            outs[-1].start()
        seg = jnp.zeros_like(position)
        for k in range(1, 4):
            bound = jnp.where(
                position < seq,
                info[k, first_row + 2 * m],
                info[k, first_row + 2 * m + 1] + seq,
            )
            seg += (position >= bound).astype(jnp.int32)
        member = ((seg == doc) & same_row).astype(jnp.float32)
        total = jnp.sum(member, -1, keepdims=True)
        pooled = jnp.dot(member.astype(jnp.bfloat16), encoded, preferred_element_type=jnp.float32)
        pooled = pooled * (1.0 / jnp.maximum(total, 1.0))
        square = jnp.mean(pooled * pooled, -1, keepdims=True)
        embedded = (pooled * lax.rsqrt(square + 1e-06)).astype(jnp.bfloat16)
        emb[me, m * 16 : (m + 1) * 16, :] = embedded[:, :half]
        emb[1 - me, m * 16 : (m + 1) * 16, :] = embedded[:, half:]
    for copy in outs:
        copy.wait()


def layer(core, info, received, x_other, weights, gain_attn, gain_ffn):
    rows, body, _ = x_other.shape
    half = body * LANES // HD
    tokens = rows * HD
    model = 2 * half
    wu, wd = weights[4], weights[6]
    flops = 2 * tokens * model * (3 * model + model + 4 * wu.shape[1])
    any_spec = pl.BlockSpec(memory_space=pltpu.HBM)
    vmem = pl.BlockSpec(memory_space=pltpu.VMEM)
    return pl.pallas_call(
        layer_kernel,
        out_shape=(
            jax.ShapeDtypeStruct((tokens, half), jnp.bfloat16),
            jax.ShapeDtypeStruct((tokens, half), jnp.bfloat16),
            jax.ShapeDtypeStruct((2, rows * 8, half), jnp.bfloat16),
        ),
        in_specs=[pl.BlockSpec(memory_space=pltpu.SMEM)] * 2
        + [any_spec] * 10
        + [vmem] * 2,
        out_specs=(any_spec, any_spec, vmem),
        scratch_shapes=[
            pltpu.VMEM((rows, 2 * body, LANES), jnp.bfloat16),
            pltpu.VMEM((tokens, 3 * model), jnp.bfloat16),
            pltpu.VMEM((tokens, model), jnp.float32),
            pltpu.VMEM((6, model, half), jnp.bfloat16),
            pltpu.VMEM((2, half, model), jnp.bfloat16),
            pltpu.VMEM((2,) + wu.shape, jnp.bfloat16),
            pltpu.VMEM((2,) + wd.shape, jnp.bfloat16),
            pltpu.SemaphoreType.DMA((rows,)),
            pltpu.SemaphoreType.DMA,
            pltpu.SemaphoreType.DMA((6,)),
            pltpu.SemaphoreType.DMA((3, 2)),
            pltpu.SemaphoreType.DMA((rows // 2, 2)),
        ],
        compiler_params=pltpu.CompilerParams(vmem_limit_bytes=60 * 1024 * 1024),
        cost_estimate=pl.CostEstimate(
            flops=flops, bytes_accessed=28 * 1024 * 1024, transcendentals=0
        ),
        name="layer",
    )(core, info, received, x_other, *weights, gain_attn, gain_ffn)


def shards(tokens, doc_ids, dest, owner, w_qkv, w_out, gain_attn, w_up, w_down, gain_ffn):
    devices = lax.axis_size("dp")
    row_count, seq, half = tokens.shape
    docs = owner.shape[1]
    mine = row_count // 2
    me = lax.axis_index("mp")

    qkv_own = jnp.moveaxis(w_qkv, 1, 0)
    weights = []
    for own in (qkv_own, w_out, w_up, w_down):
        weights += [own, lax.ppermute(own, "mp", SWAP)]

    received = lax.all_to_all(
        pack(dest, doc_ids, tokens, devices), "dp", split_axis=0, concat_axis=0, tiled=True
    )
    core = me.astype(jnp.int32)[None]
    x_send, info = unpack(core, received, mine)
    x_other = lax.ppermute(x_send, "mp", SWAP)
    enc_own, enc_oth, emb = layer(
        core, info, received, x_other, weights, gain_attn[None], gain_ffn[None]
    )
    emb_recv = lax.ppermute(emb[1], "mp", SWAP)
    enc_oth, emb_recv = lax.optimization_barrier((enc_oth, emb_recv))
    enc_recv = lax.ppermute(enc_oth, "mp", SWAP)

    owners = owner.reshape(-1)
    position = jnp.arange(row_count * docs, dtype=jnp.int32)
    earlier = (owners[:, None] == owners[None, :]) & (position[None, :] < position[:, None])
    rank = jnp.sum(earlier.astype(jnp.int32), -1)
    target = jnp.pad(
        (owners * SLOTS + rank).reshape(2, mine, docs), ((0, 0), (0, 0), (0, 8 - docs)),
        constant_values=-1,
    ).reshape(2, mine * 8)
    out_slot = jnp.arange(devices * SLOTS, dtype=jnp.int32)[:, None]
    place_own = (lax.dynamic_index_in_dim(target, me, 0) == out_slot).astype(jnp.bfloat16)
    place_oth = (lax.dynamic_index_in_dim(target, 1 - me, 0) == out_slot).astype(jnp.bfloat16)
    sending = (
        jnp.dot(place_own, emb[0], preferred_element_type=jnp.float32)
        + jnp.dot(place_oth, emb_recv, preferred_element_type=jnp.float32)
    ).astype(jnp.bfloat16)
    got = lax.all_to_all(
        sending.reshape(devices, SLOTS, half), "dp", split_axis=0, concat_axis=0, tiled=True
    )
    enc_own = enc_own.reshape(mine, seq, half)
    enc_recv = enc_recv.reshape(mine, seq, half)
    first = me == 0
    encoded = jnp.concatenate(
        [jnp.where(first, enc_own, enc_recv), jnp.where(first, enc_recv, enc_own)], 0
    )
    got, encoded = lax.optimization_barrier((got, encoded))
    index_part = got[:, : SLOTS - 1].astype(jnp.float32).reshape(1, devices * (SLOTS - 1), half)
    return (encoded, index_part)


def solution(mesh):
    return jax.shard_map(
        shards,
        mesh=mesh,
        in_specs=(
            P("dp", None, "mp"),
            P("dp", None),
            P("dp"),
            P("dp", None),
            P(None, None, "mp"),
            P("mp", None),
            P(),
            P(None, "mp"),
            P("mp", None),
            P(),
        ),
        out_specs=(P("dp", None, "mp"), P("dp", None, "mp")),
        check_vma=False,
    )
```

```python
import math

import jax
import jax.numpy as jnp
from jax import lax
from jax.experimental import pallas as pl
from jax.experimental.pallas import tpu as pltpu
from jax.sharding import PartitionSpec as P

HD = 64
TILE = 1024
PART = 896
SLOTS = 4
SWAP = [(0, 1), (1, 0)]
LANES = 128
FACTS = 8


def gelu(x):
    half = 0.5 * x
    return half + half * lax.erf(x * math.sqrt(0.5))


def norm(values, gain):
    mean = jnp.mean(values, -1, keepdims=True)
    centred = values - mean
    var = jnp.mean(centred * centred, -1, keepdims=True)
    return centred * lax.rsqrt(var + 1e-05) * gain


def pack_kernel(dest, doc_ids, tokens, out, raw, staged, empty, in_sems, out_sems, empty_sem):
    rows, seq, width = tokens.shape
    body = seq * width // LANES
    loads = [pltpu.make_async_copy(tokens.at[r], raw.at[r], in_sems.at[r]) for r in range(rows)]
    for copy in loads:
        copy.start()
    empty[...] = jnp.zeros_like(empty)
    clear = pltpu.make_async_copy(empty, out.at[:, pl.ds(body, FACTS)], empty_sem)
    clear.start()
    lane = lax.broadcasted_iota(jnp.int32, (rows, LANES), 1)
    facts = jnp.where(lane == 0, lax.broadcasted_iota(jnp.int32, (rows, LANES), 0) + 1, 0)
    ids = doc_ids[...]
    for k in range(1, 4):
        bound = jnp.sum((ids < k).astype(jnp.float32), -1, keepdims=True).astype(jnp.int32)
        facts = jnp.where(lane == k, bound, facts)
    facts = facts.astype(jnp.float32)
    stores = []
    for r in range(rows):
        staged[r, body:, :] = jnp.broadcast_to(facts[r : r + 1, :], (FACTS, LANES)).astype(
            jnp.bfloat16
        )
        loads[r].wait()
        for c in range(width // LANES):
            staged[r, c * seq : (c + 1) * seq, :] = raw[r, :, c * LANES : (c + 1) * LANES]
        if r == 0:
            clear.wait()
        stores.append(
            pltpu.make_async_copy(
                staged.at[r], out.at[lax.div(dest[r], rows)], out_sems.at[r]
            )
        )
        stores[-1].start()
    for copy in stores:
        copy.wait()


def pack(dest, doc_ids, tokens, slots):
    rows, seq, width = tokens.shape
    body = seq * width // LANES
    return pl.pallas_call(
        pack_kernel,
        out_shape=jax.ShapeDtypeStruct((slots, body + FACTS, LANES), tokens.dtype),
        in_specs=[
            pl.BlockSpec(memory_space=pltpu.SMEM),
            pl.BlockSpec(memory_space=pltpu.VMEM),
            pl.BlockSpec(memory_space=pltpu.HBM),
        ],
        out_specs=pl.BlockSpec(memory_space=pltpu.HBM),
        scratch_shapes=[
            pltpu.VMEM((rows, seq, width), tokens.dtype),
            pltpu.VMEM((rows, body + FACTS, LANES), tokens.dtype),
            pltpu.VMEM((slots, FACTS, LANES), tokens.dtype),
            pltpu.SemaphoreType.DMA((rows,)),
            pltpu.SemaphoreType.DMA((rows,)),
            pltpu.SemaphoreType.DMA,
        ],
        compiler_params=pltpu.CompilerParams(vmem_limit_bytes=60 * 1024 * 1024),
        name="pack_rows",
    )(dest, doc_ids, tokens)


def unpack_kernel(
    core, received, out, info, facts, table, scalars, staged, fact_sem, info_sem, sems, out_sem
):
    rows, body, _ = out.shape
    slots = received.shape[0]
    load = pltpu.make_async_copy(received.at[:, pl.ds(body, FACTS)], facts, fact_sem)
    load.start()
    load.wait()
    values = facts[...].astype(jnp.float32)
    shape = (slots, FACTS, LANES)
    here = values[:, :, :1] == (lax.broadcasted_iota(jnp.int32, shape, 2) + 1).astype(jnp.float32)
    source = lax.broadcasted_iota(jnp.int32, shape, 0).astype(jnp.float32)
    result = jnp.sum(jnp.where(here, source, 0.0), 0)
    table[0] = result.astype(jnp.int32)
    keep = pltpu.make_async_copy(table.at[0], scalars, info_sem.at[0])
    keep.start()
    keep.wait()
    first = (1 - core[0]) * rows
    copies = [
        pltpu.make_async_copy(
            received.at[scalars[0, first + r], pl.ds(0, body)], staged.at[r], sems.at[r]
        )
        for r in range(rows)
    ]
    for copy in copies:
        copy.start()
    kind = lax.broadcasted_iota(jnp.int32, (FACTS, LANES), 0)
    for k in range(1, 4):
        bound = jnp.sum(jnp.where(here, values[:, :, k : k + 1], 0.0), 0)
        result = jnp.where(kind == k, bound, result)
    table[1] = result.astype(jnp.int32)
    keep = pltpu.make_async_copy(table.at[1], info, info_sem.at[1])
    keep.start()
    for copy in copies:
        copy.wait()
    store = pltpu.make_async_copy(staged, out, out_sem)
    store.start()
    store.wait()
    keep.wait()


def unpack(core, received, rows):
    slots = received.shape[0]
    body = received.shape[1] - FACTS
    hbm = pl.BlockSpec(memory_space=pltpu.HBM)
    return pl.pallas_call(
        unpack_kernel,
        out_shape=(
            jax.ShapeDtypeStruct((rows, body, LANES), received.dtype),
            jax.ShapeDtypeStruct((FACTS, LANES), jnp.int32),
        ),
        in_specs=[pl.BlockSpec(memory_space=pltpu.SMEM), hbm],
        out_specs=(hbm, hbm),
        scratch_shapes=[
            pltpu.VMEM((slots, FACTS, LANES), received.dtype),
            pltpu.VMEM((2, FACTS, LANES), jnp.int32),
            pltpu.SMEM((FACTS, LANES), jnp.int32),
            pltpu.VMEM((rows, body, LANES), received.dtype),
            pltpu.SemaphoreType.DMA,
            pltpu.SemaphoreType.DMA((2,)),
            pltpu.SemaphoreType.DMA((rows,)),
            pltpu.SemaphoreType.DMA,
        ],
        compiler_params=pltpu.CompilerParams(vmem_limit_bytes=60 * 1024 * 1024),
        name="unpack_rows",
    )(core, received)


def layer_kernel(
    core,
    table,
    received,
    x_other,
    wq_own,
    wq_oth,
    wo_own,
    wo_oth,
    wu_own,
    wu_oth,
    wd_own,
    wd_oth,
    gain_attn,
    gain_ffn,
    enc_own,
    enc_oth,
    emb_own,
    emb_oth,
    info,
    x_scr,
    qkv_scr,
    emb_scr,
    acc_scr,
    wq,
    wo,
    wu,
    wd,
    row_sems,
    x_sem,
    q_sems,
    w_sems,
    info_sem,
    out_sems,
):
    rows = x_scr.shape[0]
    seq = HD
    tokens, half = enc_own.shape
    model = 2 * half
    chunks = model // LANES
    body = half * seq // LANES
    me = core[0]
    first_row = me * rows
    facts = pltpu.make_async_copy(table, info, info_sem)
    facts.start()
    own_at = pl.ds(pl.multiple_of(me * body, body), body)
    oth_at = pl.ds(pl.multiple_of((1 - me) * body, body), body)
    x_copies = [pltpu.make_async_copy(x_other, x_scr.at[:, oth_at], x_sem)]
    q_copies = [
        pltpu.make_async_copy(src.at[i], wq.at[3 * h + i], q_sems.at[3 * h + i])
        for h, src in enumerate((wq_own, wq_oth))
        for i in range(3)
    ]
    for copy in x_copies + q_copies[:2]:
        copy.start()
    facts.wait()
    row_copies = [
        pltpu.make_async_copy(
            received.at[info[0, first_row + r], pl.ds(0, body)], x_scr.at[r, own_at], row_sems.at[r]
        )
        for r in range(rows)
    ]
    w_pairs = ((wo_own, wo_oth, wo), (wu_own, wu_oth, wu), (wd_own, wd_oth, wd))
    w_copies = [
        pltpu.make_async_copy(pair[h], pair[2].at[h], w_sems.at[i, h])
        for i, pair in enumerate(w_pairs)
        for h in range(2)
    ]
    for copy in row_copies:
        copy.start()
    for copy in x_copies + row_copies:
        copy.wait()
    for copy in q_copies[2:]:
        copy.start()

    def inputs(first, count):
        pieces = [
            x_scr[pl.ds(first, count), c * seq : (c + 1) * seq, :].reshape(count * seq, LANES)
            for c in range(chunks)
        ]
        return jnp.concatenate(pieces, 1)

    for n in range(6):
        q_copies[n].wait()
        w_copies[n].start()
        qkv_scr[:, n * half : (n + 1) * half] = jnp.dot(
            inputs(0, rows), wq[n], preferred_element_type=jnp.float32
        ).astype(jnp.bfloat16)

    pair = 2 * HD
    block = (lax.broadcasted_iota(jnp.int32, (pair, pair), 0) < HD) == (
        lax.broadcasted_iota(jnp.int32, (pair, pair), 1) < HD
    )
    lane_low = lax.broadcasted_iota(jnp.int32, (seq, pair), 1) < HD
    key_pos = lax.broadcasted_iota(jnp.int32, (seq, pair), 0)
    query_pos = lax.broadcasted_iota(jnp.int32, (seq, pair), 1) % HD
    per_half = half // pair

    def attend(r, carry):
        here = pl.ds(pl.multiple_of(r * seq, seq), seq)
        bounds = [info[k, first_row + r] for k in range(1, 4)]
        key_seg = sum([(key_pos >= b).astype(jnp.int32) for b in bounds])
        query_seg = sum([(query_pos >= b).astype(jnp.int32) for b in bounds])
        same = key_seg == query_seg
        scores = []
        for p in range(2 * per_half):
            at = (p // per_half) * 3 * half + (p % per_half) * pair
            q = qkv_scr[here, at : at + pair]
            k = qkv_scr[here, at + half : at + half + pair]
            spread = jnp.where(block, jnp.concatenate([q, q], 0), jnp.zeros((), q.dtype))
            scores.append(
                lax.dot_general(
                    k, spread, (((1,), (1,)), ((), ())), preferred_element_type=jnp.float32
                )
            )
        probs = []
        for score in scores:
            score = jnp.where(same, score * (1.0 / math.sqrt(HD)), jnp.float32(-1e30))
            weight = jnp.exp(score - jnp.max(score, 0, keepdims=True))
            probs.append(
                (weight * (1.0 / jnp.sum(weight, 0, keepdims=True))).astype(jnp.bfloat16)
            )
        mixed = []
        for p in range(2 * per_half):
            at = (p // per_half) * 3 * half + 2 * half + (p % per_half) * pair
            mixed.append(
                lax.dot_general(
                    probs[p],
                    qkv_scr[here, at : at + pair],
                    (((0,), (0,)), ((), ())),
                    preferred_element_type=jnp.float32,
                )
            )
        for p in range(2 * per_half):
            at = (p // per_half) * 3 * half + (p % per_half) * pair
            qkv_scr[here, at : at + pair] = jnp.where(
                lane_low, mixed[p][:seq], mixed[p][seq:]
            ).astype(jnp.bfloat16)
        return carry

    lax.fori_loop(0, rows, attend, 0)

    for copy in w_copies[:2]:
        copy.wait()
    count = 2
    for m in range(rows // count):
        at = slice(m * count * seq, (m + 1) * count * seq)
        mixed = jnp.dot(qkv_scr[at, :half], wo[0], preferred_element_type=jnp.float32)
        mixed += jnp.dot(
            qkv_scr[at, 3 * half : 4 * half], wo[1], preferred_element_type=jnp.float32
        )
        mixed = mixed + inputs(m * count, count).astype(jnp.float32)
        normed = norm(mixed, gain_attn[...]).astype(jnp.bfloat16)
        qkv_scr[at, half : 3 * half] = normed
        acc_scr[at, :] = normed.astype(jnp.float32)

    for copy in w_copies[2:]:
        copy.wait()
    tiles = wu.shape[2] // TILE
    parts = tokens // PART

    def feed(t, carry):
        h = t // (tiles * parts)
        at = pl.ds(pl.multiple_of((t % tiles) * TILE, TILE), TILE)
        here = pl.ds(pl.multiple_of((t // tiles) % parts * PART, PART), PART)
        normed = qkv_scr[here, half : 3 * half]
        up = jnp.dot(normed, wu[h, :, at], preferred_element_type=jnp.float32)
        acc_scr[here, :] += jnp.dot(
            gelu(up).astype(jnp.bfloat16), wd[h, at, :], preferred_element_type=jnp.float32
        )
        return carry

    lax.fori_loop(0, 2 * tiles * parts, feed, 0)

    two = 2 * seq
    doc = lax.broadcasted_iota(jnp.int32, (16, two), 0)
    position = lax.broadcasted_iota(jnp.int32, (16, two), 1)
    same_row = (doc < 8) == (position < seq)
    doc = doc % 8
    own_col = pl.ds(pl.multiple_of(me * half, half), half)
    oth_col = pl.ds(pl.multiple_of((1 - me) * half, half), half)
    outs = []
    for m in range(rows // 2):
        at = slice(m * two, (m + 1) * two)
        encoded = norm(acc_scr[at, :], gain_ffn[...]).astype(jnp.bfloat16)
        qkv_scr[at, : 2 * half] = encoded
        for i, (col, out) in enumerate(((own_col, enc_own), (oth_col, enc_oth))):
            outs.append(
                pltpu.make_async_copy(
                    qkv_scr.at[pl.ds(m * two, two), col],
                    out.at[pl.ds(m * two, two)],
                    out_sems.at[m, i],
                )
            )
            outs[-1].start()
        seg = jnp.zeros_like(position)
        for k in range(1, 4):
            bound = jnp.where(
                position < seq,
                info[k, first_row + 2 * m],
                info[k, first_row + 2 * m + 1] + seq,
            )
            seg += (position >= bound).astype(jnp.int32)
        member = ((seg == doc) & same_row).astype(jnp.float32)
        total = jnp.sum(member, -1, keepdims=True)
        pooled = jnp.dot(member.astype(jnp.bfloat16), encoded, preferred_element_type=jnp.float32)
        pooled = pooled * (1.0 / jnp.maximum(total, 1.0))
        square = jnp.mean(pooled * pooled, -1, keepdims=True)
        embedded = (pooled * lax.rsqrt(square + 1e-06)).astype(jnp.bfloat16)
        emb_scr[0, m * 16 : (m + 1) * 16, :] = embedded[:, :half]
        emb_scr[1, m * 16 : (m + 1) * 16, :] = embedded[:, half:]
    for i, out in enumerate((emb_own, emb_oth)):
        which = me if i == 0 else 1 - me
        outs.append(pltpu.make_async_copy(emb_scr.at[which], out, out_sems.at[rows // 2, i]))
        outs[-1].start()
    for copy in outs:
        copy.wait()


def layer(core, table, received, x_other, weights, gain_attn, gain_ffn):
    rows, body, _ = x_other.shape
    half = body * LANES // HD
    tokens = rows * HD
    model = 2 * half
    wu, wd = weights[4], weights[6]
    flops = 2 * tokens * model * (3 * model + model + 4 * wu.shape[1])
    any_spec = pl.BlockSpec(memory_space=pltpu.HBM)
    vmem = pl.BlockSpec(memory_space=pltpu.VMEM)
    return pl.pallas_call(
        layer_kernel,
        out_shape=(
            jax.ShapeDtypeStruct((tokens, half), jnp.bfloat16),
            jax.ShapeDtypeStruct((tokens, half), jnp.bfloat16),
            jax.ShapeDtypeStruct((rows * 8, half), jnp.bfloat16),
            jax.ShapeDtypeStruct((rows * 8, half), jnp.bfloat16),
        ),
        in_specs=[pl.BlockSpec(memory_space=pltpu.SMEM)]
        + [any_spec] * 11
        + [vmem] * 2,
        out_specs=(any_spec,) * 4,
        scratch_shapes=[
            pltpu.SMEM(table.shape, jnp.int32),
            pltpu.VMEM((rows, 2 * body, LANES), jnp.bfloat16),
            pltpu.VMEM((tokens, 3 * model), jnp.bfloat16),
            pltpu.VMEM((2, rows * 8, half), jnp.bfloat16),
            pltpu.VMEM((tokens, model), jnp.float32),
            pltpu.VMEM((6, model, half), jnp.bfloat16),
            pltpu.VMEM((2, half, model), jnp.bfloat16),
            pltpu.VMEM((2,) + wu.shape, jnp.bfloat16),
            pltpu.VMEM((2,) + wd.shape, jnp.bfloat16),
            pltpu.SemaphoreType.DMA((rows,)),
            pltpu.SemaphoreType.DMA,
            pltpu.SemaphoreType.DMA((6,)),
            pltpu.SemaphoreType.DMA((3, 2)),
            pltpu.SemaphoreType.DMA,
            pltpu.SemaphoreType.DMA((rows // 2 + 1, 2)),
        ],
        compiler_params=pltpu.CompilerParams(vmem_limit_bytes=60 * 1024 * 1024),
        cost_estimate=pl.CostEstimate(
            flops=flops, bytes_accessed=28 * 1024 * 1024, transcendentals=0
        ),
        name="layer",
    )(core, table, received, x_other, *weights, gain_attn, gain_ffn)


def shards(tokens, doc_ids, dest, owner, w_qkv, w_out, gain_attn, w_up, w_down, gain_ffn):
    devices = lax.axis_size("dp")
    row_count, seq, half = tokens.shape
    docs = owner.shape[1]
    mine = row_count // 2
    me = lax.axis_index("mp")

    qkv_own = jnp.moveaxis(w_qkv, 1, 0)
    weights = []
    for own in (qkv_own, w_out, w_up, w_down):
        weights += [own, lax.ppermute(own, "mp", SWAP)]

    received = lax.all_to_all(
        pack(dest, doc_ids, tokens, devices), "dp", split_axis=0, concat_axis=0, tiled=True
    )
    core = me.astype(jnp.int32)[None]
    x_send, info = unpack(core, received, mine)
    x_other = lax.ppermute(x_send, "mp", SWAP)
    enc_own, enc_oth, emb_own, emb_oth = layer(
        core, info, received, x_other, weights, gain_attn[None], gain_ffn[None]
    )
    emb_recv = lax.ppermute(emb_oth, "mp", SWAP)
    enc_oth, emb_recv = lax.optimization_barrier((enc_oth, emb_recv))
    enc_recv = lax.ppermute(enc_oth, "mp", SWAP)

    owners = owner.reshape(-1)
    position = jnp.arange(row_count * docs, dtype=jnp.int32)
    earlier = (owners[:, None] == owners[None, :]) & (position[None, :] < position[:, None])
    rank = jnp.sum(earlier.astype(jnp.int32), -1)
    target = jnp.pad(
        (owners * SLOTS + rank).reshape(2, mine, docs), ((0, 0), (0, 0), (0, 8 - docs)),
        constant_values=-1,
    ).reshape(2, mine * 8)
    out_slot = jnp.arange(devices * SLOTS, dtype=jnp.int32)[:, None]
    place_own = (lax.dynamic_index_in_dim(target, me, 0) == out_slot).astype(jnp.bfloat16)
    place_oth = (lax.dynamic_index_in_dim(target, 1 - me, 0) == out_slot).astype(jnp.bfloat16)
    sending = (
        jnp.dot(place_own, emb_own, preferred_element_type=jnp.float32)
        + jnp.dot(place_oth, emb_recv, preferred_element_type=jnp.float32)
    ).astype(jnp.bfloat16)
    got = lax.all_to_all(
        sending.reshape(devices, SLOTS, half), "dp", split_axis=0, concat_axis=0, tiled=True
    )
    enc_own = enc_own.reshape(mine, seq, half)
    enc_recv = enc_recv.reshape(mine, seq, half)
    first = me == 0
    encoded = jnp.concatenate(
        [jnp.where(first, enc_own, enc_recv), jnp.where(first, enc_recv, enc_own)], 0
    )
    got, encoded = lax.optimization_barrier((got, encoded))
    index_part = got[:, : SLOTS - 1].astype(jnp.float32).reshape(1, devices * (SLOTS - 1), half)
    return (encoded, index_part)


def solution(mesh):
    return jax.shard_map(
        shards,
        mesh=mesh,
        in_specs=(
            P("dp", None, "mp"),
            P("dp", None),
            P("dp"),
            P("dp", None),
            P(None, None, "mp"),
            P("mp", None),
            P(),
            P(None, "mp"),
            P("mp", None),
            P(),
        ),
        out_specs=(P("dp", None, "mp"), P("dp", None, "mp")),
        check_vma=False,
    )
```

```python
import math

import jax
import jax.numpy as jnp
from jax import lax
from jax.experimental import pallas as pl
from jax.experimental.pallas import tpu as pltpu
from jax.sharding import PartitionSpec as P

HD = 64
TILE = 1024
PART = 896
SLOTS = 4
SWAP = [(0, 1), (1, 0)]
LANES = 128
FACTS = 8


def gelu(x):
    half = 0.5 * x
    return half + half * lax.erf(x * math.sqrt(0.5))


def norm(values, gain):
    mean = jnp.mean(values, -1, keepdims=True)
    centred = values - mean
    var = jnp.mean(centred * centred, -1, keepdims=True)
    return centred * lax.rsqrt(var + 1e-05) * gain


def pack_kernel(dest, doc_ids, tokens, out, raw, staged, empty, in_sems, out_sems, empty_sem):
    rows, seq, width = tokens.shape
    body = seq * width // LANES
    loads = [pltpu.make_async_copy(tokens.at[r], raw.at[r], in_sems.at[r]) for r in range(rows)]
    for copy in loads:
        copy.start()
    empty[...] = jnp.zeros_like(empty)
    clear = pltpu.make_async_copy(empty, out.at[:, pl.ds(body, FACTS)], empty_sem)
    clear.start()
    lane = lax.broadcasted_iota(jnp.int32, (rows, LANES), 1)
    facts = jnp.where(lane == 0, lax.broadcasted_iota(jnp.int32, (rows, LANES), 0) + 1, 0)
    ids = doc_ids[...]
    for k in range(1, 4):
        bound = jnp.sum((ids < k).astype(jnp.float32), -1, keepdims=True).astype(jnp.int32)
        facts = jnp.where(lane == k, bound, facts)
    facts = facts.astype(jnp.float32)
    stores = []
    for r in range(rows):
        staged[r, body:, :] = jnp.broadcast_to(facts[r : r + 1, :], (FACTS, LANES)).astype(
            jnp.bfloat16
        )
        loads[r].wait()
        for c in range(width // LANES):
            staged[r, c * seq : (c + 1) * seq, :] = raw[r, :, c * LANES : (c + 1) * LANES]
        if r == 0:
            clear.wait()
        stores.append(
            pltpu.make_async_copy(
                staged.at[r], out.at[lax.div(dest[r], rows)], out_sems.at[r]
            )
        )
        stores[-1].start()
    for copy in stores:
        copy.wait()


def pack(dest, doc_ids, tokens, slots):
    rows, seq, width = tokens.shape
    body = seq * width // LANES
    return pl.pallas_call(
        pack_kernel,
        out_shape=jax.ShapeDtypeStruct((slots, body + FACTS, LANES), tokens.dtype),
        in_specs=[
            pl.BlockSpec(memory_space=pltpu.SMEM),
            pl.BlockSpec(memory_space=pltpu.VMEM),
            pl.BlockSpec(memory_space=pltpu.HBM),
        ],
        out_specs=pl.BlockSpec(memory_space=pltpu.HBM),
        scratch_shapes=[
            pltpu.VMEM((rows, seq, width), tokens.dtype),
            pltpu.VMEM((rows, body + FACTS, LANES), tokens.dtype),
            pltpu.VMEM((slots, FACTS, LANES), tokens.dtype),
            pltpu.SemaphoreType.DMA((rows,)),
            pltpu.SemaphoreType.DMA((rows,)),
            pltpu.SemaphoreType.DMA,
        ],
        compiler_params=pltpu.CompilerParams(vmem_limit_bytes=60 * 1024 * 1024),
        name="pack_rows",
    )(dest, doc_ids, tokens)


def unpack_kernel(
    core, received, out, info, facts, table, scalars, staged, fact_sem, info_sem, sems, out_sem
):
    rows, body, _ = out.shape
    slots = received.shape[0]
    load = pltpu.make_async_copy(received.at[:, pl.ds(body, FACTS)], facts, fact_sem)
    load.start()
    load.wait()
    values = facts[...].astype(jnp.float32)
    shape = (slots, FACTS, LANES)
    here = values[:, :, :1] == (lax.broadcasted_iota(jnp.int32, shape, 2) + 1).astype(jnp.float32)
    source = lax.broadcasted_iota(jnp.int32, shape, 0).astype(jnp.float32)
    result = jnp.sum(jnp.where(here, source, 0.0), 0)
    table[0] = result.astype(jnp.int32)
    keep = pltpu.make_async_copy(table.at[0], scalars, info_sem.at[0])
    keep.start()
    keep.wait()
    first = (1 - core[0]) * rows
    copies = [
        pltpu.make_async_copy(
            received.at[scalars[0, first + r], pl.ds(0, body)], staged.at[r], sems.at[r]
        )
        for r in range(rows)
    ]
    for copy in copies:
        copy.start()
    kind = lax.broadcasted_iota(jnp.int32, (FACTS, LANES), 0)
    for k in range(1, 4):
        bound = jnp.sum(jnp.where(here, values[:, :, k : k + 1], 0.0), 0)
        result = jnp.where(kind == k, bound, result)
    table[1] = result.astype(jnp.int32)
    keep = pltpu.make_async_copy(table.at[1], info, info_sem.at[1])
    keep.start()
    for copy in copies:
        copy.wait()
    store = pltpu.make_async_copy(staged, out, out_sem)
    store.start()
    store.wait()
    keep.wait()


def unpack(core, received, rows):
    slots = received.shape[0]
    body = received.shape[1] - FACTS
    hbm = pl.BlockSpec(memory_space=pltpu.HBM)
    return pl.pallas_call(
        unpack_kernel,
        out_shape=(
            jax.ShapeDtypeStruct((rows, body, LANES), received.dtype),
            jax.ShapeDtypeStruct((FACTS, LANES), jnp.int32),
        ),
        in_specs=[pl.BlockSpec(memory_space=pltpu.SMEM), hbm],
        out_specs=(hbm, hbm),
        scratch_shapes=[
            pltpu.VMEM((slots, FACTS, LANES), received.dtype),
            pltpu.VMEM((2, FACTS, LANES), jnp.int32),
            pltpu.SMEM((FACTS, LANES), jnp.int32),
            pltpu.VMEM((rows, body, LANES), received.dtype),
            pltpu.SemaphoreType.DMA,
            pltpu.SemaphoreType.DMA((2,)),
            pltpu.SemaphoreType.DMA((rows,)),
            pltpu.SemaphoreType.DMA,
        ],
        compiler_params=pltpu.CompilerParams(vmem_limit_bytes=60 * 1024 * 1024),
        name="unpack_rows",
    )(core, received)


def layer_kernel(
    core,
    table,
    received,
    x_other,
    wq_own,
    wq_oth,
    wo_own,
    wo_oth,
    wu_own,
    wu_oth,
    wd_own,
    wd_oth,
    gain_attn,
    gain_ffn,
    enc_own,
    enc_oth,
    emb_own,
    emb_oth,
    info,
    x_scr,
    qkv_scr,
    emb_scr,
    acc_scr,
    wq,
    wo,
    wu,
    wd,
    row_sems,
    x_sem,
    q_sems,
    w_sems,
    info_sem,
    out_sems,
):
    rows = x_scr.shape[0]
    seq = HD
    tokens, half = enc_own.shape
    model = 2 * half
    chunks = model // LANES
    body = half * seq // LANES
    me = core[0]
    first_row = me * rows
    facts = pltpu.make_async_copy(table, info, info_sem)
    facts.start()
    own_at = pl.ds(pl.multiple_of(me * body, body), body)
    oth_at = pl.ds(pl.multiple_of((1 - me) * body, body), body)
    x_copies = [pltpu.make_async_copy(x_other, x_scr.at[:, oth_at], x_sem)]
    q_copies = [
        pltpu.make_async_copy(src.at[i], wq.at[3 * h + i], q_sems.at[3 * h + i])
        for h, src in enumerate((wq_own, wq_oth))
        for i in range(3)
    ]
    for copy in x_copies + q_copies[:2]:
        copy.start()
    facts.wait()
    row_copies = [
        pltpu.make_async_copy(
            received.at[info[0, first_row + r], pl.ds(0, body)], x_scr.at[r, own_at], row_sems.at[r]
        )
        for r in range(rows)
    ]
    w_pairs = ((wo_own, wo_oth, wo), (wu_own, wu_oth, wu), (wd_own, wd_oth, wd))
    w_copies = [
        pltpu.make_async_copy(pair[h], pair[2].at[h], w_sems.at[i, h])
        for i, pair in enumerate(w_pairs)
        for h in range(2)
    ]
    for copy in row_copies:
        copy.start()
    for copy in x_copies + row_copies:
        copy.wait()
    for copy in q_copies[2:]:
        copy.start()

    def inputs(first, count):
        pieces = [
            x_scr[pl.ds(first, count), c * seq : (c + 1) * seq, :].reshape(count * seq, LANES)
            for c in range(chunks)
        ]
        return jnp.concatenate(pieces, 1)

    for n in range(6):
        q_copies[n].wait()
        w_copies[n].start()
        qkv_scr[:, n * half : (n + 1) * half] = jnp.dot(
            inputs(0, rows), wq[n], preferred_element_type=jnp.float32
        ).astype(jnp.bfloat16)

    pair = 2 * HD
    block = (lax.broadcasted_iota(jnp.int32, (pair, pair), 0) < HD) == (
        lax.broadcasted_iota(jnp.int32, (pair, pair), 1) < HD
    )
    lane_low = lax.broadcasted_iota(jnp.int32, (seq, pair), 1) < HD
    key_pos = lax.broadcasted_iota(jnp.int32, (seq, pair), 0)
    query_pos = lax.broadcasted_iota(jnp.int32, (seq, pair), 1) % HD
    per_half = half // pair

    def attend(r, carry):
        here = pl.ds(pl.multiple_of(r * seq, seq), seq)
        bounds = [info[k, first_row + r] for k in range(1, 4)]
        key_seg = sum([(key_pos >= b).astype(jnp.int32) for b in bounds])
        query_seg = sum([(query_pos >= b).astype(jnp.int32) for b in bounds])
        same = key_seg == query_seg
        scores = []
        for p in range(2 * per_half):
            at = (p // per_half) * 3 * half + (p % per_half) * pair
            q = qkv_scr[here, at : at + pair]
            k = qkv_scr[here, at + half : at + half + pair]
            spread = jnp.where(block, jnp.concatenate([q, q], 0), jnp.zeros((), q.dtype))
            scores.append(
                lax.dot_general(
                    k, spread, (((1,), (1,)), ((), ())), preferred_element_type=jnp.float32
                )
            )
        probs = []
        for score in scores:
            score = jnp.where(same, score * (1.0 / math.sqrt(HD)), jnp.float32(-1e30))
            weight = jnp.exp(score - jnp.max(score, 0, keepdims=True))
            probs.append(
                (weight * (1.0 / jnp.sum(weight, 0, keepdims=True))).astype(jnp.bfloat16)
            )
        mixed = []
        for p in range(2 * per_half):
            at = (p // per_half) * 3 * half + 2 * half + (p % per_half) * pair
            mixed.append(
                lax.dot_general(
                    probs[p],
                    qkv_scr[here, at : at + pair],
                    (((0,), (0,)), ((), ())),
                    preferred_element_type=jnp.float32,
                )
            )
        for p in range(2 * per_half):
            at = (p // per_half) * 3 * half + (p % per_half) * pair
            qkv_scr[here, at : at + pair] = jnp.where(
                lane_low, mixed[p][:seq], mixed[p][seq:]
            ).astype(jnp.bfloat16)
        return carry

    lax.fori_loop(0, rows, attend, 0)

    for copy in w_copies[:2]:
        copy.wait()
    count = 2
    for m in range(rows // count):
        at = slice(m * count * seq, (m + 1) * count * seq)
        mixed = jnp.dot(qkv_scr[at, :half], wo[0], preferred_element_type=jnp.float32)
        mixed += jnp.dot(
            qkv_scr[at, 3 * half : 4 * half], wo[1], preferred_element_type=jnp.float32
        )
        mixed = mixed + inputs(m * count, count).astype(jnp.float32)
        normed = norm(mixed, gain_attn[...]).astype(jnp.bfloat16)
        qkv_scr[at, half : 3 * half] = normed
        acc_scr[at, :] = normed.astype(jnp.float32)

    for copy in w_copies[2:]:
        copy.wait()
    tiles = wu.shape[2] // TILE
    parts = tokens // PART

    def feed(t, carry):
        h = t // (tiles * parts)
        at = pl.ds(pl.multiple_of((t % tiles) * TILE, TILE), TILE)
        here = pl.ds(pl.multiple_of((t // tiles) % parts * PART, PART), PART)
        normed = qkv_scr[here, half : 3 * half]
        up = jnp.dot(normed, wu[h, :, at], preferred_element_type=jnp.float32)
        acc_scr[here, :] += jnp.dot(
            gelu(up).astype(jnp.bfloat16), wd[h, at, :], preferred_element_type=jnp.float32
        )
        return carry

    lax.fori_loop(0, 2 * tiles * parts, feed, 0)

    two = 2 * seq
    doc = lax.broadcasted_iota(jnp.int32, (16, two), 0)
    position = lax.broadcasted_iota(jnp.int32, (16, two), 1)
    same_row = (doc < 8) == (position < seq)
    doc = doc % 8
    own_col = pl.ds(pl.multiple_of(me * half, half), half)
    oth_col = pl.ds(pl.multiple_of((1 - me) * half, half), half)
    outs = []
    for m in range(rows // 2):
        at = slice(m * two, (m + 1) * two)
        encoded = norm(acc_scr[at, :], gain_ffn[...]).astype(jnp.bfloat16)
        qkv_scr[at, : 2 * half] = encoded
        for i, (col, out) in enumerate(((own_col, enc_own), (oth_col, enc_oth))):
            outs.append(
                pltpu.make_async_copy(
                    qkv_scr.at[pl.ds(m * two, two), col],
                    out.at[pl.ds(m * two, two)],
                    out_sems.at[m, i],
                )
            )
            outs[-1].start()
        seg = jnp.zeros_like(position)
        for k in range(1, 4):
            bound = jnp.where(
                position < seq,
                info[k, first_row + 2 * m],
                info[k, first_row + 2 * m + 1] + seq,
            )
            seg += (position >= bound).astype(jnp.int32)
        member = ((seg == doc) & same_row).astype(jnp.float32)
        total = jnp.sum(member, -1, keepdims=True)
        pooled = jnp.dot(member.astype(jnp.bfloat16), encoded, preferred_element_type=jnp.float32)
        pooled = pooled * (1.0 / jnp.maximum(total, 1.0))
        square = jnp.mean(pooled * pooled, -1, keepdims=True)
        embedded = (pooled * lax.rsqrt(square + 1e-06)).astype(jnp.bfloat16)
        emb_scr[0, m * 16 : (m + 1) * 16, :] = embedded[:, :half]
        emb_scr[1, m * 16 : (m + 1) * 16, :] = embedded[:, half:]
    for i, out in enumerate((emb_own, emb_oth)):
        which = me if i == 0 else 1 - me
        outs.append(pltpu.make_async_copy(emb_scr.at[which], out, out_sems.at[rows // 2, i]))
        outs[-1].start()
    for copy in outs:
        copy.wait()


def layer(core, table, received, x_other, weights, gain_attn, gain_ffn):
    rows, body, _ = x_other.shape
    half = body * LANES // HD
    tokens = rows * HD
    model = 2 * half
    wu, wd = weights[4], weights[6]
    flops = 2 * tokens * model * (3 * model + model + 4 * wu.shape[1])
    any_spec = pl.BlockSpec(memory_space=pltpu.HBM)
    vmem = pl.BlockSpec(memory_space=pltpu.VMEM)
    return pl.pallas_call(
        layer_kernel,
        out_shape=(
            jax.ShapeDtypeStruct((tokens, half), jnp.bfloat16),
            jax.ShapeDtypeStruct((tokens, half), jnp.bfloat16),
            jax.ShapeDtypeStruct((rows * 8, half), jnp.bfloat16),
            jax.ShapeDtypeStruct((rows * 8, half), jnp.bfloat16),
        ),
        in_specs=[pl.BlockSpec(memory_space=pltpu.SMEM)]
        + [any_spec] * 11
        + [vmem] * 2,
        out_specs=(any_spec,) * 4,
        scratch_shapes=[
            pltpu.SMEM(table.shape, jnp.int32),
            pltpu.VMEM((rows, 2 * body, LANES), jnp.bfloat16),
            pltpu.VMEM((tokens, 3 * model), jnp.bfloat16),
            pltpu.VMEM((2, rows * 8, half), jnp.bfloat16),
            pltpu.VMEM((tokens, model), jnp.float32),
            pltpu.VMEM((6, model, half), jnp.bfloat16),
            pltpu.VMEM((2, half, model), jnp.bfloat16),
            pltpu.VMEM((2,) + wu.shape, jnp.bfloat16),
            pltpu.VMEM((2,) + wd.shape, jnp.bfloat16),
            pltpu.SemaphoreType.DMA((rows,)),
            pltpu.SemaphoreType.DMA,
            pltpu.SemaphoreType.DMA((6,)),
            pltpu.SemaphoreType.DMA((3, 2)),
            pltpu.SemaphoreType.DMA,
            pltpu.SemaphoreType.DMA((rows // 2 + 1, 2)),
        ],
        compiler_params=pltpu.CompilerParams(vmem_limit_bytes=60 * 1024 * 1024),
        cost_estimate=pl.CostEstimate(
            flops=flops, bytes_accessed=28 * 1024 * 1024, transcendentals=0
        ),
        name="layer",
    )(core, table, received, x_other, *weights, gain_attn, gain_ffn)


def shards(tokens, doc_ids, dest, owner, w_qkv, w_out, gain_attn, w_up, w_down, gain_ffn):
    devices = lax.axis_size("dp")
    row_count, seq, half = tokens.shape
    docs = owner.shape[1]
    mine = row_count // 2
    me = lax.axis_index("mp")

    qkv_own = jnp.moveaxis(w_qkv, 1, 0)
    weights = []
    for own in (qkv_own, w_out, w_up, w_down):
        weights += [own, lax.ppermute(own, "mp", SWAP)]

    received = lax.all_to_all(
        pack(dest, doc_ids, tokens, devices), "dp", split_axis=0, concat_axis=0, tiled=True
    )
    owners = owner.reshape(-1)
    position = jnp.arange(row_count * docs, dtype=jnp.int32)
    earlier = (owners[:, None] == owners[None, :]) & (position[None, :] < position[:, None])
    rank = jnp.sum(earlier.astype(jnp.int32), -1)
    target = jnp.pad(
        (owners * SLOTS + rank).reshape(2, mine, docs), ((0, 0), (0, 0), (0, 8 - docs)),
        constant_values=-1,
    ).reshape(2, mine * 8)
    out_slot = jnp.arange(devices * SLOTS, dtype=jnp.int32)[:, None]
    place_own = (lax.dynamic_index_in_dim(target, me, 0) == out_slot).astype(jnp.bfloat16)
    place_oth = (lax.dynamic_index_in_dim(target, 1 - me, 0) == out_slot).astype(jnp.bfloat16)
    core = me.astype(jnp.int32)[None]
    core, place_own, place_oth = lax.optimization_barrier((core, place_own, place_oth))
    x_send, info = unpack(core, received, mine)
    x_other = lax.ppermute(x_send, "mp", SWAP)
    enc_own, enc_oth, emb_own, emb_oth = layer(
        core, info, received, x_other, weights, gain_attn[None], gain_ffn[None]
    )
    emb_recv = lax.ppermute(emb_oth, "mp", SWAP)
    own_part = jnp.dot(place_own, emb_own, preferred_element_type=jnp.float32)
    own_part, emb_recv = lax.optimization_barrier((own_part, emb_recv))
    enc_oth, emb_recv = lax.optimization_barrier((enc_oth, emb_recv))
    enc_recv = lax.ppermute(enc_oth, "mp", SWAP)

    sending = jnp.dot(place_oth, emb_recv, preferred_element_type=jnp.float32)
    sending = (sending + own_part).astype(jnp.bfloat16)
    got = lax.all_to_all(
        sending.reshape(devices, SLOTS, half), "dp", split_axis=0, concat_axis=0, tiled=True
    )
    enc_own = enc_own.reshape(mine, seq, half)
    enc_recv = enc_recv.reshape(mine, seq, half)
    first = me == 0
    encoded = jnp.concatenate(
        [jnp.where(first, enc_own, enc_recv), jnp.where(first, enc_recv, enc_own)], 0
    )
    got, encoded = lax.optimization_barrier((got, encoded))
    index_part = got[:, : SLOTS - 1].astype(jnp.float32).reshape(1, devices * (SLOTS - 1), half)
    return (encoded, index_part)


def solution(mesh):
    return jax.shard_map(
        shards,
        mesh=mesh,
        in_specs=(
            P("dp", None, "mp"),
            P("dp", None),
            P("dp"),
            P("dp", None),
            P(None, None, "mp"),
            P("mp", None),
            P(),
            P(None, "mp"),
            P("mp", None),
            P(),
        ),
        out_specs=(P("dp", None, "mp"), P("dp", None, "mp")),
        check_vma=False,
    )
```

```python
import math

import jax
import jax.numpy as jnp
from jax import lax
from jax.experimental import pallas as pl
from jax.experimental.pallas import tpu as pltpu
from jax.sharding import PartitionSpec as P

HD = 64
TILE = 1024
PART = 896
SLOTS = 4
SWAP = [(0, 1), (1, 0)]
LANES = 128
FACTS = 8


def gelu(x):
    half = 0.5 * x
    return half + half * lax.erf(x * math.sqrt(0.5))


def norm(values, gain):
    mean = jnp.mean(values, -1, keepdims=True)
    centred = values - mean
    var = jnp.mean(centred * centred, -1, keepdims=True)
    return centred * lax.rsqrt(var + 1e-05) * gain


def pack_kernel(dest, doc_ids, tokens, out, raw, staged, empty, in_sems, out_sems, empty_sem):
    rows, seq, width = tokens.shape
    body = seq * width // LANES
    loads = [pltpu.make_async_copy(tokens.at[r], raw.at[r], in_sems.at[r]) for r in range(rows)]
    for copy in loads:
        copy.start()
    empty[...] = jnp.zeros_like(empty)
    clear = pltpu.make_async_copy(empty, out.at[:, pl.ds(body, FACTS)], empty_sem)
    clear.start()
    lane = lax.broadcasted_iota(jnp.int32, (rows, LANES), 1)
    facts = jnp.where(lane == 0, lax.broadcasted_iota(jnp.int32, (rows, LANES), 0) + 1, 0)
    ids = doc_ids[...]
    for k in range(1, 4):
        bound = jnp.sum((ids < k).astype(jnp.float32), -1, keepdims=True).astype(jnp.int32)
        facts = jnp.where(lane == k, bound, facts)
    facts = facts.astype(jnp.float32)
    stores = []
    for r in range(rows):
        staged[r, body:, :] = jnp.broadcast_to(facts[r : r + 1, :], (FACTS, LANES)).astype(
            jnp.bfloat16
        )
        loads[r].wait()
        for c in range(width // LANES):
            staged[r, c * seq : (c + 1) * seq, :] = raw[r, :, c * LANES : (c + 1) * LANES]
        if r == 0:
            clear.wait()
        stores.append(
            pltpu.make_async_copy(
                staged.at[r], out.at[lax.div(dest[r], rows)], out_sems.at[r]
            )
        )
        stores[-1].start()
    for copy in stores:
        copy.wait()


def pack(dest, doc_ids, tokens, slots):
    rows, seq, width = tokens.shape
    body = seq * width // LANES
    return pl.pallas_call(
        pack_kernel,
        out_shape=jax.ShapeDtypeStruct((slots, body + FACTS, LANES), tokens.dtype),
        in_specs=[
            pl.BlockSpec(memory_space=pltpu.SMEM),
            pl.BlockSpec(memory_space=pltpu.VMEM),
            pl.BlockSpec(memory_space=pltpu.HBM),
        ],
        out_specs=pl.BlockSpec(memory_space=pltpu.HBM),
        scratch_shapes=[
            pltpu.VMEM((rows, seq, width), tokens.dtype),
            pltpu.VMEM((rows, body + FACTS, LANES), tokens.dtype),
            pltpu.VMEM((slots, FACTS, LANES), tokens.dtype),
            pltpu.SemaphoreType.DMA((rows,)),
            pltpu.SemaphoreType.DMA((rows,)),
            pltpu.SemaphoreType.DMA,
        ],
        compiler_params=pltpu.CompilerParams(vmem_limit_bytes=62 * 1024 * 1024),
        name="pack_rows",
    )(dest, doc_ids, tokens)


def unpack_kernel(
    core, received, out, info, facts, table, scalars, staged, fact_sem, info_sem, sems, out_sems
):
    rows, body, _ = out.shape
    slots = received.shape[0]
    load = pltpu.make_async_copy(received.at[:, pl.ds(body, FACTS)], facts, fact_sem)
    load.start()
    load.wait()
    values = facts[...].astype(jnp.float32)
    shape = (slots, FACTS, LANES)
    here = values[:, :, :1] == (lax.broadcasted_iota(jnp.int32, shape, 2) + 1).astype(jnp.float32)
    source = lax.broadcasted_iota(jnp.int32, shape, 0).astype(jnp.float32)
    result = jnp.sum(jnp.where(here, source, 0.0), 0)
    table[0] = result.astype(jnp.int32)
    keep = pltpu.make_async_copy(table.at[0], scalars, info_sem.at[0])
    keep.start()
    keep.wait()
    first = (1 - core[0]) * rows
    copies = [
        pltpu.make_async_copy(
            received.at[scalars[0, first + r], pl.ds(0, body)], staged.at[r], sems.at[r]
        )
        for r in range(rows)
    ]
    for copy in copies:
        copy.start()
    kind = lax.broadcasted_iota(jnp.int32, (FACTS, LANES), 0)
    for k in range(1, 4):
        bound = jnp.sum(jnp.where(here, values[:, :, k : k + 1], 0.0), 0)
        result = jnp.where(kind == k, bound, result)
    table[1] = result.astype(jnp.int32)
    keep = pltpu.make_async_copy(table.at[1], info, info_sem.at[1])
    keep.start()
    stores = []
    for r in range(rows):
        copies[r].wait()
        stores.append(pltpu.make_async_copy(staged.at[r], out.at[r], out_sems.at[r]))
        stores[-1].start()
    for copy in stores:
        copy.wait()
    keep.wait()


def unpack(core, received, rows):
    slots = received.shape[0]
    body = received.shape[1] - FACTS
    hbm = pl.BlockSpec(memory_space=pltpu.HBM)
    return pl.pallas_call(
        unpack_kernel,
        out_shape=(
            jax.ShapeDtypeStruct((rows, body, LANES), received.dtype),
            jax.ShapeDtypeStruct((FACTS, LANES), jnp.int32),
        ),
        in_specs=[pl.BlockSpec(memory_space=pltpu.SMEM), hbm],
        out_specs=(hbm, hbm),
        scratch_shapes=[
            pltpu.VMEM((slots, FACTS, LANES), received.dtype),
            pltpu.VMEM((2, FACTS, LANES), jnp.int32),
            pltpu.SMEM((FACTS, LANES), jnp.int32),
            pltpu.VMEM((rows, body, LANES), received.dtype),
            pltpu.SemaphoreType.DMA,
            pltpu.SemaphoreType.DMA((2,)),
            pltpu.SemaphoreType.DMA((rows,)),
            pltpu.SemaphoreType.DMA((rows,)),
        ],
        compiler_params=pltpu.CompilerParams(vmem_limit_bytes=62 * 1024 * 1024),
        name="unpack_rows",
    )(core, received)


def layer_kernel(
    core,
    table,
    received,
    x_other,
    wq_own,
    wq_oth,
    wo_own,
    wo_oth,
    wu_own,
    wu_oth,
    wd_own,
    wd_oth,
    gain_attn,
    gain_ffn,
    enc_own,
    enc_oth,
    emb_own,
    emb_oth,
    info,
    x_scr,
    qkv_scr,
    emb_scr,
    acc_scr,
    wq,
    wo,
    wu,
    wd,
    row_sems,
    x_sem,
    q_sems,
    w_sems,
    info_sem,
    out_sems,
):
    rows = x_scr.shape[0]
    seq = HD
    tokens, half = enc_own.shape
    model = 2 * half
    chunks = model // LANES
    body = half * seq // LANES
    me = core[0]
    first_row = me * rows
    facts = pltpu.make_async_copy(table, info, info_sem)
    facts.start()
    own_at = pl.ds(pl.multiple_of(me * body, body), body)
    oth_at = pl.ds(pl.multiple_of((1 - me) * body, body), body)
    x_copies = [pltpu.make_async_copy(x_other, x_scr.at[:, oth_at], x_sem)]
    q_copies = [
        pltpu.make_async_copy(src.at[i], wq.at[3 * h + i], q_sems.at[3 * h + i])
        for h, src in enumerate((wq_own, wq_oth))
        for i in range(3)
    ]
    for copy in x_copies + q_copies[:2]:
        copy.start()
    facts.wait()
    row_copies = [
        pltpu.make_async_copy(
            received.at[info[0, first_row + r], pl.ds(0, body)], x_scr.at[r, own_at], row_sems.at[r]
        )
        for r in range(rows)
    ]
    w_pairs = ((wo_own, wo_oth, wo), (wu_own, wu_oth, wu), (wd_own, wd_oth, wd))
    w_copies = [
        pltpu.make_async_copy(pair[h], pair[2].at[h], w_sems.at[i, h])
        for i, pair in enumerate(w_pairs)
        for h in range(2)
    ]
    for copy in row_copies:
        copy.start()
    for copy in x_copies + row_copies:
        copy.wait()
    for copy in q_copies[2:]:
        copy.start()

    def inputs(first, count):
        pieces = [
            x_scr[pl.ds(first, count), c * seq : (c + 1) * seq, :].reshape(count * seq, LANES)
            for c in range(chunks)
        ]
        return jnp.concatenate(pieces, 1)

    for n in range(6):
        q_copies[n].wait()
        w_copies[n].start()
        qkv_scr[:, n * half : (n + 1) * half] = jnp.dot(
            inputs(0, rows), wq[n], preferred_element_type=jnp.float32
        ).astype(jnp.bfloat16)

    pair = 2 * HD
    block = (lax.broadcasted_iota(jnp.int32, (pair, pair), 0) < HD) == (
        lax.broadcasted_iota(jnp.int32, (pair, pair), 1) < HD
    )
    lane_low = lax.broadcasted_iota(jnp.int32, (seq, pair), 1) < HD
    key_pos = lax.broadcasted_iota(jnp.int32, (seq, pair), 0)
    query_pos = lax.broadcasted_iota(jnp.int32, (seq, pair), 1) % HD
    per_half = half // pair

    def attend(r, carry):
        here = pl.ds(pl.multiple_of(r * seq, seq), seq)
        bounds = [info[k, first_row + r] for k in range(1, 4)]
        key_seg = sum([(key_pos >= b).astype(jnp.int32) for b in bounds])
        query_seg = sum([(query_pos >= b).astype(jnp.int32) for b in bounds])
        same = key_seg == query_seg
        scores = []
        for p in range(2 * per_half):
            at = (p // per_half) * 3 * half + (p % per_half) * pair
            q = qkv_scr[here, at : at + pair]
            k = qkv_scr[here, at + half : at + half + pair]
            spread = jnp.where(block, jnp.concatenate([q, q], 0), jnp.zeros((), q.dtype))
            scores.append(
                lax.dot_general(
                    k, spread, (((1,), (1,)), ((), ())), preferred_element_type=jnp.float32
                )
            )
        probs = []
        for score in scores:
            score = jnp.where(same, score * (1.0 / math.sqrt(HD)), jnp.float32(-1e30))
            weight = jnp.exp(score - jnp.max(score, 0, keepdims=True))
            probs.append(
                (weight * (1.0 / jnp.sum(weight, 0, keepdims=True))).astype(jnp.bfloat16)
            )
        mixed = []
        for p in range(2 * per_half):
            at = (p // per_half) * 3 * half + 2 * half + (p % per_half) * pair
            mixed.append(
                lax.dot_general(
                    probs[p],
                    qkv_scr[here, at : at + pair],
                    (((0,), (0,)), ((), ())),
                    preferred_element_type=jnp.float32,
                )
            )
        for p in range(2 * per_half):
            at = (p // per_half) * 3 * half + (p % per_half) * pair
            qkv_scr[here, at : at + pair] = jnp.where(
                lane_low, mixed[p][:seq], mixed[p][seq:]
            ).astype(jnp.bfloat16)
        return carry

    lax.fori_loop(0, rows, attend, 0)

    for copy in w_copies[:2]:
        copy.wait()
    count = 2
    for m in range(rows // count):
        at = slice(m * count * seq, (m + 1) * count * seq)
        mixed = jnp.dot(qkv_scr[at, :half], wo[0], preferred_element_type=jnp.float32)
        mixed += jnp.dot(
            qkv_scr[at, 3 * half : 4 * half], wo[1], preferred_element_type=jnp.float32
        )
        mixed = mixed + inputs(m * count, count).astype(jnp.float32)
        normed = norm(mixed, gain_attn[...]).astype(jnp.bfloat16)
        qkv_scr[at, half : 3 * half] = normed
        acc_scr[at, :] = normed.astype(jnp.float32)

    for copy in w_copies[2:]:
        copy.wait()
    tiles = wu.shape[2] // TILE
    parts = tokens // PART

    def feed(t, carry):
        h = t // (tiles * parts)
        at = pl.ds(pl.multiple_of((t % tiles) * TILE, TILE), TILE)
        here = pl.ds(pl.multiple_of((t // tiles) % parts * PART, PART), PART)
        normed = qkv_scr[here, half : 3 * half]
        up = jnp.dot(normed, wu[h, :, at], preferred_element_type=jnp.float32)
        acc_scr[here, :] += jnp.dot(
            gelu(up).astype(jnp.bfloat16), wd[h, at, :], preferred_element_type=jnp.float32
        )
        return carry

    lax.fori_loop(0, 2 * tiles * parts, feed, 0)

    two = 2 * seq
    doc = lax.broadcasted_iota(jnp.int32, (16, two), 0)
    position = lax.broadcasted_iota(jnp.int32, (16, two), 1)
    same_row = (doc < 8) == (position < seq)
    doc = doc % 8
    quarter = half // 2
    own_col = pl.ds(pl.multiple_of(me * half, half), half)
    oth_col = pl.ds(pl.multiple_of((1 - me) * half, half), half)
    outs = []
    for m in range(rows // 2):
        at = slice(m * two, (m + 1) * two)
        encoded = norm(acc_scr[at, :], gain_ffn[...]).astype(jnp.bfloat16)
        qkv_scr[at, : 2 * half] = encoded
        for i, (col, out) in enumerate(((own_col, enc_own), (oth_col, enc_oth))):
            outs.append(
                pltpu.make_async_copy(
                    qkv_scr.at[pl.ds(m * two, two), col],
                    out.at[pl.ds(m * two, two)],
                    out_sems.at[m, i],
                )
            )
            outs[-1].start()
        seg = jnp.zeros_like(position)
        for k in range(1, 4):
            bound = jnp.where(
                position < seq,
                info[k, first_row + 2 * m],
                info[k, first_row + 2 * m + 1] + seq,
            )
            seg += (position >= bound).astype(jnp.int32)
        member = ((seg == doc) & same_row).astype(jnp.float32)
        total = jnp.sum(member, -1, keepdims=True)
        pooled = jnp.dot(member.astype(jnp.bfloat16), encoded, preferred_element_type=jnp.float32)
        pooled = pooled * (1.0 / jnp.maximum(total, 1.0))
        square = jnp.mean(pooled * pooled, -1, keepdims=True)
        embedded = (pooled * lax.rsqrt(square + 1e-06)).astype(jnp.bfloat16)
        for i in range(2 * model // half):
            at = slice((i % 2 * rows + 2 * m) * 8, (i % 2 * rows + 2 * m + 2) * 8)
            emb_scr[i // 2, at, :] = embedded[:, i * quarter : (i + 1) * quarter]
    for i, out in enumerate((emb_own, emb_oth)):
        which = me if i == 0 else 1 - me
        outs.append(pltpu.make_async_copy(emb_scr.at[which], out, out_sems.at[rows // 2, i]))
        outs[-1].start()
    for copy in outs:
        copy.wait()


def layer(core, table, received, x_other, weights, gain_attn, gain_ffn):
    rows, body, _ = x_other.shape
    half = body * LANES // HD
    tokens = rows * HD
    model = 2 * half
    wu, wd = weights[4], weights[6]
    flops = 2 * tokens * model * (3 * model + model + 4 * wu.shape[1])
    any_spec = pl.BlockSpec(memory_space=pltpu.HBM)
    vmem = pl.BlockSpec(memory_space=pltpu.VMEM)
    return pl.pallas_call(
        layer_kernel,
        out_shape=(
            jax.ShapeDtypeStruct((tokens, half), jnp.bfloat16),
            jax.ShapeDtypeStruct((tokens, half), jnp.bfloat16),
            jax.ShapeDtypeStruct((2 * rows * 8, half // 2), jnp.bfloat16),
            jax.ShapeDtypeStruct((2 * rows * 8, half // 2), jnp.bfloat16),
        ),
        in_specs=[pl.BlockSpec(memory_space=pltpu.SMEM)]
        + [any_spec] * 11
        + [vmem] * 2,
        out_specs=(any_spec,) * 4,
        scratch_shapes=[
            pltpu.SMEM(table.shape, jnp.int32),
            pltpu.VMEM((rows, 2 * body, LANES), jnp.bfloat16),
            pltpu.VMEM((tokens, 3 * model), jnp.bfloat16),
            pltpu.VMEM((2, 2 * rows * 8, half // 2), jnp.bfloat16),
            pltpu.VMEM((tokens, model), jnp.float32),
            pltpu.VMEM((6, model, half), jnp.bfloat16),
            pltpu.VMEM((2, half, model), jnp.bfloat16),
            pltpu.VMEM((2,) + wu.shape, jnp.bfloat16),
            pltpu.VMEM((2,) + wd.shape, jnp.bfloat16),
            pltpu.SemaphoreType.DMA((rows,)),
            pltpu.SemaphoreType.DMA,
            pltpu.SemaphoreType.DMA((6,)),
            pltpu.SemaphoreType.DMA((3, 2)),
            pltpu.SemaphoreType.DMA,
            pltpu.SemaphoreType.DMA((rows // 2 + 1, 2)),
        ],
        compiler_params=pltpu.CompilerParams(vmem_limit_bytes=62 * 1024 * 1024),
        cost_estimate=pl.CostEstimate(
            flops=flops, bytes_accessed=28 * 1024 * 1024, transcendentals=0
        ),
        name="layer",
    )(core, table, received, x_other, *weights, gain_attn, gain_ffn)


def shards(tokens, doc_ids, dest, owner, w_qkv, w_out, gain_attn, w_up, w_down, gain_ffn):
    devices = lax.axis_size("dp")
    row_count, seq, half = tokens.shape
    docs = owner.shape[1]
    mine = row_count // 2
    me = lax.axis_index("mp")

    qkv_own = jnp.moveaxis(w_qkv, 1, 0)
    weights = []
    for own in (qkv_own, w_out, w_up, w_down):
        weights += [own, lax.ppermute(own, "mp", SWAP)]

    received = lax.all_to_all(
        pack(dest, doc_ids, tokens, devices), "dp", split_axis=0, concat_axis=0, tiled=True
    )
    owners = owner.reshape(-1)
    position = jnp.arange(row_count * docs, dtype=jnp.int32)
    earlier = (owners[:, None] == owners[None, :]) & (position[None, :] < position[:, None])
    rank = jnp.sum(earlier.astype(jnp.int32), -1)
    target = (owners * 2 * SLOTS + rank).reshape(2, 1, mine, docs)
    target = target + jnp.array([0, SLOTS], jnp.int32).reshape(1, 2, 1, 1)
    target = jnp.pad(
        target, ((0, 0), (0, 0), (0, 0), (0, 8 - docs)), constant_values=-1
    ).reshape(2, 2 * mine * 8)
    out_slot = jnp.arange(devices * 2 * SLOTS, dtype=jnp.int32)[:, None]
    place_own = (lax.dynamic_index_in_dim(target, me, 0) == out_slot).astype(jnp.bfloat16)
    place_oth = (lax.dynamic_index_in_dim(target, 1 - me, 0) == out_slot).astype(jnp.bfloat16)
    core = me.astype(jnp.int32)[None]
    core, place_own, place_oth = lax.optimization_barrier((core, place_own, place_oth))
    x_send, info = unpack(core, received, mine)
    x_other = lax.ppermute(x_send, "mp", SWAP)
    enc_own, enc_oth, emb_own, emb_oth = layer(
        core, info, received, x_other, weights, gain_attn[None], gain_ffn[None]
    )
    emb_recv = lax.ppermute(emb_oth, "mp", SWAP)
    own_part = jnp.dot(place_own, emb_own, preferred_element_type=jnp.float32)
    own_part, emb_recv = lax.optimization_barrier((own_part, emb_recv))
    enc_oth, emb_recv = lax.optimization_barrier((enc_oth, emb_recv))
    enc_recv = lax.ppermute(enc_oth, "mp", SWAP)

    sending = jnp.dot(place_oth, emb_recv, preferred_element_type=jnp.float32)
    sending = (sending + own_part).astype(jnp.bfloat16)
    got = lax.all_to_all(
        sending.reshape(devices, 2 * SLOTS, half // 2), "dp", split_axis=0, concat_axis=0, tiled=True
    )
    enc_own = enc_own.reshape(mine, seq, half)
    enc_recv = enc_recv.reshape(mine, seq, half)
    first = me == 0
    encoded = jnp.concatenate(
        [jnp.where(first, enc_own, enc_recv), jnp.where(first, enc_recv, enc_own)], 0
    )
    got, encoded = lax.optimization_barrier((got, encoded))
    got = jnp.concatenate([got[:, : SLOTS - 1], got[:, SLOTS:-1]], -1)
    index_part = got.astype(jnp.float32).reshape(1, devices * (SLOTS - 1), half)
    return (encoded, index_part)


def solution(mesh):
    return jax.shard_map(
        shards,
        mesh=mesh,
        in_specs=(
            P("dp", None, "mp"),
            P("dp", None),
            P("dp"),
            P("dp", None),
            P(None, None, "mp"),
            P("mp", None),
            P(),
            P(None, "mp"),
            P("mp", None),
            P(),
        ),
        out_specs=(P("dp", None, "mp"), P("dp", None, "mp")),
        check_vma=False,
    )
```

```python
import math

import jax
import jax.numpy as jnp
from jax import lax
from jax.experimental import pallas as pl
from jax.experimental.pallas import tpu as pltpu
from jax.sharding import PartitionSpec as P

HD = 64
TILE = 1024
PART = 896
SLOTS = 4
SWAP = [(0, 1), (1, 0)]
LANES = 128
FACTS = 16


def gelu(x):
    half = 0.5 * x
    return half + half * lax.erf(x * math.sqrt(0.5))


def norm(values, gain):
    mean = jnp.mean(values, -1, keepdims=True)
    centred = values - mean
    var = jnp.mean(centred * centred, -1, keepdims=True)
    return centred * lax.rsqrt(var + 1e-05) * gain


def pack_kernel(dest, doc_ids, tokens, out, raw, staged, empty, in_sems, out_sems, empty_sem):
    rows, seq, width = tokens.shape
    body = seq * width // LANES
    loads = [pltpu.make_async_copy(tokens.at[r], raw.at[r], in_sems.at[r]) for r in range(rows)]
    for copy in loads:
        copy.start()
    empty[...] = jnp.zeros_like(empty)
    clear = pltpu.make_async_copy(empty, out.at[:, pl.ds(body, FACTS)], empty_sem)
    clear.start()
    lane = lax.broadcasted_iota(jnp.int32, (rows, LANES), 1)
    facts = jnp.where(lane == 0, lax.broadcasted_iota(jnp.int32, (rows, LANES), 0) + 1, 0)
    ids = doc_ids[...]
    for k in range(1, 4):
        bound = jnp.sum((ids < k).astype(jnp.float32), -1, keepdims=True).astype(jnp.int32)
        facts = jnp.where(lane == k, bound, facts)
    facts = facts.astype(jnp.float32)
    stores = []
    for r in range(rows):
        staged[r, body:, :] = jnp.broadcast_to(facts[r : r + 1, :], (FACTS, LANES)).astype(
            jnp.bfloat16
        )
        loads[r].wait()
        for c in range(width // LANES):
            staged[r, c * seq : (c + 1) * seq, :] = raw[r, :, c * LANES : (c + 1) * LANES]
        if r == 0:
            clear.wait()
        stores.append(
            pltpu.make_async_copy(
                staged.at[r], out.at[lax.div(dest[r], rows)], out_sems.at[r]
            )
        )
        stores[-1].start()
    for copy in stores:
        copy.wait()


def pack(dest, doc_ids, tokens, slots):
    rows, seq, width = tokens.shape
    body = seq * width // LANES
    return pl.pallas_call(
        pack_kernel,
        out_shape=jax.ShapeDtypeStruct((slots, body + FACTS, LANES), tokens.dtype),
        in_specs=[
            pl.BlockSpec(memory_space=pltpu.SMEM),
            pl.BlockSpec(memory_space=pltpu.VMEM),
            pl.BlockSpec(memory_space=pltpu.HBM),
        ],
        out_specs=pl.BlockSpec(memory_space=pltpu.HBM),
        scratch_shapes=[
            pltpu.VMEM((rows, seq, width), tokens.dtype),
            pltpu.VMEM((rows, body + FACTS, LANES), tokens.dtype),
            pltpu.VMEM((slots, FACTS, LANES), tokens.dtype),
            pltpu.SemaphoreType.DMA((rows,)),
            pltpu.SemaphoreType.DMA((rows,)),
            pltpu.SemaphoreType.DMA,
        ],
        compiler_params=pltpu.CompilerParams(vmem_limit_bytes=62 * 1024 * 1024),
        name="pack_rows",
    )(dest, doc_ids, tokens)


def unpack_kernel(
    core, received, out, info, facts, table, scalars, staged, fact_sem, info_sem, sems, out_sems
):
    rows, body, _ = out.shape
    slots = received.shape[0]
    load = pltpu.make_async_copy(received.at[:, pl.ds(body, FACTS)], facts, fact_sem)
    load.start()
    load.wait()
    values = facts[...].astype(jnp.float32)
    shape = (slots, FACTS, LANES)
    here = values[:, :, :1] == (lax.broadcasted_iota(jnp.int32, shape, 2) + 1).astype(jnp.float32)
    source = lax.broadcasted_iota(jnp.int32, shape, 0).astype(jnp.float32)
    result = jnp.sum(jnp.where(here, source, 0.0), 0)
    table[0] = result.astype(jnp.int32)
    keep = pltpu.make_async_copy(table.at[0], scalars, info_sem.at[0])
    keep.start()
    keep.wait()
    first = (1 - core[0]) * rows
    copies = [
        pltpu.make_async_copy(
            received.at[scalars[0, first + r], pl.ds(0, body)], staged.at[r], sems.at[r]
        )
        for r in range(rows)
    ]
    for copy in copies:
        copy.start()
    kind = lax.broadcasted_iota(jnp.int32, (FACTS, LANES), 0)
    for k in range(1, 4):
        bound = jnp.sum(jnp.where(here, values[:, :, k : k + 1], 0.0), 0)
        result = jnp.where(kind == k, bound, result)
    table[1] = result.astype(jnp.int32)
    keep = pltpu.make_async_copy(table.at[1], info, info_sem.at[1])
    keep.start()
    stores = []
    for r in range(rows):
        copies[r].wait()
        stores.append(pltpu.make_async_copy(staged.at[r], out.at[r], out_sems.at[r]))
        stores[-1].start()
    for copy in stores:
        copy.wait()
    keep.wait()


def unpack(core, received, rows):
    slots = received.shape[0]
    body = received.shape[1] - FACTS
    hbm = pl.BlockSpec(memory_space=pltpu.HBM)
    return pl.pallas_call(
        unpack_kernel,
        out_shape=(
            jax.ShapeDtypeStruct((rows, body, LANES), received.dtype),
            jax.ShapeDtypeStruct((FACTS, LANES), jnp.int32),
        ),
        in_specs=[pl.BlockSpec(memory_space=pltpu.SMEM), hbm],
        out_specs=(hbm, hbm),
        scratch_shapes=[
            pltpu.VMEM((slots, FACTS, LANES), received.dtype),
            pltpu.VMEM((2, FACTS, LANES), jnp.int32),
            pltpu.SMEM((FACTS, LANES), jnp.int32),
            pltpu.VMEM((rows, body, LANES), received.dtype),
            pltpu.SemaphoreType.DMA,
            pltpu.SemaphoreType.DMA((2,)),
            pltpu.SemaphoreType.DMA((rows,)),
            pltpu.SemaphoreType.DMA((rows,)),
        ],
        compiler_params=pltpu.CompilerParams(vmem_limit_bytes=62 * 1024 * 1024),
        name="unpack_rows",
    )(core, received)


def layer_kernel(
    core,
    table,
    received,
    x_other,
    wq_own,
    wq_oth,
    wo_own,
    wo_oth,
    wu_own,
    wu_oth,
    wd_own,
    wd_oth,
    gain_attn,
    gain_ffn,
    enc_own,
    enc_oth,
    emb_own,
    emb_oth,
    info,
    x_scr,
    qkv_scr,
    emb_scr,
    acc_scr,
    wq,
    wo,
    wu,
    wd,
    row_sems,
    x_sem,
    q_sems,
    w_sems,
    info_sem,
    out_sems,
):
    rows = x_scr.shape[0]
    seq = HD
    tokens, half = enc_own.shape
    model = 2 * half
    chunks = model // LANES
    body = half * seq // LANES
    me = core[0]
    first_row = me * rows
    facts = pltpu.make_async_copy(table, info, info_sem)
    facts.start()
    own_at = pl.ds(pl.multiple_of(me * body, body), body)
    oth_at = pl.ds(pl.multiple_of((1 - me) * body, body), body)
    x_copies = [pltpu.make_async_copy(x_other, x_scr.at[:, oth_at], x_sem)]
    q_copies = [
        pltpu.make_async_copy(src.at[i], wq.at[3 * h + i], q_sems.at[3 * h + i])
        for h, src in enumerate((wq_own, wq_oth))
        for i in range(3)
    ]
    for copy in x_copies + q_copies[:2]:
        copy.start()
    facts.wait()
    row_copies = [
        pltpu.make_async_copy(
            received.at[info[0, first_row + r], pl.ds(0, body)], x_scr.at[r, own_at], row_sems.at[r]
        )
        for r in range(rows)
    ]
    w_pairs = ((wo_own, wo_oth, wo), (wu_own, wu_oth, wu), (wd_own, wd_oth, wd))
    w_copies = [
        pltpu.make_async_copy(pair[h], pair[2].at[h], w_sems.at[i, h])
        for i, pair in enumerate(w_pairs)
        for h in range(2)
    ]
    for copy in row_copies:
        copy.start()
    for copy in x_copies + row_copies:
        copy.wait()
    for copy in q_copies[2:]:
        copy.start()

    def inputs(first, count):
        pieces = [
            x_scr[pl.ds(first, count), c * seq : (c + 1) * seq, :].reshape(count * seq, LANES)
            for c in range(chunks)
        ]
        return jnp.concatenate(pieces, 1)

    for n in range(6):
        q_copies[n].wait()
        w_copies[n].start()
        qkv_scr[:, n * half : (n + 1) * half] = jnp.dot(
            inputs(0, rows), wq[n], preferred_element_type=jnp.float32
        ).astype(jnp.bfloat16)

    pair = 2 * HD
    block = (lax.broadcasted_iota(jnp.int32, (pair, pair), 0) < HD) == (
        lax.broadcasted_iota(jnp.int32, (pair, pair), 1) < HD
    )
    lane_low = lax.broadcasted_iota(jnp.int32, (seq, pair), 1) < HD
    key_pos = lax.broadcasted_iota(jnp.int32, (seq, pair), 0)
    query_pos = lax.broadcasted_iota(jnp.int32, (seq, pair), 1) % HD
    per_half = half // pair

    def attend(r, carry):
        here = pl.ds(pl.multiple_of(r * seq, seq), seq)
        bounds = [info[k, first_row + r] for k in range(1, 4)]
        key_seg = sum([(key_pos >= b).astype(jnp.int32) for b in bounds])
        query_seg = sum([(query_pos >= b).astype(jnp.int32) for b in bounds])
        same = key_seg == query_seg
        scores = []
        for p in range(2 * per_half):
            at = (p // per_half) * 3 * half + (p % per_half) * pair
            q = qkv_scr[here, at : at + pair]
            k = qkv_scr[here, at + half : at + half + pair]
            spread = jnp.where(block, jnp.concatenate([q, q], 0), jnp.zeros((), q.dtype))
            scores.append(
                lax.dot_general(
                    k, spread, (((1,), (1,)), ((), ())), preferred_element_type=jnp.float32
                )
            )
        probs = []
        for score in scores:
            score = jnp.where(same, score * (1.0 / math.sqrt(HD)), jnp.float32(-1e30))
            weight = jnp.exp(score - jnp.max(score, 0, keepdims=True))
            probs.append(
                (weight * (1.0 / jnp.sum(weight, 0, keepdims=True))).astype(jnp.bfloat16)
            )
        mixed = []
        for p in range(2 * per_half):
            at = (p // per_half) * 3 * half + 2 * half + (p % per_half) * pair
            mixed.append(
                lax.dot_general(
                    probs[p],
                    qkv_scr[here, at : at + pair],
                    (((0,), (0,)), ((), ())),
                    preferred_element_type=jnp.float32,
                )
            )
        for p in range(2 * per_half):
            at = (p // per_half) * 3 * half + (p % per_half) * pair
            qkv_scr[here, at : at + pair] = jnp.where(
                lane_low, mixed[p][:seq], mixed[p][seq:]
            ).astype(jnp.bfloat16)
        return carry

    lax.fori_loop(0, rows, attend, 0)

    for copy in w_copies[:2]:
        copy.wait()
    count = 2
    for m in range(rows // count):
        at = slice(m * count * seq, (m + 1) * count * seq)
        mixed = jnp.dot(qkv_scr[at, :half], wo[0], preferred_element_type=jnp.float32)
        mixed += jnp.dot(
            qkv_scr[at, 3 * half : 4 * half], wo[1], preferred_element_type=jnp.float32
        )
        mixed = mixed + inputs(m * count, count).astype(jnp.float32)
        normed = norm(mixed, gain_attn[...]).astype(jnp.bfloat16)
        qkv_scr[at, half : 3 * half] = normed
        acc_scr[at, :] = normed.astype(jnp.float32)

    for copy in w_copies[2:]:
        copy.wait()
    tiles = wu.shape[2] // TILE
    parts = tokens // PART

    def feed(t, carry):
        h = t // (tiles * parts)
        at = pl.ds(pl.multiple_of((t % tiles) * TILE, TILE), TILE)
        here = pl.ds(pl.multiple_of((t // tiles) % parts * PART, PART), PART)
        normed = qkv_scr[here, half : 3 * half]
        up = jnp.dot(normed, wu[h, :, at], preferred_element_type=jnp.float32)
        acc_scr[here, :] += jnp.dot(
            gelu(up).astype(jnp.bfloat16), wd[h, at, :], preferred_element_type=jnp.float32
        )
        return carry

    lax.fori_loop(0, 2 * tiles * parts, feed, 0)

    two = 2 * seq
    doc = lax.broadcasted_iota(jnp.int32, (16, two), 0)
    position = lax.broadcasted_iota(jnp.int32, (16, two), 1)
    same_row = (doc < 8) == (position < seq)
    doc = doc % 8
    quarter = half // 2
    own_col = pl.ds(pl.multiple_of(me * half, half), half)
    oth_col = pl.ds(pl.multiple_of((1 - me) * half, half), half)
    outs = []
    for m in range(rows // 2):
        at = slice(m * two, (m + 1) * two)
        encoded = norm(acc_scr[at, :], gain_ffn[...]).astype(jnp.bfloat16)
        qkv_scr[at, : 2 * half] = encoded
        for i, (col, out) in enumerate(((own_col, enc_own), (oth_col, enc_oth))):
            outs.append(
                pltpu.make_async_copy(
                    qkv_scr.at[pl.ds(m * two, two), col],
                    out.at[pl.ds(m * two, two)],
                    out_sems.at[m, i],
                )
            )
            outs[-1].start()
        seg = jnp.zeros_like(position)
        for k in range(1, 4):
            bound = jnp.where(
                position < seq,
                info[k, first_row + 2 * m],
                info[k, first_row + 2 * m + 1] + seq,
            )
            seg += (position >= bound).astype(jnp.int32)
        member = ((seg == doc) & same_row).astype(jnp.float32)
        total = jnp.sum(member, -1, keepdims=True)
        pooled = jnp.dot(member.astype(jnp.bfloat16), encoded, preferred_element_type=jnp.float32)
        pooled = pooled * (1.0 / jnp.maximum(total, 1.0))
        square = jnp.mean(pooled * pooled, -1, keepdims=True)
        embedded = (pooled * lax.rsqrt(square + 1e-06)).astype(jnp.bfloat16)
        for i in range(2 * model // half):
            at = slice((i % 2 * rows + 2 * m) * 8, (i % 2 * rows + 2 * m + 2) * 8)
            emb_scr[i // 2, at, :] = embedded[:, i * quarter : (i + 1) * quarter]
    for i, out in enumerate((emb_own, emb_oth)):
        which = me if i == 0 else 1 - me
        outs.append(pltpu.make_async_copy(emb_scr.at[which], out, out_sems.at[rows // 2, i]))
        outs[-1].start()
    for copy in outs:
        copy.wait()


def layer(core, table, received, x_other, weights, gain_attn, gain_ffn):
    rows, body, _ = x_other.shape
    half = body * LANES // HD
    tokens = rows * HD
    model = 2 * half
    wu, wd = weights[4], weights[6]
    flops = 2 * tokens * model * (3 * model + model + 4 * wu.shape[1])
    any_spec = pl.BlockSpec(memory_space=pltpu.HBM)
    vmem = pl.BlockSpec(memory_space=pltpu.VMEM)
    return pl.pallas_call(
        layer_kernel,
        out_shape=(
            jax.ShapeDtypeStruct((tokens, half), jnp.bfloat16),
            jax.ShapeDtypeStruct((tokens, half), jnp.bfloat16),
            jax.ShapeDtypeStruct((2 * rows * 8, half // 2), jnp.bfloat16),
            jax.ShapeDtypeStruct((2 * rows * 8, half // 2), jnp.bfloat16),
        ),
        in_specs=[pl.BlockSpec(memory_space=pltpu.SMEM)]
        + [any_spec] * 11
        + [vmem] * 2,
        out_specs=(any_spec,) * 4,
        scratch_shapes=[
            pltpu.SMEM(table.shape, jnp.int32),
            pltpu.VMEM((rows, 2 * body, LANES), jnp.bfloat16),
            pltpu.VMEM((tokens, 3 * model), jnp.bfloat16),
            pltpu.VMEM((2, 2 * rows * 8, half // 2), jnp.bfloat16),
            pltpu.VMEM((tokens, model), jnp.float32),
            pltpu.VMEM((6, model, half), jnp.bfloat16),
            pltpu.VMEM((2, half, model), jnp.bfloat16),
            pltpu.VMEM((2,) + wu.shape, jnp.bfloat16),
            pltpu.VMEM((2,) + wd.shape, jnp.bfloat16),
            pltpu.SemaphoreType.DMA((rows,)),
            pltpu.SemaphoreType.DMA,
            pltpu.SemaphoreType.DMA((6,)),
            pltpu.SemaphoreType.DMA((3, 2)),
            pltpu.SemaphoreType.DMA,
            pltpu.SemaphoreType.DMA((rows // 2 + 1, 2)),
        ],
        compiler_params=pltpu.CompilerParams(vmem_limit_bytes=62 * 1024 * 1024),
        cost_estimate=pl.CostEstimate(
            flops=flops, bytes_accessed=28 * 1024 * 1024, transcendentals=0
        ),
        name="layer",
    )(core, table, received, x_other, *weights, gain_attn, gain_ffn)


def shards(tokens, doc_ids, dest, owner, w_qkv, w_out, gain_attn, w_up, w_down, gain_ffn):
    devices = lax.axis_size("dp")
    row_count, seq, half = tokens.shape
    docs = owner.shape[1]
    mine = row_count // 2
    me = lax.axis_index("mp")

    qkv_own = jnp.moveaxis(w_qkv, 1, 0)
    weights = []
    for own in (qkv_own, w_out, w_up, w_down):
        weights += [own, lax.ppermute(own, "mp", SWAP)]

    received = lax.all_to_all(
        pack(dest, doc_ids, tokens, devices), "dp", split_axis=0, concat_axis=0, tiled=True
    )
    owners = owner.reshape(-1)
    position = jnp.arange(row_count * docs, dtype=jnp.int32)
    earlier = (owners[:, None] == owners[None, :]) & (position[None, :] < position[:, None])
    rank = jnp.sum(earlier.astype(jnp.int32), -1)
    target = (owners * 2 * SLOTS + rank).reshape(2, 1, mine, docs)
    target = target + jnp.array([0, SLOTS], jnp.int32).reshape(1, 2, 1, 1)
    target = jnp.pad(
        target, ((0, 0), (0, 0), (0, 0), (0, 8 - docs)), constant_values=-1
    ).reshape(2, 2 * mine * 8)
    out_slot = jnp.arange(devices * 2 * SLOTS, dtype=jnp.int32)[:, None]
    place_own = (lax.dynamic_index_in_dim(target, me, 0) == out_slot).astype(jnp.bfloat16)
    place_oth = (lax.dynamic_index_in_dim(target, 1 - me, 0) == out_slot).astype(jnp.bfloat16)
    core = me.astype(jnp.int32)[None]
    core, place_own, place_oth = lax.optimization_barrier((core, place_own, place_oth))
    x_send, info = unpack(core, received, mine)
    x_other = lax.ppermute(x_send, "mp", SWAP)
    enc_own, enc_oth, emb_own, emb_oth = layer(
        core, info, received, x_other, weights, gain_attn[None], gain_ffn[None]
    )
    emb_recv = lax.ppermute(emb_oth, "mp", SWAP)
    own_part = jnp.dot(place_own, emb_own, preferred_element_type=jnp.float32)
    own_part, emb_recv = lax.optimization_barrier((own_part, emb_recv))
    enc_oth, emb_recv = lax.optimization_barrier((enc_oth, emb_recv))
    enc_recv = lax.ppermute(enc_oth, "mp", SWAP)

    sending = jnp.dot(place_oth, emb_recv, preferred_element_type=jnp.float32)
    sending = (sending + own_part).astype(jnp.bfloat16)
    got = lax.all_to_all(
        sending.reshape(devices, 2 * SLOTS, half // 2), "dp", split_axis=0, concat_axis=0, tiled=True
    )
    enc_own = enc_own.reshape(mine, seq, half)
    enc_recv = enc_recv.reshape(mine, seq, half)
    first = me == 0
    encoded = jnp.concatenate(
        [jnp.where(first, enc_own, enc_recv), jnp.where(first, enc_recv, enc_own)], 0
    )
    got, encoded = lax.optimization_barrier((got, encoded))
    got = jnp.concatenate([got[:, : SLOTS - 1], got[:, SLOTS:-1]], -1)
    index_part = got.astype(jnp.float32).reshape(1, devices * (SLOTS - 1), half)
    return (encoded, index_part)


def solution(mesh):
    return jax.shard_map(
        shards,
        mesh=mesh,
        in_specs=(
            P("dp", None, "mp"),
            P("dp", None),
            P("dp"),
            P("dp", None),
            P(None, None, "mp"),
            P("mp", None),
            P(),
            P(None, "mp"),
            P("mp", None),
            P(),
        ),
        out_specs=(P("dp", None, "mp"), P("dp", None, "mp")),
        check_vma=False,
    )
```
